32 devices in a mesh: row: 16 (over z, y, core), ch: 2 (over x).
Axes of the slice: x: 2, y: 2, z: 4, core: 2. Of those that a mesh axis runs over, the one named last changes fastest.
Arguments:
- pair_act: bfloat16 [256, 256, 128], P('row', 'ch'), may hold values from -6 to 6
- valid_count: int32 [1], replicated, may hold values from 129 to 256
- edge_proj: bfloat16 [128, 256], replicated, may hold values from -0.5 to 0.5
- edge_gate: bfloat16 [128, 256], replicated, may hold values from -0.5 to 0.5
- tri_gate: bfloat16 [128, 128], replicated, may hold values from -0.5 to 0.5
- tri_out: bfloat16 [128, 128], replicated, may hold values from -0.5 to 0.5
- attn_proj: bfloat16 [128, 512], replicated, may hold values from -0.5 to 0.5
- bias_proj: bfloat16 [128, 4], replicated, may hold values from -24 to 24, as said below
- attn_out: bfloat16 [128, 128], replicated, may hold values from -0.5 to 0.5
Outputs:
- pair_out: bfloat16 [256, 256, 128], P('row', 'ch')
The draws below stay inside these ranges and needn't reach their ends.
Inputs may be any that keep to these rules, and one draw needn't show every extreme that they name: `bias_proj`: biases' projection; its columns differ in scale.
All inputs are finite; a program needn't handle non-finite values.
Results may differ from the reference program's by a relative error of at most 0.038.
Values may be sent and summed in bfloat16 or wider, within the bound.
No kernel may reach another device: no remote copies, remote signals or barrier semaphores. Data moves between devices by JAX's collectives and lax.ppermute only.
A program may use at most 128 MiB of HBM per device.

```python
import math
import jax
import jax.numpy as jnp
from jax import lax

C = 128
HEADS = 4
HEAD_DIM = 32
TOKENS = 256


def draw_bias_proj(key, part):
    key = jax.random.fold_in(key, 11)
    base = jnp.clip(jax.random.normal(key, (C, HEADS), jnp.float32), -4.0, 4.0) * C ** (-0.5)
    factors = jnp.exp(jax.random.uniform(jax.random.fold_in(key, 1), (HEADS,), jnp.float32, 0.0, math.log(3.0)))
    return (base * factors[None, :]).astype(jnp.bfloat16)


def levels(key, shape, shards, low, top_value):
    def one(dim, blocks):
        draws = jax.random.uniform(jax.random.fold_in(jax.random.fold_in(key, 6), dim), (blocks,), jnp.float32, low / len(shards), top_value / len(shards))
        return jnp.repeat(jnp.exp(draws), shape[dim] // blocks).reshape((-1,) + (1,) * (len(shape) - dim - 1))

    gain = one(*shards[0])
    for cut in shards[1:]:
        gain = gain * one(*cut)
    return gain


def centred(stream_key, dims, width, most, cuts=(), dtype=jnp.bfloat16):
    factor_of = levels(stream_key, dims, cuts, -0.22, 0.18) if cuts else 1.0
    array = jax.random.normal(stream_key, dims, jnp.float32) * width * factor_of
    return jnp.minimum(jnp.maximum(array, -most), most).astype(dtype)


def setup_inputs(seed: int = 0) -> dict:
    seeds = jax.random.split(jax.random.key(seed), 10)
    pair_act = centred(seeds[0], (TOKENS, TOKENS, C), 1.0, 6.0, ((0, 16), (1, 2)))
    valid_count = jax.random.randint(seeds[1], (1,), TOKENS // 2 + 1, TOKENS + 1).astype(jnp.int32)
    edge_proj = centred(seeds[2], (C, 2 * C), C ** -0.5, 0.5)
    edge_gate = centred(seeds[3], (C, 2 * C), C ** -0.5, 0.5)
    tri_gate = centred(seeds[4], (C, C), C ** -0.5, 0.5)
    tri_out = centred(seeds[5], (C, C), C ** -0.5, 0.5)
    attn_proj = centred(seeds[6], (C, 4 * C), C ** -0.5, 0.5)
    bias_proj = draw_bias_proj(jax.random.fold_in(seeds[9], 71), 0)
    attn_out = centred(seeds[8], (C, C), C ** -0.5, 0.5)
    return dict(pair_act=pair_act, valid_count=valid_count, edge_proj=edge_proj, edge_gate=edge_gate, tri_gate=tri_gate, tri_out=tri_out, attn_proj=attn_proj, bias_proj=bias_proj, attn_out=attn_out)


EPS = 1e-05

def layer_norm(values):
    centre = values - lax.optimization_barrier(jnp.mean(values, axis=-1, keepdims=True))
    spread = lax.optimization_barrier(jnp.mean(centre * centre, axis=-1, keepdims=True))
    return centre * lax.rsqrt(spread + EPS)

def reference(pair_act, valid_count, edge_proj, edge_gate, tri_gate, tri_out, attn_proj, bias_proj, attn_out):
    length = valid_count[0]
    token_valid = (jnp.arange(TOKENS) < length).astype(jnp.float32)
    pair_valid = token_valid[:, None] * token_valid[None, :]
    source = pair_act.astype(jnp.float32)
    normed = layer_norm(source).astype(jnp.bfloat16)
    projected = jnp.dot(normed, edge_proj, preferred_element_type=jnp.float32)
    gating = jnp.dot(normed, edge_gate, preferred_element_type=jnp.float32)
    edges = (jax.nn.sigmoid(gating) * projected * pair_valid[:, :, None]).astype(jnp.bfloat16)
    left_edges = edges[:, :, :C].astype(jnp.float32)
    right_edges = edges[:, :, C:].astype(jnp.float32)
    triangle = jnp.einsum('ikc,jkc->ijc', left_edges, right_edges)
    tri_normed = layer_norm(triangle).astype(jnp.bfloat16)
    update = jax.nn.sigmoid(jnp.dot(normed, tri_gate, preferred_element_type=jnp.float32)) * jnp.dot(tri_normed, tri_out, preferred_element_type=jnp.float32)
    updated = (source + update).astype(jnp.bfloat16)
    attn_normed = layer_norm(updated.astype(jnp.float32)).astype(jnp.bfloat16)
    mixed = jnp.dot(attn_normed, attn_proj, preferred_element_type=jnp.float32)
    query = mixed[..., :C].astype(jnp.bfloat16)
    keys = mixed[..., C:2 * C].astype(jnp.bfloat16)
    values = mixed[..., 2 * C:3 * C].astype(jnp.bfloat16)
    attn_gate = jax.nn.sigmoid(mixed[..., 3 * C:])
    head_bias = jnp.transpose(jnp.dot(attn_normed, bias_proj, preferred_element_type=jnp.float32), (2, 0, 1)).astype(jnp.bfloat16)
    bias_float = head_bias.astype(jnp.float32)
    key_term = (token_valid - 1.0) * 1000000000.0
    score_scale = HEAD_DIM ** (-0.5)
    group = 16

    def attend(block):
        query_rows, key_rows, value_rows = block
        query_heads = query_rows.astype(jnp.float32).reshape(group, TOKENS, HEADS, HEAD_DIM)
        key_heads = key_rows.astype(jnp.float32).reshape(group, TOKENS, HEADS, HEAD_DIM)
        value_heads = value_rows.astype(jnp.float32).reshape(group, TOKENS, HEADS, HEAD_DIM)
        logits = jnp.einsum('ijhd,ikhd->ihjk', query_heads, key_heads) * score_scale
        logits = logits + bias_float[None] + key_term[None, None, None, :]
        attn_weights = jax.nn.softmax(logits, axis=-1).astype(jnp.bfloat16)
        output = jnp.einsum('ihjk,ikhd->ijhd', attn_weights.astype(jnp.float32), value_heads)
        return output.reshape(group, TOKENS, C)
    blocks = TOKENS // group
    attended = lax.map(attend, (query.reshape(blocks, group, TOKENS, C), keys.reshape(blocks, group, TOKENS, C), values.reshape(blocks, group, TOKENS, C)))
    attended = attended.reshape(TOKENS, TOKENS, C)
    gated = (attended * attn_gate).astype(jnp.bfloat16)
    return (updated.astype(jnp.float32) + jnp.dot(gated, attn_out, preferred_element_type=jnp.float32)).astype(jnp.bfloat16)
```

```python
import functools
import math

import jax
import jax.numpy as jnp
from jax import lax
from jax.experimental import pallas as pl
from jax.experimental.pallas import tpu as pltpu
from jax.sharding import PartitionSpec as P

EPS = 1e-05
BOTH = ("row", "ch")
F32 = jnp.float32
BF16 = jnp.bfloat16
VMEM = pl.BlockSpec(memory_space=pltpu.VMEM)
SMEM = pl.BlockSpec(memory_space=pltpu.SMEM)
HBM = pl.BlockSpec(memory_space=pltpu.HBM)
ANY = pl.BlockSpec(memory_space=pl.ANY)


def layer_norm(values, axis):
    centre = values - jnp.mean(values, axis=axis, keepdims=True)
    spread = jnp.mean(centre * centre, axis=axis, keepdims=True)
    return centre * lax.rsqrt(spread + EPS)


def in_hbm(array):
    return pltpu.with_memory_space_constraint(array, pltpu.HBM)


def sigmoid(values):
    return 0.5 * jnp.tanh(0.5 * values) + 0.5


def dot(a, b, dims):
    return lax.dot_general(a, b, ((dims[:1], dims[1:]), ((), ())), preferred_element_type=F32)


def call(body, name, outs, ins, scratch=(), flops=1e8, smem=0, space=VMEM, out_space=VMEM, specs=None):
    sizes = [math.prod(a.shape) * a.dtype.itemsize for a in outs]
    if out_space is HBM:
        outs = [pltpu.HBM(a.shape, a.dtype) for a in outs]
    return pl.pallas_call(
        body,
        out_shape=outs,
        in_specs=specs or [SMEM] * smem + [space] * (ins - smem),
        out_specs=[out_space] * len(outs),
        scratch_shapes=list(scratch),
        compiler_params=pltpu.CompilerParams(vmem_limit_bytes=16 * 2**20),
        cost_estimate=pl.CostEstimate(
            flops=int(flops), bytes_accessed=2 * sum(sizes), transcendentals=0
        ),
        name=name,
    )


def turned(weights):
    return weights.astype(F32).T.astype(BF16)


def run(copies):
    for copy in copies:
        copy.start()
    for copy in copies:
        copy.wait()


def place():
    per_half = lax.axis_size("row") // 2
    columns = lax.axis_size("ch")
    row = lax.rem(lax.axis_index("row"), per_half)
    core = lax.rem(row, 2)
    return (row - core) * columns + lax.axis_index("ch"), core


def chip_offsets():
    columns = lax.axis_size("ch")
    share = lax.axis_size("row") // 2 * columns
    return [o for o in range(share) if o // columns % 2 == 0]


def chunked(pairs, sems, first, chunks):
    rows = pairs[0][0].shape[0]
    size = rows // chunks
    return [
        [
            pltpu.make_async_copy(
                source.at[pl.ds(chunk * size, size)],
                target.at[pl.ds(chunk * size, size)],
                sems.at[first + k, chunk],
            )
            for k, (source, target) in enumerate(pairs)
        ]
        for chunk in range(chunks)
    ]


def edges_body(length, source_hbm, proj_hbm, gate_hbm, *rest, side):
    outs = rest[:-6]
    source, proj, gate, held, out, sems = rest[-6:]
    rows, cols, channels = source.shape
    share, own = out.shape[:2]
    columns = lax.axis_size("ch")
    span = pl.ds(side * channels, channels)
    fetches = [
        pltpu.make_async_copy(proj_hbm.at[:, span], proj, sems.at[0, 2]),
        pltpu.make_async_copy(gate_hbm.at[:, span], gate, sems.at[0, 3]),
    ]
    chunks = chunked([(source_hbm, source)], sems, 0, 2)
    for copy in fetches + chunks[0] + chunks[1]:
        copy.start()
    row_offset = lax.axis_index("row") * rows
    col_offset = lax.axis_index("ch") * cols
    count = length[0]
    tokens = col_offset + lax.broadcasted_iota(jnp.int32, (1, cols), 1)
    col_valid = jnp.where(tokens < count, 0.5, 0.0)
    for copy in fetches:
        copy.wait()
    weights = jnp.concatenate([turned(proj[...]), turned(gate[...])], axis=0)

    def step(row, carry):
        values = source[row]
        if side:
            values = layer_norm(values.astype(F32), -1).astype(BF16)
            source[row] = values
        mixed = dot(weights, values, (1, 1))
        valid = col_valid * (row_offset + row < count).astype(F32)
        twice = jnp.tanh(0.5 * mixed[channels:]) + 1.0
        held[pl.ds(row, channels, stride=rows), :] = twice * (mixed[:channels] * valid)
        return carry

    for (copy,) in chunks:
        copy.wait()
    lax.fori_loop(0, rows, step, 0, unroll=rows)
    sends = []
    if side:
        sends.append(pltpu.make_async_copy(source, outs[1], sems.at[1, 0]))
        sends[0].start()
    group = share // 4
    for device in range(share):
        part = held[device * own * rows : (device + 1) * own * rows, :].astype(BF16)
        position = share - 1 - device
        out[position] = part.reshape(own, rows, cols)
        if side and device % group == group - 1:
            for k in range(2):
                source_part = out.at[pl.ds(position, group)]
                target = outs[0].at[pl.ds(k * share + position, group)]
                sends.append(
                    pltpu.make_async_copy(source_part, target, sems.at[1 + k, 1 + device // group])
                )
                sends[-1].start()
    if not side:
        chip, core = place()
        for k, offset in enumerate(chip_offsets()):
            for other in range(2):
                index = jnp.bitwise_xor(chip, offset) + lax.rem(core + other, 2) * columns
                outs[other][k] = out[index]
    for copy in sends:
        copy.wait()


def pack_body(mine, sibling, *outs):
    _, core = place()
    for k, out in enumerate(outs):
        out[core] = mine[k]
        out[1 - core] = sibling[k]


def gate_body(pair, normed, weights, out, source):
    turned_weights = turned(weights[...])

    def step(row, carry):
        out[row] = sigmoid(dot(turned_weights, normed[row], (1, 1))).astype(BF16)
        source[row] = pair[row].astype(F32).T.astype(BF16)
        return carry

    lax.fori_loop(0, pair.shape[0], step, 0, unroll=2)


def triangle_body(right, *rest):
    parts, out, held, sent = rest[:-3], rest[-3], rest[-2], rest[-1]
    row_devices, col_devices, own, rows, cols = right.shape
    chip, _ = place()
    chip_row = lax.div(chip, col_devices)
    me = lax.axis_index("ch")
    groups = [(first, core) for first in range(0, row_devices // 2, 2) for core in range(2)]
    offsets = chip_offsets()
    for channel in range(own):
        left, whole = [], []
        for flip in range(col_devices):
            left.append(
                jnp.concatenate(
                    [
                        parts[offsets.index(first * col_devices + flip)][core, channel]
                        for first, core in groups
                    ],
                    axis=0,
                )
            )
            whole.append(right[:, jnp.bitwise_xor(me, flip), channel].reshape(-1, cols))
        triangle = dot(
            jnp.concatenate(left, axis=1), jnp.concatenate(whole, axis=1), (1, 1)
        ).astype(BF16)
        for k, (first, core) in enumerate(groups):
            for part in range(col_devices):
                row = row_devices // 2 - 1 - core - jnp.bitwise_xor(chip_row, first)
                held[row, col_devices - 1 - part, channel] = triangle[
                    k * rows : (k + 1) * rows, part * cols : (part + 1) * cols
                ]
    run([pltpu.make_async_copy(held, out, sent)])


def copies_body(bias, out):
    for k in range(out.shape[0]):
        out[k] = bias[...]


def spread_sum(values):
    lead = 8
    split = values.reshape((values.shape[0] // lead, lead) + values.shape[1:])
    return jnp.sum(jnp.sum(split, axis=0), axis=0, keepdims=True)


def update_body(triangle, source, gate, tri_out, bias_proj, updated, bias, held, bias_held):
    channels, rows, cols = triangle.shape
    heads = bias_proj.shape[1]
    values = triangle[...].astype(F32)
    centre = values - spread_sum(values) * (1.0 / channels)
    spread = spread_sum(centre * centre) * (1.0 / channels)
    held[...] = (centre * lax.rsqrt(spread + EPS)).reshape(channels * rows, cols)
    out_weights = turned(tri_out[...])
    bias_weights = turned(bias_proj[...])

    def step(row, carry):
        tri_normed = held[pl.ds(row, channels, stride=rows), :].astype(BF16)
        update = gate[row].astype(F32) * dot(out_weights, tri_normed, (1, 0))
        mine = (source[row].astype(F32) + update).astype(BF16)
        updated[row] = mine
        normed = layer_norm(mine.astype(F32), 0).astype(BF16)
        bias_held[pl.ds(row, heads, stride=rows), :] = dot(bias_weights, normed, (1, 0))
        return carry

    lax.fori_loop(0, rows, step, 0, unroll=8)
    bias[...] = bias_held[...].astype(BF16).reshape(heads, rows, cols)


def project(updated, attn_proj, mixed, row, score_scale):
    channels = updated.shape[1]
    values = updated[row].astype(F32)
    normed = layer_norm(values, 0)
    natural = normed.T.astype(BF16)

    def put(block, array):
        mixed[row, :, block * channels : (block + 1) * channels] = array.astype(BF16)

    put(0, dot(turned(attn_proj[:, channels : 2 * channels]), normed.astype(BF16), (1, 0)))
    put(1, dot(natural, attn_proj[:, 2 * channels : 3 * channels], (1, 0)))
    if score_scale is not None:
        put(2, dot(natural, attn_proj[:, :channels], (1, 0)) * score_scale)
        put(3, sigmoid(dot(natural, attn_proj[:, 3 * channels :], (1, 0))))
        put(4, values.T)


def own_body(updated, attn_proj, mixed_hbm, mixed, sems, *, score_scale):
    rows = updated.shape[0]

    def step(row, carry):
        project(updated, attn_proj, mixed, row, score_scale)
        return carry

    sends = chunked([(mixed, mixed_hbm)], sems, 0, 2)
    for chunk in range(2):
        lax.fori_loop(chunk * rows // 2, (chunk + 1) * rows // 2, step, 0, unroll=rows // 2)
        sends[chunk][0].start()
    for (copy,) in sends:
        copy.wait()


def other_body(mixed_hbm, attn_proj, *rest):
    pieces = (len(rest) - 2) // 2
    others, mixed, keys, sem = rest[:pieces], rest[pieces], rest[pieces + 1 : -1], rest[-1]
    fetch = pltpu.make_async_copy(mixed_hbm, mixed, sem)
    fetch.start()
    rows = mixed.shape[0]
    for updated, target in zip(others, keys):

        def step(row, carry):
            project(updated, attn_proj, target, row, None)
            return carry

        lax.fori_loop(0, rows, step, 0, unroll=rows // 2)
    fetch.wait()


def attend_body(length, mine, sibling, attn_out, *rest):
    mixed, (out_hbm, out, bias_held, sems) = rest[:-4], rest[-4:]
    pieces = len(mixed)
    rows, cols, channels = out.shape
    heads = mine.shape[1]
    me = lax.axis_index("ch")
    its_core = lax.rem(lax.axis_index("row"), 2)
    head_of = lax.broadcasted_iota(jnp.int32, (1, channels), 1) // (channels // heads)
    count = sems.shape[1]
    sends = chunked([(out, out_hbm)], sems, 0, count)
    chips = cols // rows // 2
    for piece in range(pieces):
        block = lax.rem(me + piece, pieces)
        token = block * cols + lax.broadcasted_iota(jnp.int32, (1, cols), 1)
        key_term = jnp.where(token < length[0], 0.0, -1e9)
        for part, core in ((mine, its_core), (sibling, 1 - its_core)):
            for chip in range(chips):
                tiles = part[(me * chips + chip) * pieces + block]
                for head in range(heads):
                    first = pl.multiple_of(head * cols + (chip * 2 + core) * rows, rows)
                    bias_held[pl.ds(first, rows), piece * cols : (piece + 1) * cols] = (
                        tiles[head].astype(F32) + key_term
                    )
    both_of = jnp.concatenate([head_of, head_of], axis=1)
    masks = [(head_of == head).astype(BF16) for head in range(heads)]
    ones = jnp.ones((pieces * cols, channels), BF16)

    def load(row):
        keys = jnp.concatenate([part[row, :, :channels] for part in mixed], axis=1)
        values = jnp.concatenate([part[row, :, channels : 2 * channels] for part in mixed], axis=0)
        values = jnp.concatenate([values, ones], axis=1)
        return keys, values, mixed[0][row, :, 2 * channels : 3 * channels]

    def finish(row, total):
        attended = total[:, :channels] / total[:, channels:]
        gate = mixed[0][row, :, 3 * channels : 4 * channels].astype(F32)
        gated = (attended * gate).astype(BF16)
        residual = mixed[0][row, :, 4 * channels :].astype(F32)
        out[row] = (residual + dot(gated, attn_out[...], (1, 0))).astype(BF16)

    per_chunk = rows // count
    loaded, logits, weights = {}, {}, {}
    for time in range(rows + 2):
        row = time
        if row < rows:
            loaded[row] = load(row)
            keys, _, query = loaded[row]
            queries = jnp.concatenate([query * mask for mask in masks], axis=0)
            logits[row] = dot(queries, keys, (1, 0)) + bias_held[...]
        row = time - 1
        if 0 <= row < rows:
            scores = logits.pop(row)
            top = jnp.max(scores, axis=-1, keepdims=True)
            weights[row] = jnp.exp((scores - top).astype(BF16))
        row = time - 2
        if row >= 0:
            sums = dot(weights.pop(row), loaded.pop(row)[1], (1, 0))
            total = sums[:cols]
            for head in range(1, heads):
                total = jnp.where(both_of == head, sums[head * cols : (head + 1) * cols], total)
            finish(row, total)
            chunk, place_in = divmod(row, per_chunk)
            if place_in == per_chunk - 1:
                for copy in sends[chunk]:
                    copy.start()
    for send in sends:
        for copy in send:
            copy.wait()


def local(
    pair_act, valid_count, edge_proj, edge_gate, tri_gate, tri_out, attn_proj, bias_proj, attn_out
):
    rows, cols, channels = pair_act.shape
    heads = bias_proj.shape[1]
    row_devices = lax.axis_size("row")
    col_devices = lax.axis_size("ch")
    devices = row_devices * col_devices
    share = devices // 2
    own = channels // share
    everyone = list(reversed(range(devices)))
    halves = [everyone[share:], everyone[:share]]
    shape = jax.ShapeDtypeStruct
    block = (rows, cols, channels)
    turned_block = (rows, channels, cols)

    def in_half(array):
        return lax.all_to_all(
            array, BOTH, split_axis=0, concat_axis=0, axis_index_groups=halves, tiled=True
        )


    weight = pltpu.VMEM((channels, channels), BF16)
    offsets = chip_offsets()
    tile = (own, rows, cols)

    def edges(side, source):
        outs = [shape((devices,) + tile, BF16), shape(block, BF16)]
        return call(
            functools.partial(edges_body, side=side),
            "right_edges" if side else "left_edges",
            outs if side else [shape((len(offsets),) + tile, BF16)] * 2,
            4,
            [
                pltpu.VMEM(block, BF16),
                weight,
                weight,
                pltpu.VMEM((channels * rows, cols), F32),
                pltpu.VMEM((share,) + tile, BF16),
                pltpu.SemaphoreType.DMA((3, 5)),
            ],
            smem=1,
            space=HBM,
            out_space=HBM if side else VMEM,
            flops=3e9,
        )(valid_count, *[in_hbm(a) for a in (source, edge_proj, edge_gate)])

    def flipped(array, bits):
        return lax.ppermute(array, BOTH, [(d, d ^ bits) for d in range(devices)])

    right, normed = edges(1, pair_act)
    right = lax.all_to_all(right, BOTH, split_axis=0, concat_axis=0, tiled=True)
    mine, theirs = edges(0, normed)
    left = call(pack_body, "pack", [shape((2,) + tile, BF16)] * len(offsets), 2)(
        mine, flipped(theirs, col_devices)
    )
    left = [flipped(part, offset) if offset else part for part, offset in zip(left, offsets)]
    tri_gating, source = call(
        gate_body, "tri_gate", [shape(turned_block, BF16)] * 2, 3, flops=2e9
    )(pair_act, normed, tri_gate)
    triangle_shape = (row_devices // 2, col_devices, own, rows, cols)
    (triangle,) = call(
        triangle_body,
        "triangle",
        [shape(triangle_shape, BF16)],
        1 + len(left),
        [pltpu.VMEM(triangle_shape, BF16), pltpu.SemaphoreType.DMA(())],
        out_space=HBM,
        flops=2e9,
    )(right.reshape((row_devices,) + triangle_shape[1:]), *left)
    triangle = in_half(triangle.reshape(share, own, rows, cols))
    bias_shape = (heads, rows, cols)
    updated, bias = call(
        update_body,
        "update",
        [shape(turned_block, BF16), shape(bias_shape, BF16)],
        5,
        [pltpu.VMEM((channels * rows, cols), F32), pltpu.VMEM((heads * rows, cols), F32)],
        flops=2e9,
    )(triangle.reshape(channels, rows, cols), source, tri_gating, tri_out, bias_proj)
    one_core = [
        [d for d in range(devices) if d // col_devices % 2 == core] for core in range(2)
    ]
    (copies,) = call(
        copies_body,
        "bias_copies",
        [shape((share,) + bias_shape, BF16)],
        1,
        flops=1e9,
    )(bias)

    others = [
        lax.ppermute(updated, "ch", [((c + s) % col_devices, c) for c in range(col_devices)])
        for s in range(1, col_devices)
    ]
    bias = lax.all_to_all(
        copies, BOTH, split_axis=0, concat_axis=0, axis_index_groups=one_core, tiled=True
    )

    mixed_shape = (rows, cols, 5 * channels)
    key_shape = (rows, cols, 2 * channels)
    (mixed,) = call(
        functools.partial(own_body, score_scale=(channels // heads) ** (-0.5)),
        "own_projections",
        [shape(mixed_shape, BF16)],
        2,
        [pltpu.VMEM(mixed_shape, BF16), pltpu.SemaphoreType.DMA((1, 2))],
        out_space=HBM,
        flops=3e9,
    )(updated, attn_proj)
    bias, *others = lax.optimization_barrier((bias, *others))
    mixed = call(
        other_body,
        "other_keys",
        [shape(mixed_shape, BF16)] + [shape(key_shape, BF16)] * len(others),
        2 + len(others),
        [pltpu.SemaphoreType.DMA(())],
        specs=[HBM] + [VMEM] * (1 + len(others)),
        flops=3e9,
    )(in_hbm(mixed), attn_proj, *others)
    (result,) = call(
        attend_body,
        "attend",
        [shape(block, BF16)],
        4 + col_devices,
        [
            pltpu.VMEM(block, BF16),
            pltpu.VMEM((heads * cols, col_devices * cols), F32),
            pltpu.SemaphoreType.DMA((1, rows // 2)),
        ],
        smem=1,
        out_space=HBM,
    )(valid_count, bias, flipped(bias, col_devices), attn_out, *mixed)
    return result


def solution(mesh):
    placed = (P("row", "ch", None), P(), P(), P(), P(), P(), P(), P(), P())
    return jax.shard_map(
        local, mesh=mesh, in_specs=placed, out_specs=P("row", "ch", None), check_vma=False
    )
```

```python
import functools
import math

import jax
import jax.numpy as jnp
from jax import lax
from jax.experimental import pallas as pl
from jax.experimental.pallas import tpu as pltpu
from jax.sharding import PartitionSpec as P

EPS = 1e-05
BOTH = ("row", "ch")
F32 = jnp.float32
BF16 = jnp.bfloat16
VMEM = pl.BlockSpec(memory_space=pltpu.VMEM)
SMEM = pl.BlockSpec(memory_space=pltpu.SMEM)
HBM = pl.BlockSpec(memory_space=pltpu.HBM)
ANY = pl.BlockSpec(memory_space=pl.ANY)


def layer_norm(values, axis):
    centre = values - jnp.mean(values, axis=axis, keepdims=True)
    spread = jnp.mean(centre * centre, axis=axis, keepdims=True)
    return centre * lax.rsqrt(spread + EPS)


def in_hbm(array):
    return pltpu.with_memory_space_constraint(array, pltpu.HBM)


def sigmoid(values):
    return 0.5 * jnp.tanh(0.5 * values) + 0.5


def dot(a, b, dims):
    return lax.dot_general(a, b, ((dims[:1], dims[1:]), ((), ())), preferred_element_type=F32)


def call(body, name, outs, ins, scratch=(), flops=1e8, smem=0, space=VMEM, out_space=VMEM, specs=None):
    sizes = [math.prod(a.shape) * a.dtype.itemsize for a in outs]
    if out_space is HBM:
        outs = [pltpu.HBM(a.shape, a.dtype) for a in outs]
    return pl.pallas_call(
        body,
        out_shape=outs,
        in_specs=specs or [SMEM] * smem + [space] * (ins - smem),
        out_specs=[out_space] * len(outs),
        scratch_shapes=list(scratch),
        compiler_params=pltpu.CompilerParams(vmem_limit_bytes=16 * 2**20),
        cost_estimate=pl.CostEstimate(
            flops=int(flops), bytes_accessed=2 * sum(sizes), transcendentals=0
        ),
        name=name,
    )


def turned(weights):
    return weights.astype(F32).T.astype(BF16)


def run(copies):
    for copy in copies:
        copy.start()
    for copy in copies:
        copy.wait()


def place():
    per_half = lax.axis_size("row") // 2
    columns = lax.axis_size("ch")
    row = lax.rem(lax.axis_index("row"), per_half)
    core = lax.rem(row, 2)
    return (row - core) * columns + lax.axis_index("ch"), core


def chip_offsets():
    columns = lax.axis_size("ch")
    share = lax.axis_size("row") // 2 * columns
    return [o for o in range(share) if o // columns % 2 == 0]


def chunked(pairs, sems, first, chunks):
    rows = pairs[0][0].shape[0]
    size = rows // chunks
    return [
        [
            pltpu.make_async_copy(
                source.at[pl.ds(chunk * size, size)],
                target.at[pl.ds(chunk * size, size)],
                sems.at[first + k, chunk],
            )
            for k, (source, target) in enumerate(pairs)
        ]
        for chunk in range(chunks)
    ]


def edges_body(length, source_hbm, proj_hbm, gate_hbm, *rest, side):
    outs = rest[:-6]
    source, proj, gate, held, out, sems = rest[-6:]
    rows, cols, channels = source.shape
    share, own = out.shape[:2]
    columns = lax.axis_size("ch")
    span = pl.ds(side * channels, channels)
    fetches = [
        pltpu.make_async_copy(proj_hbm.at[:, span], proj, sems.at[0, 2]),
        pltpu.make_async_copy(gate_hbm.at[:, span], gate, sems.at[0, 3]),
    ]
    chunks = chunked([(source_hbm, source)], sems, 0, 2)
    for copy in fetches + chunks[0] + chunks[1]:
        copy.start()
    row_offset = lax.axis_index("row") * rows
    col_offset = lax.axis_index("ch") * cols
    count = length[0]
    tokens = col_offset + lax.broadcasted_iota(jnp.int32, (1, cols), 1)
    col_valid = jnp.where(tokens < count, 0.5, 0.0)
    for copy in fetches:
        copy.wait()
    weights = jnp.concatenate([turned(proj[...]), turned(gate[...])], axis=0)

    def step(row, carry):
        values = source[row]
        if side:
            values = layer_norm(values.astype(F32), -1).astype(BF16)
            source[row] = values
        mixed = dot(weights, values, (1, 1))
        valid = col_valid * (row_offset + row < count).astype(F32)
        twice = jnp.tanh(0.5 * mixed[channels:]) + 1.0
        held[pl.ds(row, channels, stride=rows), :] = twice * (mixed[:channels] * valid)
        return carry

    for (copy,) in chunks:
        copy.wait()
    lax.fori_loop(0, rows, step, 0, unroll=rows)
    sends = []
    if side:
        sends.append(pltpu.make_async_copy(source, outs[1], sems.at[1, 0]))
        sends[0].start()
    group = share // 4
    for device in range(share):
        part = held[device * own * rows : (device + 1) * own * rows, :].astype(BF16)
        position = share - 1 - device
        out[position] = part.reshape(own, rows, cols)
        if side and device % group == group - 1:
            for k in range(2):
                source_part = out.at[pl.ds(position, group)]
                target = outs[0].at[pl.ds(k * share + position, group)]
                sends.append(
                    pltpu.make_async_copy(source_part, target, sems.at[1 + k, 1 + device // group])
                )
                sends[-1].start()
    if not side:
        chip, core = place()
        for k, offset in enumerate(chip_offsets()):
            for other in range(2):
                index = jnp.bitwise_xor(chip, offset) + lax.rem(core + other, 2) * columns
                outs[other][k] = out[index]
    for copy in sends:
        copy.wait()


def pack_body(mine, sibling, *outs):
    _, core = place()
    for k, out in enumerate(outs):
        out[core] = mine[k]
        out[1 - core] = sibling[k]


def gate_body(pair, normed, weights, out, source):
    turned_weights = turned(weights[...])

    def step(row, carry):
        out[row] = sigmoid(dot(turned_weights, normed[row], (1, 1))).astype(BF16)
        source[row] = pair[row].astype(F32).T.astype(BF16)
        return carry

    lax.fori_loop(0, pair.shape[0], step, 0, unroll=2)


def triangle_body(right, *rest):
    parts, out, held, sent = rest[:-3], rest[-3], rest[-2], rest[-1]
    row_devices, col_devices, own, rows, cols = right.shape
    chip, _ = place()
    chip_row = lax.div(chip, col_devices)
    me = lax.axis_index("ch")
    groups = [(first, core) for first in range(0, row_devices // 2, 2) for core in range(2)]
    offsets = chip_offsets()
    for channel in range(own):
        left, whole = [], []
        for flip in range(col_devices):
            left.append(
                jnp.concatenate(
                    [
                        parts[offsets.index(first * col_devices + flip)][core, channel]
                        for first, core in groups
                    ],
                    axis=0,
                )
            )
            whole.append(right[:, jnp.bitwise_xor(me, flip), channel].reshape(-1, cols))
        triangle = dot(
            jnp.concatenate(left, axis=1), jnp.concatenate(whole, axis=1), (1, 1)
        ).astype(BF16)
        for k, (first, core) in enumerate(groups):
            for part in range(col_devices):
                row = row_devices // 2 - 1 - core - jnp.bitwise_xor(chip_row, first)
                held[row, col_devices - 1 - part, channel] = triangle[
                    k * rows : (k + 1) * rows, part * cols : (part + 1) * cols
                ]
    run([pltpu.make_async_copy(held, out, sent)])


def deal_body(*refs):
    parts, out = refs[:-1], refs[-1]
    columns = len(parts)
    per_part = lax.axis_size("row") // columns
    part = lax.div(lax.axis_index("row"), per_part)
    for col in range(columns):
        value = parts[0][...]
        for flip in range(1, columns):
            value = jnp.where(jnp.bitwise_xor(part, col) == flip, parts[flip][...], value)
        for chip in range(out.shape[0] // columns):
            out[chip * columns + col] = value


def spread_sum(values):
    lead = 8
    split = values.reshape((values.shape[0] // lead, lead) + values.shape[1:])
    return jnp.sum(jnp.sum(split, axis=0), axis=0, keepdims=True)


def update_body(triangle, source, gate, tri_out, bias_proj, updated, bias, held, bias_held):
    channels, rows, cols = triangle.shape
    heads = bias_proj.shape[1]
    values = triangle[...].astype(F32)
    centre = values - spread_sum(values) * (1.0 / channels)
    spread = spread_sum(centre * centre) * (1.0 / channels)
    held[...] = (centre * lax.rsqrt(spread + EPS)).reshape(channels * rows, cols)
    out_weights = turned(tri_out[...])
    bias_weights = turned(bias_proj[...])

    def step(row, carry):
        tri_normed = held[pl.ds(row, channels, stride=rows), :].astype(BF16)
        update = gate[row].astype(F32) * dot(out_weights, tri_normed, (1, 0))
        mine = (source[row].astype(F32) + update).astype(BF16)
        updated[row] = mine
        normed = layer_norm(mine.astype(F32), 0).astype(BF16)
        bias_held[pl.ds(row, heads, stride=rows), :] = dot(bias_weights, normed, (1, 0))
        return carry

    lax.fori_loop(0, rows, step, 0, unroll=8)
    bias[...] = bias_held[...].astype(BF16).reshape(heads, rows, cols)


def project(updated, attn_proj, mixed, row, score_scale):
    channels = updated.shape[1]
    values = updated[row].astype(F32)
    normed = layer_norm(values, 0)
    natural = normed.T.astype(BF16)

    def put(block, array):
        mixed[row, :, block * channels : (block + 1) * channels] = array.astype(BF16)

    put(0, dot(turned(attn_proj[:, channels : 2 * channels]), normed.astype(BF16), (1, 0)))
    put(1, dot(natural, attn_proj[:, 2 * channels : 3 * channels], (1, 0)))
    if score_scale is not None:
        put(2, dot(natural, attn_proj[:, :channels], (1, 0)) * score_scale)
        put(3, sigmoid(dot(natural, attn_proj[:, 3 * channels :], (1, 0))))
        put(4, values.T)


def own_body(updated, attn_proj, mixed_hbm, mixed, sems, *, score_scale):
    rows = updated.shape[0]

    def step(row, carry):
        project(updated, attn_proj, mixed, row, score_scale)
        return carry

    sends = chunked([(mixed, mixed_hbm)], sems, 0, 2)
    for chunk in range(2):
        lax.fori_loop(chunk * rows // 2, (chunk + 1) * rows // 2, step, 0, unroll=rows // 2)
        sends[chunk][0].start()
    for (copy,) in sends:
        copy.wait()


def other_body(mixed_hbm, attn_proj, *rest):
    pieces = (len(rest) - 2) // 2
    others, mixed, keys, sem = rest[:pieces], rest[pieces], rest[pieces + 1 : -1], rest[-1]
    fetch = pltpu.make_async_copy(mixed_hbm, mixed, sem)
    fetch.start()
    rows = mixed.shape[0]
    for updated, target in zip(others, keys):

        def step(row, carry):
            project(updated, attn_proj, target, row, None)
            return carry

        lax.fori_loop(0, rows, step, 0, unroll=rows // 2)
    fetch.wait()


def attend_body(length, mine, sibling, attn_out, *rest):
    mixed, (out_hbm, out, bias_held, sems) = rest[:-4], rest[-4:]
    pieces = len(mixed)
    rows, cols, channels = out.shape
    heads = mine.shape[1]
    me = lax.axis_index("ch")
    its_core = lax.rem(lax.axis_index("row"), 2)
    head_of = lax.broadcasted_iota(jnp.int32, (1, channels), 1) // (channels // heads)
    count = sems.shape[1]
    sends = chunked([(out, out_hbm)], sems, 0, count)
    chips = cols // rows // 2
    for piece in range(pieces):
        block = lax.rem(me + piece, pieces)
        token = block * cols + lax.broadcasted_iota(jnp.int32, (1, cols), 1)
        key_term = jnp.where(token < length[0], 0.0, -1e9)
        for part, core in ((mine, its_core), (sibling, 1 - its_core)):
            for chip in range(chips):
                tiles = part[chip * pieces + block]
                for head in range(heads):
                    first = pl.multiple_of(head * cols + (chip * 2 + core) * rows, rows)
                    bias_held[pl.ds(first, rows), piece * cols : (piece + 1) * cols] = (
                        tiles[head].astype(F32) + key_term
                    )
    both_of = jnp.concatenate([head_of, head_of], axis=1)
    masks = [(head_of == head).astype(BF16) for head in range(heads)]
    ones = jnp.ones((pieces * cols, channels), BF16)

    def load(row):
        keys = jnp.concatenate([part[row, :, :channels] for part in mixed], axis=1)
        values = jnp.concatenate([part[row, :, channels : 2 * channels] for part in mixed], axis=0)
        values = jnp.concatenate([values, ones], axis=1)
        return keys, values, mixed[0][row, :, 2 * channels : 3 * channels]

    def finish(row, total):
        attended = total[:, :channels] / total[:, channels:]
        gate = mixed[0][row, :, 3 * channels : 4 * channels].astype(F32)
        gated = (attended * gate).astype(BF16)
        residual = mixed[0][row, :, 4 * channels :].astype(F32)
        out[row] = (residual + dot(gated, attn_out[...], (1, 0))).astype(BF16)

    per_chunk = rows // count
    loaded, logits, weights = {}, {}, {}
    for time in range(rows + 2):
        row = time
        if row < rows:
            loaded[row] = load(row)
            keys, _, query = loaded[row]
            queries = jnp.concatenate([query * mask for mask in masks], axis=0)
            logits[row] = dot(queries, keys, (1, 0)) + bias_held[...]
        row = time - 1
        if 0 <= row < rows:
            scores = logits.pop(row)
            top = jnp.max(scores, axis=-1, keepdims=True)
            weights[row] = jnp.exp((scores - top).astype(BF16))
        row = time - 2
        if row >= 0:
            sums = dot(weights.pop(row), loaded.pop(row)[1], (1, 0))
            total = sums[:cols]
            for head in range(1, heads):
                total = jnp.where(both_of == head, sums[head * cols : (head + 1) * cols], total)
            finish(row, total)
            chunk, place_in = divmod(row, per_chunk)
            if place_in == per_chunk - 1:
                for copy in sends[chunk]:
                    copy.start()
    for send in sends:
        for copy in send:
            copy.wait()


def local(
    pair_act, valid_count, edge_proj, edge_gate, tri_gate, tri_out, attn_proj, bias_proj, attn_out
):
    rows, cols, channels = pair_act.shape
    heads = bias_proj.shape[1]
    row_devices = lax.axis_size("row")
    col_devices = lax.axis_size("ch")
    devices = row_devices * col_devices
    share = devices // 2
    own = channels // share
    everyone = list(reversed(range(devices)))
    halves = [everyone[share:], everyone[:share]]
    shape = jax.ShapeDtypeStruct
    block = (rows, cols, channels)
    turned_block = (rows, channels, cols)

    def in_half(array):
        return lax.all_to_all(
            array, BOTH, split_axis=0, concat_axis=0, axis_index_groups=halves, tiled=True
        )


    weight = pltpu.VMEM((channels, channels), BF16)
    offsets = chip_offsets()
    tile = (own, rows, cols)

    def edges(side, source):
        outs = [shape((devices,) + tile, BF16), shape(block, BF16)]
        return call(
            functools.partial(edges_body, side=side),
            "right_edges" if side else "left_edges",
            outs if side else [shape((len(offsets),) + tile, BF16)] * 2,
            4,
            [
                pltpu.VMEM(block, BF16),
                weight,
                weight,
                pltpu.VMEM((channels * rows, cols), F32),
                pltpu.VMEM((share,) + tile, BF16),
                pltpu.SemaphoreType.DMA((3, 5)),
            ],
            smem=1,
            space=HBM,
            out_space=HBM if side else VMEM,
            flops=3e9,
        )(valid_count, *[in_hbm(a) for a in (source, edge_proj, edge_gate)])

    def flipped(array, bits):
        return lax.ppermute(array, BOTH, [(d, d ^ bits) for d in range(devices)])

    right, normed = edges(1, pair_act)
    right = lax.all_to_all(right, BOTH, split_axis=0, concat_axis=0, tiled=True)
    mine, theirs = edges(0, normed)
    left = call(pack_body, "pack", [shape((2,) + tile, BF16)] * len(offsets), 2)(
        mine, flipped(theirs, col_devices)
    )
    left = [flipped(part, offset) if offset else part for part, offset in zip(left, offsets)]
    tri_gating, source = call(
        gate_body, "tri_gate", [shape(turned_block, BF16)] * 2, 3, flops=2e9
    )(pair_act, normed, tri_gate)
    triangle_shape = (row_devices // 2, col_devices, own, rows, cols)
    (triangle,) = call(
        triangle_body,
        "triangle",
        [shape(triangle_shape, BF16)],
        1 + len(left),
        [pltpu.VMEM(triangle_shape, BF16), pltpu.SemaphoreType.DMA(())],
        out_space=HBM,
        flops=2e9,
    )(right.reshape((row_devices,) + triangle_shape[1:]), *left)
    triangle = in_half(triangle.reshape(share, own, rows, cols))
    bias_shape = (heads, rows, cols)
    updated, bias = call(
        update_body,
        "update",
        [shape(turned_block, BF16), shape(bias_shape, BF16)],
        5,
        [pltpu.VMEM((channels * rows, cols), F32), pltpu.VMEM((heads * rows, cols), F32)],
        flops=2e9,
    )(triangle.reshape(channels, rows, cols), source, tri_gating, tri_out, bias_proj)
    per_part = row_devices // col_devices
    parts = [bias] + [
        flipped(bias, flip * per_part * col_devices) for flip in range(1, col_devices)
    ]
    (dealt,) = call(
        deal_body, "deal_bias", [shape((per_part // 2 * col_devices,) + bias_shape, BF16)], col_devices
    )(*parts)
    one_core = []
    for part in range(col_devices):
        for core in range(2):
            members = range(part * per_part + core, (part + 1) * per_part, 2)
            one_core.append([r * col_devices + c for r in members for c in range(col_devices)])

    others = [
        lax.ppermute(updated, "ch", [((c + s) % col_devices, c) for c in range(col_devices)])
        for s in range(1, col_devices)
    ]
    bias = lax.all_to_all(
        dealt, BOTH, split_axis=0, concat_axis=0, axis_index_groups=one_core, tiled=True
    )

    mixed_shape = (rows, cols, 5 * channels)
    key_shape = (rows, cols, 2 * channels)
    (mixed,) = call(
        functools.partial(own_body, score_scale=(channels // heads) ** (-0.5)),
        "own_projections",
        [shape(mixed_shape, BF16)],
        2,
        [pltpu.VMEM(mixed_shape, BF16), pltpu.SemaphoreType.DMA((1, 2))],
        out_space=HBM,
        flops=3e9,
    )(updated, attn_proj)
    bias, *others = lax.optimization_barrier((bias, *others))
    mixed = call(
        other_body,
        "other_keys",
        [shape(mixed_shape, BF16)] + [shape(key_shape, BF16)] * len(others),
        2 + len(others),
        [pltpu.SemaphoreType.DMA(())],
        specs=[HBM] + [VMEM] * (1 + len(others)),
        flops=3e9,
    )(in_hbm(mixed), attn_proj, *others)
    (result,) = call(
        attend_body,
        "attend",
        [shape(block, BF16)],
        4 + col_devices,
        [
            pltpu.VMEM(block, BF16),
            pltpu.VMEM((heads * cols, col_devices * cols), F32),
            pltpu.SemaphoreType.DMA((1, rows // 2)),
        ],
        smem=1,
        out_space=HBM,
    )(valid_count, bias, flipped(bias, col_devices), attn_out, *mixed)
    return result


def solution(mesh):
    placed = (P("row", "ch", None), P(), P(), P(), P(), P(), P(), P(), P())
    return jax.shard_map(
        local, mesh=mesh, in_specs=placed, out_specs=P("row", "ch", None), check_vma=False
    )
```

```python
import functools
import math

import jax
import jax.numpy as jnp
from jax import lax
from jax.experimental import pallas as pl
from jax.experimental.pallas import tpu as pltpu
from jax.sharding import PartitionSpec as P

EPS = 1e-05
BOTH = ("row", "ch")
F32 = jnp.float32
BF16 = jnp.bfloat16
VMEM = pl.BlockSpec(memory_space=pltpu.VMEM)
SMEM = pl.BlockSpec(memory_space=pltpu.SMEM)
HBM = pl.BlockSpec(memory_space=pltpu.HBM)
ANY = pl.BlockSpec(memory_space=pl.ANY)


def layer_norm(values, axis):
    centre = values - jnp.mean(values, axis=axis, keepdims=True)
    spread = jnp.mean(centre * centre, axis=axis, keepdims=True)
    return centre * lax.rsqrt(spread + EPS)


def in_hbm(array):
    return pltpu.with_memory_space_constraint(array, pltpu.HBM)


def sigmoid(values):
    return 0.5 * jnp.tanh(0.5 * values) + 0.5


def dot(a, b, dims):
    return lax.dot_general(a, b, ((dims[:1], dims[1:]), ((), ())), preferred_element_type=F32)


def call(body, name, outs, ins, scratch=(), flops=1e8, smem=0, space=VMEM, out_space=VMEM, specs=None):
    sizes = [math.prod(a.shape) * a.dtype.itemsize for a in outs]
    spaces = out_space if isinstance(out_space, list) else [out_space] * len(outs)
    outs = [pltpu.HBM(a.shape, a.dtype) if b is HBM else a for a, b in zip(outs, spaces)]
    return pl.pallas_call(
        body,
        out_shape=outs,
        in_specs=specs or [SMEM] * smem + [space] * (ins - smem),
        out_specs=spaces,
        scratch_shapes=list(scratch),
        compiler_params=pltpu.CompilerParams(vmem_limit_bytes=16 * 2**20),
        cost_estimate=pl.CostEstimate(
            flops=int(flops), bytes_accessed=2 * sum(sizes), transcendentals=0
        ),
        name=name,
    )


def turned(weights):
    return weights.astype(F32).T.astype(BF16)


def run(copies):
    for copy in copies:
        copy.start()
    for copy in copies:
        copy.wait()


def place():
    per_half = lax.axis_size("row") // 2
    columns = lax.axis_size("ch")
    row = lax.rem(lax.axis_index("row"), per_half)
    core = lax.rem(row, 2)
    return (row - core) * columns + lax.axis_index("ch"), core


def chip_offsets():
    columns = lax.axis_size("ch")
    share = lax.axis_size("row") // 2 * columns
    return [o for o in range(share) if o // columns % 2 == 0]


def chunked(pairs, sems, first, chunks):
    rows = pairs[0][0].shape[0]
    size = rows // chunks
    return [
        [
            pltpu.make_async_copy(
                source.at[pl.ds(chunk * size, size)],
                target.at[pl.ds(chunk * size, size)],
                sems.at[first + k, chunk],
            )
            for k, (source, target) in enumerate(pairs)
        ]
        for chunk in range(chunks)
    ]


def edges_body(length, source_hbm, proj_hbm, gate_hbm, *rest, side):
    outs = rest[:-6]
    source, proj, gate, held, out, sems = rest[-6:]
    rows, cols, channels = source.shape
    share, own = out.shape[:2]
    columns = lax.axis_size("ch")
    span = pl.ds(side * channels, channels)
    fetches = [
        pltpu.make_async_copy(proj_hbm.at[:, span], proj, sems.at[0, 2]),
        pltpu.make_async_copy(gate_hbm.at[:, span], gate, sems.at[0, 3]),
    ]
    chunks = chunked([(source_hbm, source)], sems, 0, 2)
    for copy in fetches + chunks[0] + chunks[1]:
        copy.start()
    row_offset = lax.axis_index("row") * rows
    col_offset = lax.axis_index("ch") * cols
    count = length[0]
    tokens = col_offset + lax.broadcasted_iota(jnp.int32, (1, cols), 1)
    col_valid = jnp.where(tokens < count, 0.5, 0.0)
    for copy in fetches:
        copy.wait()
    weights = jnp.concatenate([turned(proj[...]), turned(gate[...])], axis=0)

    def step(row, carry):
        values = source[row]
        if side:
            values = layer_norm(values.astype(F32), -1).astype(BF16)
            source[row] = values
        mixed = dot(weights, values, (1, 1))
        valid = col_valid * (row_offset + row < count).astype(F32)
        twice = jnp.tanh(0.5 * mixed[channels:]) + 1.0
        held[pl.ds(row, channels, stride=rows), :] = twice * (mixed[:channels] * valid)
        return carry

    for (copy,) in chunks:
        copy.wait()
    lax.fori_loop(0, rows, step, 0, unroll=rows)
    sends = []
    if side:
        sends.append(pltpu.make_async_copy(source, outs[1], sems.at[1, 0]))
        sends[0].start()
    group = share // 4
    for device in range(share):
        part = held[device * own * rows : (device + 1) * own * rows, :].astype(BF16)
        position = share - 1 - device
        out[position] = part.reshape(own, rows, cols)
        if side and device % group == group - 1:
            for k in range(2):
                source_part = out.at[pl.ds(position, group)]
                target = outs[0].at[pl.ds(k * share + position, group)]
                sends.append(
                    pltpu.make_async_copy(source_part, target, sems.at[1 + k, 1 + device // group])
                )
                sends[-1].start()
    if not side:
        chip, core = place()
        for k, offset in enumerate(chip_offsets()):
            for other in range(2):
                index = jnp.bitwise_xor(chip, offset) + lax.rem(core + other, 2) * columns
                outs[other][k] = out[index]
    for copy in sends:
        copy.wait()


def pack_body(mine, sibling, *outs):
    _, core = place()
    for k, out in enumerate(outs):
        out[core] = mine[k]
        out[1 - core] = sibling[k]


def gate_body(pair, normed, weights, out, source):
    turned_weights = turned(weights[...])

    def step(row, carry):
        out[row] = sigmoid(dot(turned_weights, normed[row], (1, 1))).astype(BF16)
        source[row] = pair[row].astype(F32).T.astype(BF16)
        return carry

    lax.fori_loop(0, pair.shape[0], step, 0, unroll=2)


def triangle_body(right, *rest):
    parts, out, held, sent = rest[:-3], rest[-3], rest[-2], rest[-1]
    row_devices, col_devices, own, rows, cols = right.shape
    chip, _ = place()
    chip_row = lax.div(chip, col_devices)
    me = lax.axis_index("ch")
    groups = [(first, core) for first in range(0, row_devices // 2, 2) for core in range(2)]
    offsets = chip_offsets()
    for channel in range(own):
        left, whole = [], []
        for flip in range(col_devices):
            left.append(
                jnp.concatenate(
                    [
                        parts[offsets.index(first * col_devices + flip)][core, channel]
                        for first, core in groups
                    ],
                    axis=0,
                )
            )
            whole.append(right[:, jnp.bitwise_xor(me, flip), channel].reshape(-1, cols))
        triangle = dot(
            jnp.concatenate(left, axis=1), jnp.concatenate(whole, axis=1), (1, 1)
        ).astype(BF16)
        for k, (first, core) in enumerate(groups):
            for part in range(col_devices):
                row = row_devices // 2 - 1 - core - jnp.bitwise_xor(chip_row, first)
                held[row, col_devices - 1 - part, channel] = triangle[
                    k * rows : (k + 1) * rows, part * cols : (part + 1) * cols
                ]
    run([pltpu.make_async_copy(held, out, sent)])


def deal_body(*refs):
    parts, out = refs[:-1], refs[-1]
    columns = len(parts)
    per_part = lax.axis_size("row") // columns
    part = lax.div(lax.axis_index("row"), per_part)
    for col in range(columns):
        value = parts[0][...]
        for flip in range(1, columns):
            value = jnp.where(jnp.bitwise_xor(part, col) == flip, parts[flip][...], value)
        for chip in range(out.shape[0] // columns):
            out[chip * columns + col] = value


def spread_sum(values):
    lead = 8
    split = values.reshape((values.shape[0] // lead, lead) + values.shape[1:])
    return jnp.sum(jnp.sum(split, axis=0), axis=0, keepdims=True)


def update_body(triangle, source, gate, tri_out, bias_proj, updated, bias, held, bias_held):
    channels, rows, cols = triangle.shape
    heads = bias_proj.shape[1]
    values = triangle[...].astype(F32)
    centre = values - spread_sum(values) * (1.0 / channels)
    spread = spread_sum(centre * centre) * (1.0 / channels)
    held[...] = (centre * lax.rsqrt(spread + EPS)).reshape(channels * rows, cols)
    out_weights = turned(tri_out[...])
    bias_weights = turned(bias_proj[...])

    def step(row, carry):
        tri_normed = held[pl.ds(row, channels, stride=rows), :].astype(BF16)
        update = gate[row].astype(F32) * dot(out_weights, tri_normed, (1, 0))
        mine = (source[row].astype(F32) + update).astype(BF16)
        updated[row] = mine
        normed = layer_norm(mine.astype(F32), 0).astype(BF16)
        bias_held[pl.ds(row, heads, stride=rows), :] = dot(bias_weights, normed, (1, 0))
        return carry

    lax.fori_loop(0, rows, step, 0, unroll=8)
    bias[...] = bias_held[...].astype(BF16).reshape(heads, rows, cols)


def project(updated, attn_proj, mixed, row, score_scale, late=None):
    channels = updated.shape[1]
    values = updated[row].astype(F32)
    normed = layer_norm(values, 0)
    natural = normed.T.astype(BF16)

    def put(target, block, array):
        target[row, :, block * channels : (block + 1) * channels] = array.astype(BF16)

    put(mixed, 0, dot(turned(attn_proj[:, channels : 2 * channels]), normed.astype(BF16), (1, 0)))
    put(mixed, 1, dot(natural, attn_proj[:, 2 * channels : 3 * channels], (1, 0)))
    if late is not None:
        put(mixed, 2, dot(natural, attn_proj[:, :channels], (1, 0)) * score_scale)
        put(late, 0, sigmoid(dot(natural, attn_proj[:, 3 * channels :], (1, 0))))
        put(late, 1, values.T)


def own_body(updated, attn_proj, mixed, late_hbm, late, sems, *, score_scale):
    rows = updated.shape[0]

    def step(row, carry):
        project(updated, attn_proj, mixed, row, score_scale, late)
        return carry

    sends = chunked([(late, late_hbm)], sems, 0, 2)
    for chunk in range(2):
        lax.fori_loop(chunk * rows // 2, (chunk + 1) * rows // 2, step, 0, unroll=rows // 2)
        sends[chunk][0].start()
    for (copy,) in sends:
        copy.wait()


def other_body(late_hbm, attn_proj, *rest):
    pieces = (len(rest) - 2) // 2
    others, late, keys, sem = rest[:pieces], rest[pieces], rest[pieces + 1 : -1], rest[-1]
    fetch = pltpu.make_async_copy(late_hbm, late, sem)
    fetch.start()
    rows = late.shape[0]
    for updated, target in zip(others, keys):

        def step(row, carry):
            project(updated, attn_proj, target, row, None)
            return carry

        lax.fori_loop(0, rows, step, 0, unroll=rows // 2)
    fetch.wait()


def attend_body(length, mine, sibling, attn_out, late, *rest):
    mixed, (out_hbm, out, bias_held, sems) = rest[:-4], rest[-4:]
    pieces = len(mixed)
    rows, cols, channels = out.shape
    heads = mine.shape[1]
    me = lax.axis_index("ch")
    its_core = lax.rem(lax.axis_index("row"), 2)
    head_of = lax.broadcasted_iota(jnp.int32, (1, channels), 1) // (channels // heads)
    count = sems.shape[1]
    sends = chunked([(out, out_hbm)], sems, 0, count)
    chips = cols // rows // 2
    for piece in range(pieces):
        block = lax.rem(me + piece, pieces)
        token = block * cols + lax.broadcasted_iota(jnp.int32, (1, cols), 1)
        key_term = jnp.where(token < length[0], 0.0, -1e9)
        for part, core in ((mine, its_core), (sibling, 1 - its_core)):
            for chip in range(chips):
                tiles = part[chip * pieces + block]
                for head in range(heads):
                    first = pl.multiple_of(head * cols + (chip * 2 + core) * rows, rows)
                    bias_held[pl.ds(first, rows), piece * cols : (piece + 1) * cols] = (
                        tiles[head].astype(F32) + key_term
                    )
    both_of = jnp.concatenate([head_of, head_of], axis=1)
    masks = [(head_of == head).astype(BF16) for head in range(heads)]
    ones = jnp.ones((pieces * cols, channels), BF16)

    def load(row):
        keys = jnp.concatenate([part[row, :, :channels] for part in mixed], axis=1)
        values = jnp.concatenate([part[row, :, channels : 2 * channels] for part in mixed], axis=0)
        values = jnp.concatenate([values, ones], axis=1)
        return keys, values, mixed[0][row, :, 2 * channels :]

    def finish(row, total):
        attended = total[:, :channels] / total[:, channels:]
        gate = late[row, :, :channels].astype(F32)
        gated = (attended * gate).astype(BF16)
        residual = late[row, :, channels:].astype(F32)
        out[row] = (residual + dot(gated, attn_out[...], (1, 0))).astype(BF16)

    per_chunk = rows // count
    loaded, logits, weights = {}, {}, {}
    for time in range(rows + 2):
        row = time
        if row < rows:
            loaded[row] = load(row)
            keys, _, query = loaded[row]
            queries = jnp.concatenate([query * mask for mask in masks], axis=0)
            logits[row] = dot(queries, keys, (1, 0)) + bias_held[...]
        row = time - 1
        if 0 <= row < rows:
            scores = logits.pop(row)
            top = jnp.max(scores, axis=-1, keepdims=True)
            weights[row] = jnp.exp((scores - top).astype(BF16))
        row = time - 2
        if row >= 0:
            sums = dot(weights.pop(row), loaded.pop(row)[1], (1, 0))
            total = sums[:cols]
            for head in range(1, heads):
                total = jnp.where(both_of == head, sums[head * cols : (head + 1) * cols], total)
            finish(row, total)
            chunk, place_in = divmod(row, per_chunk)
            if place_in == per_chunk - 1:
                for copy in sends[chunk]:
                    copy.start()
    for send in sends:
        for copy in send:
            copy.wait()


def local(
    pair_act, valid_count, edge_proj, edge_gate, tri_gate, tri_out, attn_proj, bias_proj, attn_out
):
    rows, cols, channels = pair_act.shape
    heads = bias_proj.shape[1]
    row_devices = lax.axis_size("row")
    col_devices = lax.axis_size("ch")
    devices = row_devices * col_devices
    share = devices // 2
    own = channels // share
    everyone = list(reversed(range(devices)))
    halves = [everyone[share:], everyone[:share]]
    shape = jax.ShapeDtypeStruct
    block = (rows, cols, channels)
    turned_block = (rows, channels, cols)

    def in_half(array):
        return lax.all_to_all(
            array, BOTH, split_axis=0, concat_axis=0, axis_index_groups=halves, tiled=True
        )


    weight = pltpu.VMEM((channels, channels), BF16)
    offsets = chip_offsets()
    tile = (own, rows, cols)

    def edges(side, source):
        outs = [shape((devices,) + tile, BF16), shape(block, BF16)]
        return call(
            functools.partial(edges_body, side=side),
            "right_edges" if side else "left_edges",
            outs if side else [shape((len(offsets),) + tile, BF16)] * 2,
            4,
            [
                pltpu.VMEM(block, BF16),
                weight,
                weight,
                pltpu.VMEM((channels * rows, cols), F32),
                pltpu.VMEM((share,) + tile, BF16),
                pltpu.SemaphoreType.DMA((3, 5)),
            ],
            smem=1,
            space=HBM,
            out_space=HBM if side else VMEM,
            flops=3e9,
        )(valid_count, *[in_hbm(a) for a in (source, edge_proj, edge_gate)])

    def flipped(array, bits):
        return lax.ppermute(array, BOTH, [(d, d ^ bits) for d in range(devices)])

    right, normed = edges(1, pair_act)
    right = lax.all_to_all(right, BOTH, split_axis=0, concat_axis=0, tiled=True)
    mine, theirs = edges(0, normed)
    left = call(pack_body, "pack", [shape((2,) + tile, BF16)] * len(offsets), 2)(
        mine, flipped(theirs, col_devices)
    )
    left = [flipped(part, offset) if offset else part for part, offset in zip(left, offsets)]
    tri_gating, source = call(
        gate_body, "tri_gate", [shape(turned_block, BF16)] * 2, 3, flops=2e9
    )(pair_act, normed, tri_gate)
    triangle_shape = (row_devices // 2, col_devices, own, rows, cols)
    (triangle,) = call(
        triangle_body,
        "triangle",
        [shape(triangle_shape, BF16)],
        1 + len(left),
        [pltpu.VMEM(triangle_shape, BF16), pltpu.SemaphoreType.DMA(())],
        out_space=HBM,
        flops=2e9,
    )(right.reshape((row_devices,) + triangle_shape[1:]), *left)
    triangle = in_half(triangle.reshape(share, own, rows, cols))
    bias_shape = (heads, rows, cols)
    updated, bias = call(
        update_body,
        "update",
        [shape(turned_block, BF16), shape(bias_shape, BF16)],
        5,
        [pltpu.VMEM((channels * rows, cols), F32), pltpu.VMEM((heads * rows, cols), F32)],
        flops=2e9,
    )(triangle.reshape(channels, rows, cols), source, tri_gating, tri_out, bias_proj)
    per_part = row_devices // col_devices
    parts = [bias] + [
        flipped(bias, flip * per_part * col_devices) for flip in range(1, col_devices)
    ]
    (dealt,) = call(
        deal_body, "deal_bias", [shape((per_part // 2 * col_devices,) + bias_shape, BF16)], col_devices
    )(*parts)
    one_core = []
    for part in range(col_devices):
        for core in range(2):
            members = range(part * per_part + core, (part + 1) * per_part, 2)
            one_core.append([r * col_devices + c for r in members for c in range(col_devices)])

    others = [
        lax.ppermute(updated, "ch", [((c + s) % col_devices, c) for c in range(col_devices)])
        for s in range(1, col_devices)
    ]
    bias = lax.all_to_all(
        dealt, BOTH, split_axis=0, concat_axis=0, axis_index_groups=one_core, tiled=True
    )

    mixed_shape = (rows, cols, 3 * channels)
    key_shape = (rows, cols, 2 * channels)
    mixed, late = call(
        functools.partial(own_body, score_scale=(channels // heads) ** (-0.5)),
        "own_projections",
        [shape(mixed_shape, BF16), shape(key_shape, BF16)],
        2,
        [pltpu.VMEM(key_shape, BF16), pltpu.SemaphoreType.DMA((1, 2))],
        out_space=[VMEM, HBM],
        flops=3e9,
    )(updated, attn_proj)
    bias, *others = lax.optimization_barrier((bias, *others))
    late, *keys = call(
        other_body,
        "other_keys",
        [shape(key_shape, BF16)] * (1 + len(others)),
        2 + len(others),
        [pltpu.SemaphoreType.DMA(())],
        specs=[HBM] + [VMEM] * (1 + len(others)),
        flops=3e9,
    )(in_hbm(late), attn_proj, *others)
    (result,) = call(
        attend_body,
        "attend",
        [shape(block, BF16)],
        5 + col_devices,
        [
            pltpu.VMEM(block, BF16),
            pltpu.VMEM((heads * cols, col_devices * cols), F32),
            pltpu.SemaphoreType.DMA((1, rows // 2)),
        ],
        smem=1,
        out_space=HBM,
    )(valid_count, bias, flipped(bias, col_devices), attn_out, late, mixed, *keys)
    return result


def solution(mesh):
    placed = (P("row", "ch", None), P(), P(), P(), P(), P(), P(), P(), P())
    return jax.shard_map(
        local, mesh=mesh, in_specs=placed, out_specs=P("row", "ch", None), check_vma=False
    )
```

```python
import functools
import math

import jax
import jax.numpy as jnp
from jax import lax
from jax.experimental import pallas as pl
from jax.experimental.pallas import tpu as pltpu
from jax.sharding import PartitionSpec as P

EPS = 1e-05
BOTH = ("row", "ch")
F32 = jnp.float32
BF16 = jnp.bfloat16
VMEM = pl.BlockSpec(memory_space=pltpu.VMEM)
SMEM = pl.BlockSpec(memory_space=pltpu.SMEM)
HBM = pl.BlockSpec(memory_space=pltpu.HBM)
ANY = pl.BlockSpec(memory_space=pl.ANY)


def layer_norm(values, axis):
    centre = values - jnp.mean(values, axis=axis, keepdims=True)
    spread = jnp.mean(centre * centre, axis=axis, keepdims=True)
    return centre * lax.rsqrt(spread + EPS)


def in_hbm(array):
    return pltpu.with_memory_space_constraint(array, pltpu.HBM)


def sigmoid(values):
    return 0.5 * jnp.tanh(0.5 * values) + 0.5


def dot(a, b, dims):
    return lax.dot_general(a, b, ((dims[:1], dims[1:]), ((), ())), preferred_element_type=F32)


def call(body, name, outs, ins, scratch=(), flops=1e8, smem=0, space=VMEM, out_space=VMEM, specs=None):
    sizes = [math.prod(a.shape) * a.dtype.itemsize for a in outs]
    spaces = out_space if isinstance(out_space, list) else [out_space] * len(outs)
    outs = [pltpu.HBM(a.shape, a.dtype) if b is HBM else a for a, b in zip(outs, spaces)]
    return pl.pallas_call(
        body,
        out_shape=outs,
        in_specs=specs or [SMEM] * smem + [space] * (ins - smem),
        out_specs=spaces,
        scratch_shapes=list(scratch),
        compiler_params=pltpu.CompilerParams(vmem_limit_bytes=16 * 2**20),
        cost_estimate=pl.CostEstimate(
            flops=int(flops), bytes_accessed=2 * sum(sizes), transcendentals=0
        ),
        name=name,
    )


def turned(weights):
    return weights.astype(F32).T.astype(BF16)


def run(copies):
    for copy in copies:
        copy.start()
    for copy in copies:
        copy.wait()


def place():
    per_half = lax.axis_size("row") // 2
    columns = lax.axis_size("ch")
    row = lax.rem(lax.axis_index("row"), per_half)
    core = lax.rem(row, 2)
    return (row - core) * columns + lax.axis_index("ch"), core


def chip_offsets():
    columns = lax.axis_size("ch")
    share = lax.axis_size("row") // 2 * columns
    return [o for o in range(share) if o // columns % 2 == 0]


def chunked(pairs, sems, first, chunks):
    rows = pairs[0][0].shape[0]
    size = rows // chunks
    return [
        [
            pltpu.make_async_copy(
                source.at[pl.ds(chunk * size, size)],
                target.at[pl.ds(chunk * size, size)],
                sems.at[first + k, chunk],
            )
            for k, (source, target) in enumerate(pairs)
        ]
        for chunk in range(chunks)
    ]


def edges_body(length, source_hbm, proj_hbm, gate_hbm, *rest, side):
    outs = rest[:-6]
    source, proj, gate, held, out, sems = rest[-6:]
    rows, cols, channels = source.shape
    share, own = out.shape[:2]
    columns = lax.axis_size("ch")
    span = pl.ds(side * channels, channels)
    fetches = [
        pltpu.make_async_copy(proj_hbm.at[:, span], proj, sems.at[0, 2]),
        pltpu.make_async_copy(gate_hbm.at[:, span], gate, sems.at[0, 3]),
    ]
    chunks = chunked([(source_hbm, source)], sems, 0, 2)
    for copy in fetches + chunks[0] + chunks[1]:
        copy.start()
    row_offset = lax.axis_index("row") * rows
    col_offset = lax.axis_index("ch") * cols
    count = length[0]
    tokens = col_offset + lax.broadcasted_iota(jnp.int32, (1, cols), 1)
    col_valid = jnp.where(tokens < count, 0.5, 0.0)
    for copy in fetches:
        copy.wait()
    weights = jnp.concatenate([turned(proj[...]), turned(gate[...])], axis=0)

    def step(row, carry):
        values = source[row]
        if side:
            values = layer_norm(values.astype(F32), -1).astype(BF16)
            source[row] = values
        mixed = dot(weights, values, (1, 1))
        valid = col_valid * (row_offset + row < count).astype(F32)
        twice = jnp.tanh(0.5 * mixed[channels:]) + 1.0
        held[pl.ds(row, channels, stride=rows), :] = twice * (mixed[:channels] * valid)
        return carry

    for (copy,) in chunks:
        copy.wait()
    lax.fori_loop(0, rows, step, 0, unroll=rows)
    sends = []
    if side:
        sends.append(pltpu.make_async_copy(source, outs[1], sems.at[1, 0]))
        sends[0].start()
    group = share // 4
    for device in range(share):
        part = held[device * own * rows : (device + 1) * own * rows, :].astype(BF16)
        position = share - 1 - device
        out[position] = part.reshape(own, rows, cols)
        if side and device % group == group - 1:
            for k in range(2):
                source_part = out.at[pl.ds(position, group)]
                target = outs[0].at[pl.ds(k * share + position, group)]
                sends.append(
                    pltpu.make_async_copy(source_part, target, sems.at[1 + k, 1 + device // group])
                )
                sends[-1].start()
    if not side:
        chip, core = place()
        for k, offset in enumerate(chip_offsets()):
            for other in range(2):
                index = jnp.bitwise_xor(chip, offset) + lax.rem(core + other, 2) * columns
                outs[other][k] = out[index]
    for copy in sends:
        copy.wait()


def pack_body(mine, sibling, *outs):
    _, core = place()
    for k, out in enumerate(outs):
        out[core] = mine[k]
        out[1 - core] = sibling[k]


def gate_body(pair, normed, weights, out, source):
    turned_weights = turned(weights[...])

    def step(row, carry):
        out[row] = sigmoid(dot(turned_weights, normed[row], (1, 1))).astype(BF16)
        source[row] = pair[row].astype(F32).T.astype(BF16)
        return carry

    lax.fori_loop(0, pair.shape[0], step, 0, unroll=2)


def triangle_body(right, *rest):
    parts, out, held, sent = rest[:-3], rest[-3], rest[-2], rest[-1]
    row_devices, col_devices, own, rows, cols = right.shape
    chip, _ = place()
    chip_row = lax.div(chip, col_devices)
    me = lax.axis_index("ch")
    groups = [(first, core) for first in range(0, row_devices // 2, 2) for core in range(2)]
    offsets = chip_offsets()
    for channel in range(own):
        left, whole = [], []
        for flip in range(col_devices):
            left.append(
                jnp.concatenate(
                    [
                        parts[offsets.index(first * col_devices + flip)][core, channel]
                        for first, core in groups
                    ],
                    axis=0,
                )
            )
            whole.append(right[:, jnp.bitwise_xor(me, flip), channel].reshape(-1, cols))
        triangle = dot(
            jnp.concatenate(left, axis=1), jnp.concatenate(whole, axis=1), (1, 1)
        ).astype(BF16)
        for k, (first, core) in enumerate(groups):
            for part in range(col_devices):
                row = row_devices // 2 - 1 - core - jnp.bitwise_xor(chip_row, first)
                held[row, col_devices - 1 - part, channel] = triangle[
                    k * rows : (k + 1) * rows, part * cols : (part + 1) * cols
                ]
    run([pltpu.make_async_copy(held, out, sent)])


def deal_body(*refs):
    parts, out = refs[:-1], refs[-1]
    columns = len(parts)
    per_part = lax.axis_size("row") // columns
    part = lax.div(lax.axis_index("row"), per_part)
    for col in range(columns):
        value = parts[0][...]
        for flip in range(1, columns):
            value = jnp.where(jnp.bitwise_xor(part, col) == flip, parts[flip][...], value)
        for chip in range(out.shape[0] // columns):
            out[chip * columns + col] = value


def spread_sum(values):
    lead = 8
    split = values.reshape((values.shape[0] // lead, lead) + values.shape[1:])
    return jnp.sum(jnp.sum(split, axis=0), axis=0, keepdims=True)


def update_body(triangle, source, gate, tri_out, bias_proj, updated, bias, held, bias_held):
    channels, rows, cols = triangle.shape
    heads = bias_proj.shape[1]
    values = triangle[...].astype(F32)
    centre = values - spread_sum(values) * (1.0 / channels)
    spread = spread_sum(centre * centre) * (1.0 / channels)
    held[...] = (centre * lax.rsqrt(spread + EPS)).reshape(channels * rows, cols)
    out_weights = turned(tri_out[...])
    bias_weights = turned(bias_proj[...])

    def step(row, carry):
        tri_normed = held[pl.ds(row, channels, stride=rows), :].astype(BF16)
        update = gate[row].astype(F32) * dot(out_weights, tri_normed, (1, 0))
        mine = (source[row].astype(F32) + update).astype(BF16)
        updated[row] = mine
        normed = layer_norm(mine.astype(F32), 0).astype(BF16)
        bias_held[pl.ds(row, heads, stride=rows), :] = dot(bias_weights, normed, (1, 0))
        return carry

    lax.fori_loop(0, rows, step, 0, unroll=8)
    bias[...] = bias_held[...].astype(BF16).reshape(heads, rows, cols)


def project(updated, attn_proj, mixed, row, score_scale, late=None):
    channels = updated.shape[1]
    values = updated[row].astype(F32)
    normed = layer_norm(values, 0)
    natural = normed.T.astype(BF16)

    def put(target, block, array):
        target[row, :, block * channels : (block + 1) * channels] = array.astype(BF16)

    put(mixed, 0, dot(turned(attn_proj[:, channels : 2 * channels]), normed.astype(BF16), (1, 0)))
    put(mixed, 1, dot(natural, attn_proj[:, 2 * channels : 3 * channels], (1, 0)))
    if late is not None:
        put(mixed, 2, dot(natural, attn_proj[:, :channels], (1, 0)) * score_scale)
        put(late, 0, sigmoid(dot(natural, attn_proj[:, 3 * channels :], (1, 0))))
        put(late, 1, values.T)


def own_body(updated, attn_proj, mixed, late_hbm, late, sems, *, score_scale):
    rows = updated.shape[0]

    def step(row, carry):
        project(updated, attn_proj, mixed, row, score_scale, late)
        return carry

    sends = chunked([(late, late_hbm)], sems, 0, 2)
    for chunk in range(2):
        lax.fori_loop(chunk * rows // 2, (chunk + 1) * rows // 2, step, 0, unroll=rows // 2)
        sends[chunk][0].start()
    for (copy,) in sends:
        copy.wait()


def other_body(late_hbm, attn_proj, *rest):
    pieces = (len(rest) - 2) // 2
    others, late, keys, sem = rest[:pieces], rest[pieces], rest[pieces + 1 : -1], rest[-1]
    fetch = pltpu.make_async_copy(late_hbm, late, sem)
    fetch.start()
    rows = late.shape[0]
    for updated, target in zip(others, keys):

        def step(row, carry):
            project(updated, attn_proj, target, row, None)
            return carry

        lax.fori_loop(0, rows, step, 0, unroll=rows // 2)
    fetch.wait()


def attend_body(length, mine, sibling, attn_out, late, *rest):
    mixed, (out_hbm, out, bias_held, sems) = rest[:-4], rest[-4:]
    pieces = len(mixed)
    rows, cols, channels = out.shape
    heads = mine.shape[1]
    me = lax.axis_index("ch")
    its_core = lax.rem(lax.axis_index("row"), 2)
    head_of = lax.broadcasted_iota(jnp.int32, (1, channels), 1) // (channels // heads)
    count = sems.shape[1]
    sends = chunked([(out, out_hbm)], sems, 0, count)
    chips = cols // rows // 2
    for piece in range(pieces):
        block = lax.rem(me + piece, pieces)
        token = block * cols + lax.broadcasted_iota(jnp.int32, (1, cols), 1)
        key_term = jnp.where(token < length[0], 0.0, -1e9)
        for part, core in ((mine, its_core), (sibling, 1 - its_core)):
            for chip in range(chips):
                tiles = part[chip * pieces + block]
                for head in range(heads):
                    first = pl.multiple_of(head * cols + (chip * 2 + core) * rows, rows)
                    bias_held[pl.ds(first, rows), piece * cols : (piece + 1) * cols] = (
                        tiles[head].astype(F32) + key_term
                    )
    both_of = jnp.concatenate([head_of, head_of], axis=1)
    masks = [(head_of == head).astype(BF16) for head in range(heads)]
    ones = jnp.ones((pieces * cols, channels), BF16)

    def load(row):
        keys = jnp.concatenate([part[row, :, :channels] for part in mixed], axis=1)
        values = jnp.concatenate([part[row, :, channels : 2 * channels] for part in mixed], axis=0)
        values = jnp.concatenate([values, ones], axis=1)
        return keys, values, mixed[0][row, :, 2 * channels :]

    def finish(row, total):
        weight = total[:, channels:]
        inverse = pl.reciprocal(weight, approx=True)
        attended = total[:, :channels] * (inverse * (2.0 - weight * inverse))
        gate = late[row, :, :channels].astype(F32)
        gated = (attended * gate).astype(BF16)
        residual = late[row, :, channels:].astype(F32)
        out[row] = (residual + dot(gated, attn_out[...], (1, 0))).astype(BF16)

    per_chunk = rows // count
    loaded, logits, weights, total = {}, {}, {}, None
    group = 2
    per_row = heads // group
    units = rows * per_row
    for time in range(units + 2):
        if time < units:
            row, first = divmod(time, per_row)
            if first == 0:
                loaded[row] = load(row)
            keys, _, query = loaded[row]
            mine = masks[first * group : (first + 1) * group]
            queries = jnp.concatenate([query * mask for mask in mine], axis=0)
            span = slice(first * group * cols, (first + 1) * group * cols)
            logits[time] = dot(queries, keys, (1, 0)) + bias_held[span]
        if 0 <= time - 1 < units:
            scores = logits.pop(time - 1)
            top = jnp.max(scores, axis=-1, keepdims=True)
            weights[time - 1] = jnp.exp((scores - top).astype(BF16))
        if time >= 2:
            row, first = divmod(time - 2, per_row)
            sums = dot(weights.pop(time - 2), loaded[row][1], (1, 0))
            for k in range(group):
                head = first * group + k
                mine = sums[k * cols : (k + 1) * cols]
                total = mine if head == 0 else jnp.where(both_of == head, mine, total)
            if first == per_row - 1:
                finish(row, total)
                loaded.pop(row)
                chunk, place_in = divmod(row, per_chunk)
                if place_in == per_chunk - 1:
                    for copy in sends[chunk]:
                        copy.start()
    for send in sends:
        for copy in send:
            copy.wait()


def local(
    pair_act, valid_count, edge_proj, edge_gate, tri_gate, tri_out, attn_proj, bias_proj, attn_out
):
    rows, cols, channels = pair_act.shape
    heads = bias_proj.shape[1]
    row_devices = lax.axis_size("row")
    col_devices = lax.axis_size("ch")
    devices = row_devices * col_devices
    share = devices // 2
    own = channels // share
    everyone = list(reversed(range(devices)))
    halves = [everyone[share:], everyone[:share]]
    shape = jax.ShapeDtypeStruct
    block = (rows, cols, channels)
    turned_block = (rows, channels, cols)

    def in_half(array):
        return lax.all_to_all(
            array, BOTH, split_axis=0, concat_axis=0, axis_index_groups=halves, tiled=True
        )


    weight = pltpu.VMEM((channels, channels), BF16)
    offsets = chip_offsets()
    tile = (own, rows, cols)

    def edges(side, source):
        outs = [shape((devices,) + tile, BF16), shape(block, BF16)]
        return call(
            functools.partial(edges_body, side=side),
            "right_edges" if side else "left_edges",
            outs if side else [shape((len(offsets),) + tile, BF16)] * 2,
            4,
            [
                pltpu.VMEM(block, BF16),
                weight,
                weight,
                pltpu.VMEM((channels * rows, cols), F32),
                pltpu.VMEM((share,) + tile, BF16),
                pltpu.SemaphoreType.DMA((3, 5)),
            ],
            smem=1,
            space=HBM,
            out_space=HBM if side else VMEM,
            flops=3e9,
        )(valid_count, *[in_hbm(a) for a in (source, edge_proj, edge_gate)])

    def flipped(array, bits):
        return lax.ppermute(array, BOTH, [(d, d ^ bits) for d in range(devices)])

    right, normed = edges(1, pair_act)
    right = lax.all_to_all(right, BOTH, split_axis=0, concat_axis=0, tiled=True)
    mine, theirs = edges(0, normed)
    left = call(pack_body, "pack", [shape((2,) + tile, BF16)] * len(offsets), 2)(
        mine, flipped(theirs, col_devices)
    )
    left = [flipped(part, offset) if offset else part for part, offset in zip(left, offsets)]
    tri_gating, source = call(
        gate_body, "tri_gate", [shape(turned_block, BF16)] * 2, 3, flops=2e9
    )(pair_act, normed, tri_gate)
    triangle_shape = (row_devices // 2, col_devices, own, rows, cols)
    (triangle,) = call(
        triangle_body,
        "triangle",
        [shape(triangle_shape, BF16)],
        1 + len(left),
        [pltpu.VMEM(triangle_shape, BF16), pltpu.SemaphoreType.DMA(())],
        out_space=HBM,
        flops=2e9,
    )(right.reshape((row_devices,) + triangle_shape[1:]), *left)
    triangle = in_half(triangle.reshape(share, own, rows, cols))
    bias_shape = (heads, rows, cols)
    updated, bias = call(
        update_body,
        "update",
        [shape(turned_block, BF16), shape(bias_shape, BF16)],
        5,
        [pltpu.VMEM((channels * rows, cols), F32), pltpu.VMEM((heads * rows, cols), F32)],
        flops=2e9,
    )(triangle.reshape(channels, rows, cols), source, tri_gating, tri_out, bias_proj)
    per_part = row_devices // col_devices
    parts = [bias] + [
        flipped(bias, flip * per_part * col_devices) for flip in range(1, col_devices)
    ]
    (dealt,) = call(
        deal_body, "deal_bias", [shape((per_part // 2 * col_devices,) + bias_shape, BF16)], col_devices
    )(*parts)
    one_core = []
    for part in range(col_devices):
        for core in range(2):
            members = range(part * per_part + core, (part + 1) * per_part, 2)
            one_core.append([r * col_devices + c for r in members for c in range(col_devices)])

    others = [
        lax.ppermute(updated, "ch", [((c + s) % col_devices, c) for c in range(col_devices)])
        for s in range(1, col_devices)
    ]
    bias = lax.all_to_all(
        dealt, BOTH, split_axis=0, concat_axis=0, axis_index_groups=one_core, tiled=True
    )

    mixed_shape = (rows, cols, 3 * channels)
    key_shape = (rows, cols, 2 * channels)
    mixed, late = call(
        functools.partial(own_body, score_scale=(channels // heads) ** (-0.5)),
        "own_projections",
        [shape(mixed_shape, BF16), shape(key_shape, BF16)],
        2,
        [pltpu.VMEM(key_shape, BF16), pltpu.SemaphoreType.DMA((1, 2))],
        out_space=[VMEM, HBM],
        flops=3e9,
    )(updated, attn_proj)
    bias, *others = lax.optimization_barrier((bias, *others))
    late, *keys = call(
        other_body,
        "other_keys",
        [shape(key_shape, BF16)] * (1 + len(others)),
        2 + len(others),
        [pltpu.SemaphoreType.DMA(())],
        specs=[HBM] + [VMEM] * (1 + len(others)),
        flops=3e9,
    )(in_hbm(late), attn_proj, *others)
    (result,) = call(
        attend_body,
        "attend",
        [shape(block, BF16)],
        5 + col_devices,
        [
            pltpu.VMEM(block, BF16),
            pltpu.VMEM((heads * cols, col_devices * cols), F32),
            pltpu.SemaphoreType.DMA((1, rows // 2)),
        ],
        smem=1,
        out_space=HBM,
    )(valid_count, bias, flipped(bias, col_devices), attn_out, late, mixed, *keys)
    return result


def solution(mesh):
    placed = (P("row", "ch", None), P(), P(), P(), P(), P(), P(), P(), P())
    return jax.shard_map(
        local, mesh=mesh, in_specs=placed, out_specs=P("row", "ch", None), check_vma=False
    )
```

```python
import functools
import math

import jax
import jax.numpy as jnp
from jax import lax
from jax.experimental import pallas as pl
from jax.experimental.pallas import tpu as pltpu
from jax.sharding import PartitionSpec as P

EPS = 1e-05
BOTH = ("row", "ch")
F32 = jnp.float32
BF16 = jnp.bfloat16
VMEM = pl.BlockSpec(memory_space=pltpu.VMEM)
SMEM = pl.BlockSpec(memory_space=pltpu.SMEM)
HBM = pl.BlockSpec(memory_space=pltpu.HBM)
ANY = pl.BlockSpec(memory_space=pl.ANY)


def layer_norm(values, axis):
    centre = values - jnp.mean(values, axis=axis, keepdims=True)
    spread = jnp.mean(centre * centre, axis=axis, keepdims=True)
    return centre * lax.rsqrt(spread + EPS)


def in_hbm(array):
    return pltpu.with_memory_space_constraint(array, pltpu.HBM)


def sigmoid(values):
    return 0.5 * jnp.tanh(0.5 * values) + 0.5


def dot(a, b, dims):
    return lax.dot_general(a, b, ((dims[:1], dims[1:]), ((), ())), preferred_element_type=F32)


def call(body, name, outs, ins, scratch=(), flops=1e8, smem=0, space=VMEM, out_space=VMEM, specs=None):
    sizes = [math.prod(a.shape) * a.dtype.itemsize for a in outs]
    spaces = out_space if isinstance(out_space, list) else [out_space] * len(outs)
    outs = [pltpu.HBM(a.shape, a.dtype) if b is HBM else a for a, b in zip(outs, spaces)]
    return pl.pallas_call(
        body,
        out_shape=outs,
        in_specs=specs or [SMEM] * smem + [space] * (ins - smem),
        out_specs=spaces,
        scratch_shapes=list(scratch),
        compiler_params=pltpu.CompilerParams(vmem_limit_bytes=16 * 2**20),
        cost_estimate=pl.CostEstimate(
            flops=int(flops), bytes_accessed=2 * sum(sizes), transcendentals=0
        ),
        name=name,
    )


def turned(weights):
    return weights.astype(F32).T.astype(BF16)


def run(copies):
    for copy in copies:
        copy.start()
    for copy in copies:
        copy.wait()


def place():
    per_half = lax.axis_size("row") // 2
    columns = lax.axis_size("ch")
    row = lax.rem(lax.axis_index("row"), per_half)
    core = lax.rem(row, 2)
    return (row - core) * columns + lax.axis_index("ch"), core


def chip_offsets():
    columns = lax.axis_size("ch")
    share = lax.axis_size("row") // 2 * columns
    return [o for o in range(share) if o // columns % 2 == 0]


def chunked(pairs, sems, first, chunks):
    rows = pairs[0][0].shape[0]
    size = rows // chunks
    return [
        [
            pltpu.make_async_copy(
                source.at[pl.ds(chunk * size, size)],
                target.at[pl.ds(chunk * size, size)],
                sems.at[first + k, chunk],
            )
            for k, (source, target) in enumerate(pairs)
        ]
        for chunk in range(chunks)
    ]


def edges_body(length, source_hbm, proj_hbm, gate_hbm, *rest, side):
    outs = rest[:-6]
    source, proj, gate, held, out, sems = rest[-6:]
    rows, cols, channels = source.shape
    share, own = out.shape[:2]
    columns = lax.axis_size("ch")
    span = pl.ds(side * channels, channels)
    fetches = [
        pltpu.make_async_copy(proj_hbm.at[:, span], proj, sems.at[0, 2]),
        pltpu.make_async_copy(gate_hbm.at[:, span], gate, sems.at[0, 3]),
    ]
    chunks = chunked([(source_hbm, source)], sems, 0, 2)
    for copy in fetches + chunks[0] + chunks[1]:
        copy.start()
    row_offset = lax.axis_index("row") * rows
    col_offset = lax.axis_index("ch") * cols
    count = length[0]
    tokens = col_offset + lax.broadcasted_iota(jnp.int32, (1, cols), 1)
    col_valid = jnp.where(tokens < count, 0.5, 0.0)
    for copy in fetches:
        copy.wait()
    weights = jnp.concatenate([turned(proj[...]), turned(gate[...])], axis=0)

    def step(row, carry):
        values = source[row]
        if side:
            values = layer_norm(values.astype(F32), -1).astype(BF16)
            source[row] = values
        mixed = dot(weights, values, (1, 1))
        valid = col_valid * (row_offset + row < count).astype(F32)
        twice = jnp.tanh(0.5 * mixed[channels:]) + 1.0
        held[pl.ds(row, channels, stride=rows), :] = twice * (mixed[:channels] * valid)
        return carry

    for (copy,) in chunks:
        copy.wait()
    lax.fori_loop(0, rows, step, 0, unroll=rows)
    sends = []
    if side:
        sends.append(pltpu.make_async_copy(source, outs[1], sems.at[1, 0]))
        sends[0].start()
    group = share // 4
    for device in range(share):
        part = held[device * own * rows : (device + 1) * own * rows, :].astype(BF16)
        position = share - 1 - device
        out[position] = part.reshape(own, rows, cols)
        if side and device % group == group - 1:
            for k in range(2):
                source_part = out.at[pl.ds(position, group)]
                target = outs[0].at[pl.ds(k * share + position, group)]
                sends.append(
                    pltpu.make_async_copy(source_part, target, sems.at[1 + k, 1 + device // group])
                )
                sends[-1].start()
    if not side:
        chip, core = place()
        for k, offset in enumerate(chip_offsets()):
            for other in range(2):
                index = jnp.bitwise_xor(chip, offset) + lax.rem(core + other, 2) * columns
                outs[other][k] = out[index]
    for copy in sends:
        copy.wait()


def pack_body(mine, sibling, *outs):
    _, core = place()
    for k, out in enumerate(outs):
        out[core] = mine[k]
        out[1 - core] = sibling[k]


def gate_body(pair, normed, weights, out, source):
    turned_weights = turned(weights[...])

    def step(row, carry):
        out[row] = sigmoid(dot(turned_weights, normed[row], (1, 1))).astype(BF16)
        source[row] = pair[row].astype(F32).T.astype(BF16)
        return carry

    lax.fori_loop(0, pair.shape[0], step, 0, unroll=2)


def triangle_body(right, *rest):
    parts, held = rest[:-1], rest[-1]
    row_devices, col_devices, own, rows, cols = right.shape
    chip, _ = place()
    chip_row = lax.div(chip, col_devices)
    me = lax.axis_index("ch")
    groups = [(first, core) for first in range(0, row_devices // 2, 2) for core in range(2)]
    offsets = chip_offsets()
    for channel in range(own):
        left, whole = [], []
        for flip in range(col_devices):
            left.append(
                jnp.concatenate(
                    [
                        parts[offsets.index(first * col_devices + flip)][core, channel]
                        for first, core in groups
                    ],
                    axis=0,
                )
            )
            whole.append(right[:, jnp.bitwise_xor(me, flip), channel].reshape(-1, cols))
        triangle = dot(
            jnp.concatenate(left, axis=1), jnp.concatenate(whole, axis=1), (1, 1)
        ).astype(BF16)
        for k, (first, core) in enumerate(groups):
            for part in range(col_devices):
                row = row_devices // 2 - 1 - core - jnp.bitwise_xor(chip_row, first)
                held[row, col_devices - 1 - part, channel] = triangle[
                    k * rows : (k + 1) * rows, part * cols : (part + 1) * cols
                ]


def deal_body(*refs):
    parts, out = refs[:-1], refs[-1]
    columns = len(parts)
    per_part = lax.axis_size("row") // columns
    part = lax.div(lax.axis_index("row"), per_part)
    for col in range(columns):
        value = parts[0][...]
        for flip in range(1, columns):
            value = jnp.where(jnp.bitwise_xor(part, col) == flip, parts[flip][...], value)
        for chip in range(out.shape[0] // columns):
            out[chip * columns + col] = value


def spread_sum(values):
    lead = 8
    split = values.reshape((values.shape[0] // lead, lead) + values.shape[1:])
    return jnp.sum(jnp.sum(split, axis=0), axis=0, keepdims=True)


def update_body(triangle, source, gate, tri_out, bias_proj, updated, bias, held, bias_held):
    channels, rows, cols = triangle.shape
    heads = bias_proj.shape[1]
    values = triangle[...].astype(F32)
    centre = values - spread_sum(values) * (1.0 / channels)
    spread = spread_sum(centre * centre) * (1.0 / channels)
    held[...] = (centre * lax.rsqrt(spread + EPS)).reshape(channels * rows, cols)
    out_weights = turned(tri_out[...])
    bias_weights = turned(bias_proj[...])

    def step(row, carry):
        tri_normed = held[pl.ds(row, channels, stride=rows), :].astype(BF16)
        update = gate[row].astype(F32) * dot(out_weights, tri_normed, (1, 0))
        mine = (source[row].astype(F32) + update).astype(BF16)
        updated[row] = mine
        normed = layer_norm(mine.astype(F32), 0).astype(BF16)
        bias_held[pl.ds(row, heads, stride=rows), :] = dot(bias_weights, normed, (1, 0))
        return carry

    lax.fori_loop(0, rows, step, 0, unroll=8)
    bias[...] = bias_held[...].astype(BF16).reshape(heads, rows, cols)


def project(updated, attn_proj, mixed, row, score_scale, late=None):
    channels = updated.shape[1]
    values = updated[row].astype(F32)
    normed = layer_norm(values, 0)
    natural = normed.T.astype(BF16)

    def put(target, block, array):
        target[row, :, block * channels : (block + 1) * channels] = array.astype(BF16)

    put(mixed, 0, dot(turned(attn_proj[:, channels : 2 * channels]), normed.astype(BF16), (1, 0)))
    put(mixed, 1, dot(natural, attn_proj[:, 2 * channels : 3 * channels], (1, 0)))
    if late is not None:
        put(mixed, 2, dot(natural, attn_proj[:, :channels], (1, 0)) * score_scale)
        put(late, 0, sigmoid(dot(natural, attn_proj[:, 3 * channels :], (1, 0))))
        put(late, 1, values.T)


def own_body(updated, attn_proj, mixed, late_hbm, late, sems, *, score_scale):
    rows = updated.shape[0]

    def step(row, carry):
        project(updated, attn_proj, mixed, row, score_scale, late)
        return carry

    sends = chunked([(late, late_hbm)], sems, 0, 2)
    for chunk in range(2):
        lax.fori_loop(chunk * rows // 2, (chunk + 1) * rows // 2, step, 0, unroll=rows // 2)
        sends[chunk][0].start()
    for (copy,) in sends:
        copy.wait()


def other_body(late_hbm, attn_proj, *rest):
    pieces = (len(rest) - 2) // 2
    others, late, keys, sem = rest[:pieces], rest[pieces], rest[pieces + 1 : -1], rest[-1]
    fetch = pltpu.make_async_copy(late_hbm, late, sem)
    fetch.start()
    rows = late.shape[0]
    for updated, target in zip(others, keys):

        def step(row, carry):
            project(updated, attn_proj, target, row, None)
            return carry

        lax.fori_loop(0, rows, step, 0, unroll=rows // 2)
    fetch.wait()


def attend_body(length, mine, sibling, attn_out, late, *rest):
    mixed, (out_hbm, out, bias_held, sems) = rest[:-4], rest[-4:]
    pieces = len(mixed)
    rows, cols, channels = out.shape
    heads = mine.shape[1]
    me = lax.axis_index("ch")
    its_core = lax.rem(lax.axis_index("row"), 2)
    head_of = lax.broadcasted_iota(jnp.int32, (1, channels), 1) // (channels // heads)
    count = sems.shape[1]
    sends = chunked([(out, out_hbm)], sems, 0, count)
    chips = cols // rows // 2
    for piece in range(pieces):
        block = lax.rem(me + piece, pieces)
        token = block * cols + lax.broadcasted_iota(jnp.int32, (1, cols), 1)
        key_term = jnp.where(token < length[0], 0.0, -1e9)
        for part, core in ((mine, its_core), (sibling, 1 - its_core)):
            for chip in range(chips):
                tiles = part[chip * pieces + block]
                for head in range(heads):
                    first = pl.multiple_of(head * cols + (chip * 2 + core) * rows, rows)
                    bias_held[pl.ds(first, rows), piece * cols : (piece + 1) * cols] = (
                        tiles[head].astype(F32) + key_term
                    )
    both_of = jnp.concatenate([head_of, head_of], axis=1)
    masks = [(head_of == head).astype(BF16) for head in range(heads)]
    ones = jnp.ones((pieces * cols, channels), BF16)

    def load(row):
        keys = jnp.concatenate([part[row, :, :channels] for part in mixed], axis=1)
        values = jnp.concatenate([part[row, :, channels : 2 * channels] for part in mixed], axis=0)
        values = jnp.concatenate([values, ones], axis=1)
        return keys, values, mixed[0][row, :, 2 * channels :]

    def finish(row, total):
        attended = total[:, :channels] / total[:, channels:]
        gate = late[row, :, :channels].astype(F32)
        gated = (attended * gate).astype(BF16)
        residual = late[row, :, channels:].astype(F32)
        out[row] = (residual + dot(gated, attn_out[...], (1, 0))).astype(BF16)

    per_chunk = rows // count
    loaded, logits, weights = {}, {}, {}
    for time in range(rows + 2):
        row = time
        if row < rows:
            loaded[row] = load(row)
            keys, _, query = loaded[row]
            queries = jnp.concatenate([query * mask for mask in masks], axis=0)
            logits[row] = dot(queries, keys, (1, 0)) + bias_held[...]
        row = time - 1
        if 0 <= row < rows:
            scores = logits.pop(row)
            top = jnp.max(scores, axis=-1, keepdims=True)
            weights[row] = jnp.exp((scores - top).astype(BF16))
        row = time - 2
        if row >= 0:
            sums = dot(weights.pop(row), loaded.pop(row)[1], (1, 0))
            total = sums[:cols]
            for head in range(1, heads):
                total = jnp.where(both_of == head, sums[head * cols : (head + 1) * cols], total)
            finish(row, total)
            chunk, place_in = divmod(row, per_chunk)
            if place_in == per_chunk - 1:
                for copy in sends[chunk]:
                    copy.start()
    for send in sends:
        for copy in send:
            copy.wait()


def local(
    pair_act, valid_count, edge_proj, edge_gate, tri_gate, tri_out, attn_proj, bias_proj, attn_out
):
    rows, cols, channels = pair_act.shape
    heads = bias_proj.shape[1]
    row_devices = lax.axis_size("row")
    col_devices = lax.axis_size("ch")
    devices = row_devices * col_devices
    share = devices // 2
    own = channels // share
    everyone = list(reversed(range(devices)))
    halves = [everyone[share:], everyone[:share]]
    shape = jax.ShapeDtypeStruct
    block = (rows, cols, channels)
    turned_block = (rows, channels, cols)

    def in_half(array):
        return lax.all_to_all(
            array, BOTH, split_axis=0, concat_axis=0, axis_index_groups=halves, tiled=True
        )


    weight = pltpu.VMEM((channels, channels), BF16)
    offsets = chip_offsets()
    tile = (own, rows, cols)

    def edges(side, source):
        outs = [shape((devices,) + tile, BF16), shape(block, BF16)]
        return call(
            functools.partial(edges_body, side=side),
            "right_edges" if side else "left_edges",
            outs if side else [shape((len(offsets),) + tile, BF16)] * 2,
            4,
            [
                pltpu.VMEM(block, BF16),
                weight,
                weight,
                pltpu.VMEM((channels * rows, cols), F32),
                pltpu.VMEM((share,) + tile, BF16),
                pltpu.SemaphoreType.DMA((3, 5)),
            ],
            smem=1,
            space=HBM,
            out_space=HBM if side else VMEM,
            flops=3e9,
        )(valid_count, *[in_hbm(a) for a in (source, edge_proj, edge_gate)])

    def flipped(array, bits):
        return lax.ppermute(array, BOTH, [(d, d ^ bits) for d in range(devices)])

    right, normed = edges(1, pair_act)
    right = lax.all_to_all(right, BOTH, split_axis=0, concat_axis=0, tiled=True)
    mine, theirs = edges(0, normed)
    left = call(pack_body, "pack", [shape((2,) + tile, BF16)] * len(offsets), 2)(
        mine, flipped(theirs, col_devices)
    )
    left = [flipped(part, offset) if offset else part for part, offset in zip(left, offsets)]
    tri_gating, source = call(
        gate_body, "tri_gate", [shape(turned_block, BF16)] * 2, 3, flops=2e9
    )(pair_act, normed, tri_gate)
    tri_gating, source, *left = lax.optimization_barrier((tri_gating, source, *left))
    triangle_shape = (row_devices // 2, col_devices, own, rows, cols)
    (triangle,) = call(
        triangle_body,
        "triangle",
        [shape(triangle_shape, BF16)],
        1 + len(left),
        flops=2e9,
    )(right.reshape((row_devices,) + triangle_shape[1:]), *left)
    triangle = in_half(triangle.reshape(share, own, rows, cols))
    bias_shape = (heads, rows, cols)
    updated, bias = call(
        update_body,
        "update",
        [shape(turned_block, BF16), shape(bias_shape, BF16)],
        5,
        [pltpu.VMEM((channels * rows, cols), F32), pltpu.VMEM((heads * rows, cols), F32)],
        flops=2e9,
    )(triangle.reshape(channels, rows, cols), source, tri_gating, tri_out, bias_proj)
    per_part = row_devices // col_devices
    parts = [bias] + [
        flipped(bias, flip * per_part * col_devices) for flip in range(1, col_devices)
    ]
    (dealt,) = call(
        deal_body, "deal_bias", [shape((per_part // 2 * col_devices,) + bias_shape, BF16)], col_devices
    )(*parts)
    one_core = []
    for part in range(col_devices):
        for core in range(2):
            members = range(part * per_part + core, (part + 1) * per_part, 2)
            one_core.append([r * col_devices + c for r in members for c in range(col_devices)])

    others = [
        lax.ppermute(updated, "ch", [((c + s) % col_devices, c) for c in range(col_devices)])
        for s in range(1, col_devices)
    ]
    bias = lax.all_to_all(
        dealt, BOTH, split_axis=0, concat_axis=0, axis_index_groups=one_core, tiled=True
    )

    mixed_shape = (rows, cols, 3 * channels)
    key_shape = (rows, cols, 2 * channels)
    mixed, late = call(
        functools.partial(own_body, score_scale=(channels // heads) ** (-0.5)),
        "own_projections",
        [shape(mixed_shape, BF16), shape(key_shape, BF16)],
        2,
        [pltpu.VMEM(key_shape, BF16), pltpu.SemaphoreType.DMA((1, 2))],
        out_space=[VMEM, HBM],
        flops=3e9,
    )(updated, attn_proj)
    bias, *others = lax.optimization_barrier((bias, *others))
    late, *keys = call(
        other_body,
        "other_keys",
        [shape(key_shape, BF16)] * (1 + len(others)),
        2 + len(others),
        [pltpu.SemaphoreType.DMA(())],
        specs=[HBM] + [VMEM] * (1 + len(others)),
        flops=3e9,
    )(in_hbm(late), attn_proj, *others)
    (result,) = call(
        attend_body,
        "attend",
        [shape(block, BF16)],
        5 + col_devices,
        [
            pltpu.VMEM(block, BF16),
            pltpu.VMEM((heads * cols, col_devices * cols), F32),
            pltpu.SemaphoreType.DMA((1, rows // 2)),
        ],
        smem=1,
        out_space=HBM,
    )(valid_count, bias, flipped(bias, col_devices), attn_out, late, mixed, *keys)
    return result


def solution(mesh):
    placed = (P("row", "ch", None), P(), P(), P(), P(), P(), P(), P(), P())
    return jax.shard_map(
        local, mesh=mesh, in_specs=placed, out_specs=P("row", "ch", None), check_vma=False
    )
```

```python
import functools
import math

import jax
import jax.numpy as jnp
from jax import lax
from jax.experimental import pallas as pl
from jax.experimental.pallas import tpu as pltpu
from jax.sharding import PartitionSpec as P

EPS = 1e-05
BOTH = ("row", "ch")
F32 = jnp.float32
BF16 = jnp.bfloat16
VMEM = pl.BlockSpec(memory_space=pltpu.VMEM)
SMEM = pl.BlockSpec(memory_space=pltpu.SMEM)
HBM = pl.BlockSpec(memory_space=pltpu.HBM)
ANY = pl.BlockSpec(memory_space=pl.ANY)


def layer_norm(values, axis):
    centre = values - jnp.mean(values, axis=axis, keepdims=True)
    spread = jnp.mean(centre * centre, axis=axis, keepdims=True)
    return centre * lax.rsqrt(spread + EPS)


def in_hbm(array):
    return pltpu.with_memory_space_constraint(array, pltpu.HBM)


def sigmoid(values):
    return 0.5 * jnp.tanh(0.5 * values) + 0.5


def dot(a, b, dims):
    return lax.dot_general(a, b, ((dims[:1], dims[1:]), ((), ())), preferred_element_type=F32)


def call(body, name, outs, ins, scratch=(), flops=1e8, smem=0, space=VMEM, out_space=VMEM, specs=None):
    sizes = [math.prod(a.shape) * a.dtype.itemsize for a in outs]
    spaces = out_space if isinstance(out_space, list) else [out_space] * len(outs)
    outs = [pltpu.HBM(a.shape, a.dtype) if b is HBM else a for a, b in zip(outs, spaces)]
    return pl.pallas_call(
        body,
        out_shape=outs,
        in_specs=specs or [SMEM] * smem + [space] * (ins - smem),
        out_specs=spaces,
        scratch_shapes=list(scratch),
        compiler_params=pltpu.CompilerParams(vmem_limit_bytes=16 * 2**20),
        cost_estimate=pl.CostEstimate(
            flops=int(flops), bytes_accessed=2 * sum(sizes), transcendentals=0
        ),
        name=name,
    )


def turned(weights):
    return weights.astype(F32).T.astype(BF16)


def run(copies):
    for copy in copies:
        copy.start()
    for copy in copies:
        copy.wait()


def place():
    per_half = lax.axis_size("row") // 2
    columns = lax.axis_size("ch")
    row = lax.rem(lax.axis_index("row"), per_half)
    core = lax.rem(row, 2)
    return (row - core) * columns + lax.axis_index("ch"), core


def chip_offsets():
    columns = lax.axis_size("ch")
    share = lax.axis_size("row") // 2 * columns
    return [o for o in range(share) if o // columns % 2 == 0]


def chunked(pairs, sems, first, chunks):
    rows = pairs[0][0].shape[0]
    size = rows // chunks
    return [
        [
            pltpu.make_async_copy(
                source.at[pl.ds(chunk * size, size)],
                target.at[pl.ds(chunk * size, size)],
                sems.at[first + k, chunk],
            )
            for k, (source, target) in enumerate(pairs)
        ]
        for chunk in range(chunks)
    ]


def edges_body(length, source_hbm, proj_hbm, gate_hbm, *rest, side):
    outs = rest[:-6]
    source, proj, gate, held, out, sems = rest[-6:]
    rows, cols, channels = source.shape
    share, own = out.shape[:2]
    columns = lax.axis_size("ch")
    span = pl.ds(side * channels, channels)
    fetches = [
        pltpu.make_async_copy(proj_hbm.at[:, span], proj, sems.at[0, 2]),
        pltpu.make_async_copy(gate_hbm.at[:, span], gate, sems.at[0, 3]),
    ]
    chunks = chunked([(source_hbm, source)], sems, 0, 2)
    for copy in fetches + chunks[0] + chunks[1]:
        copy.start()
    row_offset = lax.axis_index("row") * rows
    col_offset = lax.axis_index("ch") * cols
    count = length[0]
    tokens = col_offset + lax.broadcasted_iota(jnp.int32, (1, cols), 1)
    col_valid = jnp.where(tokens < count, 0.5, 0.0)
    for copy in fetches:
        copy.wait()
    weights = jnp.concatenate([turned(proj[...]), turned(gate[...])], axis=0)

    def step(row, carry):
        values = source[row]
        if side:
            values = layer_norm(values.astype(F32), -1).astype(BF16)
            source[row] = values
        mixed = dot(weights, values, (1, 1))
        valid = col_valid * (row_offset + row < count).astype(F32)
        twice = jnp.tanh(0.5 * mixed[channels:]) + 1.0
        held[pl.ds(row, channels, stride=rows), :] = twice * (mixed[:channels] * valid)
        return carry

    for (copy,) in chunks:
        copy.wait()
    lax.fori_loop(0, rows, step, 0, unroll=rows)
    sends = []
    if side:
        sends.append(pltpu.make_async_copy(source, outs[1], sems.at[1, 0]))
        sends[0].start()
    group = share // 4
    for device in range(share):
        part = held[device * own * rows : (device + 1) * own * rows, :].astype(BF16)
        position = share - 1 - device
        out[position] = part.reshape(own, rows, cols)
        if side and device % group == group - 1:
            for k in range(2):
                source_part = out.at[pl.ds(position, group)]
                target = outs[0].at[pl.ds(k * share + position, group)]
                sends.append(
                    pltpu.make_async_copy(source_part, target, sems.at[1 + k, 1 + device // group])
                )
                sends[-1].start()
    if not side:
        chip, core = place()
        for k, offset in enumerate(chip_offsets()):
            for other in range(2):
                index = jnp.bitwise_xor(chip, offset) + lax.rem(core + other, 2) * columns
                outs[other][k] = out[index]
    for copy in sends:
        copy.wait()


def pack_body(mine, sibling, *outs):
    _, core = place()
    for k, out in enumerate(outs):
        out[core] = mine[k]
        out[1 - core] = sibling[k]


def gate_body(pair, normed, weights, bias_proj, out, source, bias_weights):
    turned_weights = turned(weights[...])
    bias_weights[...] = turned(bias_proj[...])

    def step(row, carry):
        out[row] = sigmoid(dot(turned_weights, normed[row], (1, 1))).astype(BF16)
        source[row] = pair[row].astype(F32).T.astype(BF16)
        return carry

    lax.fori_loop(0, pair.shape[0], step, 0, unroll=2)


def triangle_body(right, *rest):
    parts, held = rest[:-1], rest[-1]
    row_devices, col_devices, own, rows, cols = right.shape
    chip, _ = place()
    chip_row = lax.div(chip, col_devices)
    me = lax.axis_index("ch")
    groups = [(first, core) for first in range(0, row_devices // 2, 2) for core in range(2)]
    offsets = chip_offsets()
    for channel in range(own):
        left, whole = [], []
        for flip in range(col_devices):
            left.append(
                jnp.concatenate(
                    [
                        parts[offsets.index(first * col_devices + flip)][core, channel]
                        for first, core in groups
                    ],
                    axis=0,
                )
            )
            whole.append(right[:, jnp.bitwise_xor(me, flip), channel].reshape(-1, cols))
        triangle = dot(
            jnp.concatenate(left, axis=1), jnp.concatenate(whole, axis=1), (1, 1)
        ).astype(BF16)
        for k, (first, core) in enumerate(groups):
            for part in range(col_devices):
                row = row_devices // 2 - 1 - core - jnp.bitwise_xor(chip_row, first)
                held[row, col_devices - 1 - part, channel] = triangle[
                    k * rows : (k + 1) * rows, part * cols : (part + 1) * cols
                ]


def deal_body(*refs):
    parts, out = refs[:-1], refs[-1]
    columns = len(parts)
    per_part = lax.axis_size("row") // columns
    part = lax.div(lax.axis_index("row"), per_part)
    for col in range(columns):
        value = parts[0][...]
        for flip in range(1, columns):
            value = jnp.where(jnp.bitwise_xor(part, col) == flip, parts[flip][...], value)
        for chip in range(out.shape[0] // columns):
            out[chip * columns + col] = value


def spread_sum(values):
    lead = 8
    split = values.reshape((values.shape[0] // lead, lead) + values.shape[1:])
    return jnp.sum(jnp.sum(split, axis=0), axis=0, keepdims=True)


def update_body(triangle, source, gate, tri_out, bias_proj, updated, bias, held, bias_held):
    channels, rows, cols = triangle.shape
    heads = bias_proj.shape[0]
    values = triangle[...].astype(F32)
    centre = values - spread_sum(values) * (1.0 / channels)
    spread = spread_sum(centre * centre) * (1.0 / channels)
    held[...] = (centre * lax.rsqrt(spread + EPS)).reshape(channels * rows, cols)
    out_weights = turned(tri_out[...])
    bias_weights = bias_proj[...]

    def step(row, carry):
        tri_normed = held[pl.ds(row, channels, stride=rows), :].astype(BF16)
        update = gate[row].astype(F32) * dot(out_weights, tri_normed, (1, 0))
        mine = (source[row].astype(F32) + update).astype(BF16)
        updated[row] = mine
        normed = layer_norm(mine.astype(F32), 0).astype(BF16)
        bias_held[pl.ds(row, heads, stride=rows), :] = dot(bias_weights, normed, (1, 0))
        return carry

    lax.fori_loop(0, rows, step, 0, unroll=8)
    bias[...] = bias_held[...].astype(BF16).reshape(heads, rows, cols)


def project(updated, attn_proj, mixed, row, score_scale, late=None):
    channels = updated.shape[1]
    values = updated[row].astype(F32)
    normed = layer_norm(values, 0)
    natural = normed.T.astype(BF16)

    def put(target, block, array):
        target[row, :, block * channels : (block + 1) * channels] = array.astype(BF16)

    put(mixed, 0, dot(turned(attn_proj[:, channels : 2 * channels]), normed.astype(BF16), (1, 0)))
    put(mixed, 1, dot(natural, attn_proj[:, 2 * channels : 3 * channels], (1, 0)))
    if late is not None:
        put(mixed, 2, dot(natural, attn_proj[:, :channels], (1, 0)) * score_scale)
        put(late, 0, sigmoid(dot(natural, attn_proj[:, 3 * channels :], (1, 0))))
        put(late, 1, values.T)


def own_body(updated, attn_proj, mixed, late_hbm, late, sems, *, score_scale):
    rows = updated.shape[0]

    def step(row, carry):
        project(updated, attn_proj, mixed, row, score_scale, late)
        return carry

    sends = chunked([(late, late_hbm)], sems, 0, 2)
    for chunk in range(2):
        lax.fori_loop(chunk * rows // 2, (chunk + 1) * rows // 2, step, 0, unroll=rows // 2)
        sends[chunk][0].start()
    for (copy,) in sends:
        copy.wait()


def other_body(late_hbm, attn_proj, *rest):
    pieces = (len(rest) - 2) // 2
    others, late, keys, sem = rest[:pieces], rest[pieces], rest[pieces + 1 : -1], rest[-1]
    fetch = pltpu.make_async_copy(late_hbm, late, sem)
    fetch.start()
    rows = late.shape[0]
    for updated, target in zip(others, keys):

        def step(row, carry):
            project(updated, attn_proj, target, row, None)
            return carry

        lax.fori_loop(0, rows, step, 0, unroll=rows // 2)
    fetch.wait()


def attend_body(length, mine, sibling, attn_out, late, *rest):
    mixed, (out_hbm, out, bias_held, sems) = rest[:-4], rest[-4:]
    pieces = len(mixed)
    rows, cols, channels = out.shape
    heads = mine.shape[1]
    me = lax.axis_index("ch")
    its_core = lax.rem(lax.axis_index("row"), 2)
    head_of = lax.broadcasted_iota(jnp.int32, (1, channels), 1) // (channels // heads)
    count = sems.shape[1]
    sends = chunked([(out, out_hbm)], sems, 0, count)
    chips = cols // rows // 2
    for piece in range(pieces):
        block = lax.rem(me + piece, pieces)
        token = block * cols + lax.broadcasted_iota(jnp.int32, (1, cols), 1)
        key_term = jnp.where(token < length[0], 0.0, -1e9)
        for part, core in ((mine, its_core), (sibling, 1 - its_core)):
            for chip in range(chips):
                tiles = part[chip * pieces + block]
                for head in range(heads):
                    first = pl.multiple_of(head * cols + (chip * 2 + core) * rows, rows)
                    bias_held[pl.ds(first, rows), piece * cols : (piece + 1) * cols] = (
                        tiles[head].astype(F32) + key_term
                    )
    both_of = jnp.concatenate([head_of, head_of], axis=1)
    masks = [(head_of == head).astype(BF16) for head in range(heads)]
    ones = jnp.ones((pieces * cols, channels), BF16)

    def load(row):
        keys = jnp.concatenate([part[row, :, :channels] for part in mixed], axis=1)
        values = jnp.concatenate([part[row, :, channels : 2 * channels] for part in mixed], axis=0)
        values = jnp.concatenate([values, ones], axis=1)
        return keys, values, mixed[0][row, :, 2 * channels :]

    def finish(row, total):
        attended = total[:, :channels] / total[:, channels:]
        gate = late[row, :, :channels].astype(F32)
        gated = (attended * gate).astype(BF16)
        residual = late[row, :, channels:].astype(F32)
        out[row] = (residual + dot(gated, attn_out[...], (1, 0))).astype(BF16)

    per_chunk = rows // count
    loaded, logits, weights = {}, {}, {}
    for time in range(rows + 2):
        row = time
        if row < rows:
            loaded[row] = load(row)
            keys, _, query = loaded[row]
            queries = jnp.concatenate([query * mask for mask in masks], axis=0)
            logits[row] = dot(queries, keys, (1, 0)) + bias_held[...]
        row = time - 1
        if 0 <= row < rows:
            scores = logits.pop(row)
            top = jnp.max(scores, axis=-1, keepdims=True)
            weights[row] = jnp.exp((scores - top).astype(BF16))
        row = time - 2
        if row >= 0:
            sums = dot(weights.pop(row), loaded.pop(row)[1], (1, 0))
            total = sums[:cols]
            for head in range(1, heads):
                total = jnp.where(both_of == head, sums[head * cols : (head + 1) * cols], total)
            finish(row, total)
            chunk, place_in = divmod(row, per_chunk)
            if place_in == per_chunk - 1:
                for copy in sends[chunk]:
                    copy.start()
    for send in sends:
        for copy in send:
            copy.wait()


def local(
    pair_act, valid_count, edge_proj, edge_gate, tri_gate, tri_out, attn_proj, bias_proj, attn_out
):
    rows, cols, channels = pair_act.shape
    heads = bias_proj.shape[1]
    row_devices = lax.axis_size("row")
    col_devices = lax.axis_size("ch")
    devices = row_devices * col_devices
    share = devices // 2
    own = channels // share
    everyone = list(reversed(range(devices)))
    halves = [everyone[share:], everyone[:share]]
    shape = jax.ShapeDtypeStruct
    block = (rows, cols, channels)
    turned_block = (rows, channels, cols)

    def in_half(array):
        return lax.all_to_all(
            array, BOTH, split_axis=0, concat_axis=0, axis_index_groups=halves, tiled=True
        )


    weight = pltpu.VMEM((channels, channels), BF16)
    offsets = chip_offsets()
    tile = (own, rows, cols)

    def edges(side, source):
        outs = [shape((devices,) + tile, BF16), shape(block, BF16)]
        return call(
            functools.partial(edges_body, side=side),
            "right_edges" if side else "left_edges",
            outs if side else [shape((len(offsets),) + tile, BF16)] * 2,
            4,
            [
                pltpu.VMEM(block, BF16),
                weight,
                weight,
                pltpu.VMEM((channels * rows, cols), F32),
                pltpu.VMEM((share,) + tile, BF16),
                pltpu.SemaphoreType.DMA((3, 5)),
            ],
            smem=1,
            space=HBM,
            out_space=HBM if side else VMEM,
            flops=3e9,
        )(valid_count, *[in_hbm(a) for a in (source, edge_proj, edge_gate)])

    def flipped(array, bits):
        return lax.ppermute(array, BOTH, [(d, d ^ bits) for d in range(devices)])

    right, normed = edges(1, pair_act)
    right = lax.all_to_all(right, BOTH, split_axis=0, concat_axis=0, tiled=True)
    mine, theirs = edges(0, normed)
    left = call(pack_body, "pack", [shape((2,) + tile, BF16)] * len(offsets), 2)(
        mine, flipped(theirs, col_devices)
    )
    left = [flipped(part, offset) if offset else part for part, offset in zip(left, offsets)]
    tri_gating, source, bias_weights = call(
        gate_body,
        "tri_gate",
        [shape(turned_block, BF16)] * 2 + [shape((heads, channels), BF16)],
        4,
        flops=2e9,
    )(pair_act, normed, tri_gate, bias_proj)
    tri_gating, source, bias_weights, *left = lax.optimization_barrier(
        (tri_gating, source, bias_weights, *left)
    )
    triangle_shape = (row_devices // 2, col_devices, own, rows, cols)
    (triangle,) = call(
        triangle_body,
        "triangle",
        [shape(triangle_shape, BF16)],
        1 + len(left),
        flops=2e9,
    )(right.reshape((row_devices,) + triangle_shape[1:]), *left)
    triangle = in_half(triangle.reshape(share, own, rows, cols))
    bias_shape = (heads, rows, cols)
    updated, bias = call(
        update_body,
        "update",
        [shape(turned_block, BF16), shape(bias_shape, BF16)],
        5,
        [pltpu.VMEM((channels * rows, cols), F32), pltpu.VMEM((heads * rows, cols), F32)],
        flops=2e9,
    )(triangle.reshape(channels, rows, cols), source, tri_gating, tri_out, bias_weights)
    per_part = row_devices // col_devices
    parts = [bias] + [
        flipped(bias, flip * per_part * col_devices) for flip in range(1, col_devices)
    ]
    (dealt,) = call(
        deal_body, "deal_bias", [shape((per_part // 2 * col_devices,) + bias_shape, BF16)], col_devices
    )(*parts)
    one_core = []
    for part in range(col_devices):
        for core in range(2):
            members = range(part * per_part + core, (part + 1) * per_part, 2)
            one_core.append([r * col_devices + c for r in members for c in range(col_devices)])

    others = [
        lax.ppermute(updated, "ch", [((c + s) % col_devices, c) for c in range(col_devices)])
        for s in range(1, col_devices)
    ]
    bias = lax.all_to_all(
        dealt, BOTH, split_axis=0, concat_axis=0, axis_index_groups=one_core, tiled=True
    )

    mixed_shape = (rows, cols, 3 * channels)
    key_shape = (rows, cols, 2 * channels)
    mixed, late = call(
        functools.partial(own_body, score_scale=(channels // heads) ** (-0.5)),
        "own_projections",
        [shape(mixed_shape, BF16), shape(key_shape, BF16)],
        2,
        [pltpu.VMEM(key_shape, BF16), pltpu.SemaphoreType.DMA((1, 2))],
        out_space=[VMEM, HBM],
        flops=3e9,
    )(updated, attn_proj)
    bias, *others = lax.optimization_barrier((bias, *others))
    late, *keys = call(
        other_body,
        "other_keys",
        [shape(key_shape, BF16)] * (1 + len(others)),
        2 + len(others),
        [pltpu.SemaphoreType.DMA(())],
        specs=[HBM] + [VMEM] * (1 + len(others)),
        flops=3e9,
    )(in_hbm(late), attn_proj, *others)
    (result,) = call(
        attend_body,
        "attend",
        [shape(block, BF16)],
        5 + col_devices,
        [
            pltpu.VMEM(block, BF16),
            pltpu.VMEM((heads * cols, col_devices * cols), F32),
            pltpu.SemaphoreType.DMA((1, rows // 2)),
        ],
        smem=1,
        out_space=HBM,
    )(valid_count, bias, flipped(bias, col_devices), attn_out, late, mixed, *keys)
    return result


def solution(mesh):
    placed = (P("row", "ch", None), P(), P(), P(), P(), P(), P(), P(), P())
    return jax.shard_map(
        local, mesh=mesh, in_specs=placed, out_specs=P("row", "ch", None), check_vma=False
    )
```

```python
import functools
import math

import jax
import jax.numpy as jnp
from jax import lax
from jax.experimental import pallas as pl
from jax.experimental.pallas import tpu as pltpu
from jax.sharding import PartitionSpec as P

EPS = 1e-05
BOTH = ("row", "ch")
F32 = jnp.float32
BF16 = jnp.bfloat16
VMEM = pl.BlockSpec(memory_space=pltpu.VMEM)
SMEM = pl.BlockSpec(memory_space=pltpu.SMEM)
HBM = pl.BlockSpec(memory_space=pltpu.HBM)
ANY = pl.BlockSpec(memory_space=pl.ANY)


def layer_norm(values, axis):
    centre = values - jnp.mean(values, axis=axis, keepdims=True)
    spread = jnp.mean(centre * centre, axis=axis, keepdims=True)
    return centre * lax.rsqrt(spread + EPS)


def in_hbm(array):
    return pltpu.with_memory_space_constraint(array, pltpu.HBM)


def sigmoid(values):
    return 0.5 * jnp.tanh(0.5 * values) + 0.5


def dot(a, b, dims):
    return lax.dot_general(a, b, ((dims[:1], dims[1:]), ((), ())), preferred_element_type=F32)


def call(body, name, outs, ins, scratch=(), flops=1e8, smem=0, space=VMEM, out_space=VMEM, specs=None):
    sizes = [math.prod(a.shape) * a.dtype.itemsize for a in outs]
    spaces = out_space if isinstance(out_space, list) else [out_space] * len(outs)
    outs = [pltpu.HBM(a.shape, a.dtype) if b is HBM else a for a, b in zip(outs, spaces)]
    return pl.pallas_call(
        body,
        out_shape=outs,
        in_specs=specs or [SMEM] * smem + [space] * (ins - smem),
        out_specs=spaces,
        scratch_shapes=list(scratch),
        compiler_params=pltpu.CompilerParams(vmem_limit_bytes=16 * 2**20),
        cost_estimate=pl.CostEstimate(
            flops=int(flops), bytes_accessed=2 * sum(sizes), transcendentals=0
        ),
        name=name,
    )


def turned(weights):
    return weights.astype(F32).T.astype(BF16)


def run(copies):
    for copy in copies:
        copy.start()
    for copy in copies:
        copy.wait()


def place():
    per_half = lax.axis_size("row") // 2
    columns = lax.axis_size("ch")
    row = lax.rem(lax.axis_index("row"), per_half)
    core = lax.rem(row, 2)
    return (row - core) * columns + lax.axis_index("ch"), core


def chip_offsets():
    columns = lax.axis_size("ch")
    share = lax.axis_size("row") // 2 * columns
    return [o for o in range(share) if o // columns % 2 == 0]


def chunked(pairs, sems, first, chunks):
    rows = pairs[0][0].shape[0]
    size = rows // chunks
    return [
        [
            pltpu.make_async_copy(
                source.at[pl.ds(chunk * size, size)],
                target.at[pl.ds(chunk * size, size)],
                sems.at[first + k, chunk],
            )
            for k, (source, target) in enumerate(pairs)
        ]
        for chunk in range(chunks)
    ]


def edges_body(length, source_hbm, proj_hbm, gate_hbm, *rest, side):
    outs = rest[:-6]
    source, proj, gate, held, out, sems = rest[-6:]
    rows, cols, channels = source.shape
    share, own = out.shape[:2]
    columns = lax.axis_size("ch")
    span = pl.ds(side * channels, channels)
    fetches = [
        pltpu.make_async_copy(proj_hbm.at[:, span], proj, sems.at[0, 2]),
        pltpu.make_async_copy(gate_hbm.at[:, span], gate, sems.at[0, 3]),
    ]
    chunks = chunked([(source_hbm, source)], sems, 0, 2)
    for copy in fetches + chunks[0] + chunks[1]:
        copy.start()
    row_offset = lax.axis_index("row") * rows
    col_offset = lax.axis_index("ch") * cols
    count = length[0]
    tokens = col_offset + lax.broadcasted_iota(jnp.int32, (1, cols), 1)
    col_valid = jnp.where(tokens < count, 0.5, 0.0)
    for copy in fetches:
        copy.wait()
    weights = jnp.concatenate([turned(proj[...]), turned(gate[...])], axis=0)

    def step(row, carry):
        values = source[row]
        if side:
            values = layer_norm(values.astype(F32), -1).astype(BF16)
            source[row] = values
        mixed = dot(weights, values, (1, 1))
        valid = col_valid * (row_offset + row < count).astype(F32)
        twice = jnp.tanh(0.5 * mixed[channels:]) + 1.0
        held[pl.ds(row, channels, stride=rows), :] = twice * (mixed[:channels] * valid)
        return carry

    for (copy,) in chunks:
        copy.wait()
    lax.fori_loop(0, rows, step, 0, unroll=rows)
    sends = []
    if side:
        sends.append(pltpu.make_async_copy(source, outs[1], sems.at[1, 0]))
        sends[0].start()
    group = share // 4
    for device in range(share):
        part = held[device * own * rows : (device + 1) * own * rows, :].astype(BF16)
        position = share - 1 - device
        out[position] = part.reshape(own, rows, cols)
        if side and device % group == group - 1:
            for k in range(2):
                source_part = out.at[pl.ds(position, group)]
                target = outs[0].at[pl.ds(k * share + position, group)]
                sends.append(
                    pltpu.make_async_copy(source_part, target, sems.at[1 + k, 1 + device // group])
                )
                sends[-1].start()
    if not side:
        chip, core = place()
        for k, offset in enumerate(chip_offsets()):
            for other in range(2):
                index = jnp.bitwise_xor(chip, offset) + lax.rem(core + other, 2) * columns
                outs[other][k] = out[index]
    for copy in sends:
        copy.wait()


def pack_body(mine, sibling, *outs):
    _, core = place()
    for k, out in enumerate(outs):
        out[core] = mine[k]
        out[1 - core] = sibling[k]


def gate_body(pair, normed, weights, bias_proj, out, source, bias_weights):
    turned_weights = turned(weights[...])
    bias_weights[...] = turned(bias_proj[...])

    def step(row, carry):
        out[row] = sigmoid(dot(turned_weights, normed[row], (1, 1))).astype(BF16)
        source[row] = pair[row].astype(F32).T.astype(BF16)
        return carry

    lax.fori_loop(0, pair.shape[0], step, 0, unroll=2)


def triangle_body(right, *rest):
    parts, held = rest[:-1], rest[-1]
    row_devices, col_devices, own, rows, cols = right.shape
    chip, _ = place()
    chip_row = lax.div(chip, col_devices)
    me = lax.axis_index("ch")
    groups = [(first, core) for first in range(0, row_devices // 2, 2) for core in range(2)]
    offsets = chip_offsets()
    for channel in range(own):
        left, whole = [], []
        for flip in range(col_devices):
            left.append(
                jnp.concatenate(
                    [
                        parts[offsets.index(first * col_devices + flip)][core, channel]
                        for first, core in groups
                    ],
                    axis=0,
                )
            )
            whole.append(right[:, jnp.bitwise_xor(me, flip), channel].reshape(-1, cols))
        triangle = dot(
            jnp.concatenate(left, axis=1), jnp.concatenate(whole, axis=1), (1, 1)
        ).astype(BF16)
        for k, (first, core) in enumerate(groups):
            for part in range(col_devices):
                row = row_devices // 2 - 1 - core - jnp.bitwise_xor(chip_row, first)
                held[row, col_devices - 1 - part, channel] = triangle[
                    k * rows : (k + 1) * rows, part * cols : (part + 1) * cols
                ]


def deal_body(*refs):
    parts, out = refs[:-1], refs[-1]
    columns = len(parts)
    per_part = lax.axis_size("row") // columns
    part = lax.div(lax.axis_index("row"), per_part)
    for col in range(columns):
        value = parts[0][...]
        for flip in range(1, columns):
            value = jnp.where(jnp.bitwise_xor(part, col) == flip, parts[flip][...], value)
        for chip in range(out.shape[0] // columns):
            out[chip * columns + col] = value


def spread_sum(values):
    lead = 8
    split = values.reshape((values.shape[0] // lead, lead) + values.shape[1:])
    return jnp.sum(jnp.sum(split, axis=0), axis=0, keepdims=True)


def update_body(triangle, source, gate, tri_out, bias_proj, updated, bias, held, bias_held):
    channels, rows, cols = triangle.shape
    heads = bias_proj.shape[0]
    values = triangle[...].astype(F32)
    centre = values - spread_sum(values) * (1.0 / channels)
    spread = spread_sum(centre * centre) * (1.0 / channels)
    held[...] = (centre * lax.rsqrt(spread + EPS)).reshape(channels * rows, cols)
    out_weights = turned(tri_out[...])
    bias_weights = bias_proj[...]

    def step(row, carry):
        tri_normed = held[pl.ds(row, channels, stride=rows), :].astype(BF16)
        update = gate[row].astype(F32) * dot(out_weights, tri_normed, (1, 0))
        mine = (source[row].astype(F32) + update).astype(BF16)
        updated[row] = mine
        normed = layer_norm(mine.astype(F32), 0).astype(BF16)
        bias_held[pl.ds(row, heads, stride=rows), :] = dot(bias_weights, normed, (1, 0))
        return carry

    lax.fori_loop(0, rows, step, 0, unroll=8)
    bias[...] = bias_held[...].astype(BF16).reshape(heads, rows, cols)


def project(updated, attn_proj, mixed, row, score_scale, late=None):
    channels = updated.shape[1]
    values = updated[row].astype(F32)
    normed = layer_norm(values, 0)
    natural = normed.T.astype(BF16)

    def put(target, block, array):
        target[row, :, block * channels : (block + 1) * channels] = array.astype(BF16)

    put(mixed, 0, dot(turned(attn_proj[:, channels : 2 * channels]), normed.astype(BF16), (1, 0)))
    put(mixed, 1, dot(natural, attn_proj[:, 2 * channels : 3 * channels], (1, 0)))
    if late is not None:
        put(mixed, 2, dot(natural, attn_proj[:, :channels], (1, 0)) * score_scale)
        put(late, 0, sigmoid(dot(natural, attn_proj[:, 3 * channels :], (1, 0))))
        put(late, 1, values.T)


def own_body(updated, attn_proj, mixed, late, *, score_scale):
    def step(row, carry):
        project(updated, attn_proj, mixed, row, score_scale, late)
        return carry

    lax.fori_loop(0, updated.shape[0], step, 0, unroll=8)


def other_body(attn_proj, *rest):
    pieces = len(rest) // 2
    for updated, target in zip(rest[:pieces], rest[pieces:]):

        def step(row, carry):
            project(updated, attn_proj, target, row, None)
            return carry

        lax.fori_loop(0, updated.shape[0], step, 0, unroll=8)


def attend_body(length, mine, sibling, attn_out, late, *rest):
    mixed, (out_hbm, out, bias_held, sems) = rest[:-4], rest[-4:]
    pieces = len(mixed)
    rows, cols, channels = out.shape
    heads = mine.shape[1]
    me = lax.axis_index("ch")
    its_core = lax.rem(lax.axis_index("row"), 2)
    head_of = lax.broadcasted_iota(jnp.int32, (1, channels), 1) // (channels // heads)
    count = sems.shape[1]
    sends = chunked([(out, out_hbm)], sems, 0, count)
    chips = cols // rows // 2
    for piece in range(pieces):
        block = lax.rem(me + piece, pieces)
        token = block * cols + lax.broadcasted_iota(jnp.int32, (1, cols), 1)
        key_term = jnp.where(token < length[0], 0.0, -1e9)
        for part, core in ((mine, its_core), (sibling, 1 - its_core)):
            for chip in range(chips):
                tiles = part[chip * pieces + block]
                for head in range(heads):
                    first = pl.multiple_of(head * cols + (chip * 2 + core) * rows, rows)
                    bias_held[pl.ds(first, rows), piece * cols : (piece + 1) * cols] = (
                        tiles[head].astype(F32) + key_term
                    )
    both_of = jnp.concatenate([head_of, head_of], axis=1)
    masks = [(head_of == head).astype(BF16) for head in range(heads)]
    ones = jnp.ones((pieces * cols, channels), BF16)

    def load(row):
        keys = jnp.concatenate([part[row, :, :channels] for part in mixed], axis=1)
        values = jnp.concatenate([part[row, :, channels : 2 * channels] for part in mixed], axis=0)
        values = jnp.concatenate([values, ones], axis=1)
        return keys, values, mixed[0][row, :, 2 * channels :]

    def finish(row, total):
        attended = total[:, :channels] / total[:, channels:]
        gate = late[row, :, :channels].astype(F32)
        gated = (attended * gate).astype(BF16)
        residual = late[row, :, channels:].astype(F32)
        out[row] = (residual + dot(gated, attn_out[...], (1, 0))).astype(BF16)

    per_chunk = rows // count
    loaded, logits, weights = {}, {}, {}
    for time in range(rows + 2):
        row = time
        if row < rows:
            loaded[row] = load(row)
            keys, _, query = loaded[row]
            queries = jnp.concatenate([query * mask for mask in masks], axis=0)
            logits[row] = dot(queries, keys, (1, 0)) + bias_held[...]
        row = time - 1
        if 0 <= row < rows:
            scores = logits.pop(row)
            top = jnp.max(scores, axis=-1, keepdims=True)
            weights[row] = jnp.exp((scores - top).astype(BF16))
        row = time - 2
        if row >= 0:
            sums = dot(weights.pop(row), loaded.pop(row)[1], (1, 0))
            total = sums[:cols]
            for head in range(1, heads):
                total = jnp.where(both_of == head, sums[head * cols : (head + 1) * cols], total)
            finish(row, total)
            chunk, place_in = divmod(row, per_chunk)
            if place_in == per_chunk - 1:
                for copy in sends[chunk]:
                    copy.start()
    for send in sends:
        for copy in send:
            copy.wait()


def local(
    pair_act, valid_count, edge_proj, edge_gate, tri_gate, tri_out, attn_proj, bias_proj, attn_out
):
    rows, cols, channels = pair_act.shape
    heads = bias_proj.shape[1]
    row_devices = lax.axis_size("row")
    col_devices = lax.axis_size("ch")
    devices = row_devices * col_devices
    share = devices // 2
    own = channels // share
    everyone = list(reversed(range(devices)))
    halves = [everyone[share:], everyone[:share]]
    shape = jax.ShapeDtypeStruct
    block = (rows, cols, channels)
    turned_block = (rows, channels, cols)

    def in_half(array):
        return lax.all_to_all(
            array, BOTH, split_axis=0, concat_axis=0, axis_index_groups=halves, tiled=True
        )


    weight = pltpu.VMEM((channels, channels), BF16)
    offsets = chip_offsets()
    tile = (own, rows, cols)

    def edges(side, source):
        outs = [shape((devices,) + tile, BF16), shape(block, BF16)]
        return call(
            functools.partial(edges_body, side=side),
            "right_edges" if side else "left_edges",
            outs if side else [shape((len(offsets),) + tile, BF16)] * 2,
            4,
            [
                pltpu.VMEM(block, BF16),
                weight,
                weight,
                pltpu.VMEM((channels * rows, cols), F32),
                pltpu.VMEM((share,) + tile, BF16),
                pltpu.SemaphoreType.DMA((3, 5)),
            ],
            smem=1,
            space=HBM,
            out_space=HBM if side else VMEM,
            flops=3e9,
        )(valid_count, *[in_hbm(a) for a in (source, edge_proj, edge_gate)])

    def flipped(array, bits):
        return lax.ppermute(array, BOTH, [(d, d ^ bits) for d in range(devices)])

    right, normed = edges(1, pair_act)
    right = lax.all_to_all(right, BOTH, split_axis=0, concat_axis=0, tiled=True)
    mine, theirs = edges(0, normed)
    left = call(pack_body, "pack", [shape((2,) + tile, BF16)] * len(offsets), 2)(
        mine, flipped(theirs, col_devices)
    )
    left = [flipped(part, offset) if offset else part for part, offset in zip(left, offsets)]
    tri_gating, source, bias_weights = call(
        gate_body,
        "tri_gate",
        [shape(turned_block, BF16)] * 2 + [shape((heads, channels), BF16)],
        4,
        flops=2e9,
    )(pair_act, normed, tri_gate, bias_proj)
    tri_gating, source, bias_weights, *left = lax.optimization_barrier(
        (tri_gating, source, bias_weights, *left)
    )
    triangle_shape = (row_devices // 2, col_devices, own, rows, cols)
    (triangle,) = call(
        triangle_body,
        "triangle",
        [shape(triangle_shape, BF16)],
        1 + len(left),
        flops=2e9,
    )(right.reshape((row_devices,) + triangle_shape[1:]), *left)
    triangle = in_half(triangle.reshape(share, own, rows, cols))
    bias_shape = (heads, rows, cols)
    updated, bias = call(
        update_body,
        "update",
        [shape(turned_block, BF16), shape(bias_shape, BF16)],
        5,
        [pltpu.VMEM((channels * rows, cols), F32), pltpu.VMEM((heads * rows, cols), F32)],
        flops=2e9,
    )(triangle.reshape(channels, rows, cols), source, tri_gating, tri_out, bias_weights)
    per_part = row_devices // col_devices
    parts = [bias] + [
        flipped(bias, flip * per_part * col_devices) for flip in range(1, col_devices)
    ]
    (dealt,) = call(
        deal_body, "deal_bias", [shape((per_part // 2 * col_devices,) + bias_shape, BF16)], col_devices
    )(*parts)
    one_core = []
    for part in range(col_devices):
        for core in range(2):
            members = range(part * per_part + core, (part + 1) * per_part, 2)
            one_core.append([r * col_devices + c for r in members for c in range(col_devices)])

    others = [
        lax.ppermute(updated, "ch", [((c + s) % col_devices, c) for c in range(col_devices)])
        for s in range(1, col_devices)
    ]
    mixed_shape = (rows, cols, 3 * channels)
    key_shape = (rows, cols, 2 * channels)
    mixed, late = call(
        functools.partial(own_body, score_scale=(channels // heads) ** (-0.5)),
        "own_projections",
        [shape(mixed_shape, BF16), shape(key_shape, BF16)],
        2,
        flops=2e9,
    )(updated, attn_proj)
    dealt, mixed, late = lax.optimization_barrier((dealt, mixed, late))
    bias = lax.all_to_all(
        dealt, BOTH, split_axis=0, concat_axis=0, axis_index_groups=one_core, tiled=True
    )
    bias, *others = lax.optimization_barrier((bias, *others))
    keys = call(
        other_body,
        "other_keys",
        [shape(key_shape, BF16)] * len(others),
        1 + len(others),
        flops=3e9,
    )(attn_proj, *others)
    (result,) = call(
        attend_body,
        "attend",
        [shape(block, BF16)],
        5 + col_devices,
        [
            pltpu.VMEM(block, BF16),
            pltpu.VMEM((heads * cols, col_devices * cols), F32),
            pltpu.SemaphoreType.DMA((1, rows // 2)),
        ],
        smem=1,
        out_space=HBM,
    )(valid_count, bias, flipped(bias, col_devices), attn_out, late, mixed, *keys)
    return result


def solution(mesh):
    placed = (P("row", "ch", None), P(), P(), P(), P(), P(), P(), P(), P())
    return jax.shard_map(
        local, mesh=mesh, in_specs=placed, out_specs=P("row", "ch", None), check_vma=False
    )
```

```python
import functools
import math

import jax
import jax.numpy as jnp
from jax import lax
from jax.experimental import pallas as pl
from jax.experimental.pallas import tpu as pltpu
from jax.sharding import PartitionSpec as P

EPS = 1e-05
BOTH = ("row", "ch")
F32 = jnp.float32
BF16 = jnp.bfloat16
VMEM = pl.BlockSpec(memory_space=pltpu.VMEM)
SMEM = pl.BlockSpec(memory_space=pltpu.SMEM)
HBM = pl.BlockSpec(memory_space=pltpu.HBM)
ANY = pl.BlockSpec(memory_space=pl.ANY)


def layer_norm(values, axis):
    centre = values - jnp.mean(values, axis=axis, keepdims=True)
    spread = jnp.mean(centre * centre, axis=axis, keepdims=True)
    return centre * lax.rsqrt(spread + EPS)


def in_hbm(array):
    return pltpu.with_memory_space_constraint(array, pltpu.HBM)


def sigmoid(values):
    return 0.5 * jnp.tanh(0.5 * values) + 0.5


def dot(a, b, dims):
    return lax.dot_general(a, b, ((dims[:1], dims[1:]), ((), ())), preferred_element_type=F32)


def call(body, name, outs, ins, scratch=(), flops=1e8, smem=0, space=VMEM, out_space=VMEM, specs=None):
    sizes = [math.prod(a.shape) * a.dtype.itemsize for a in outs]
    spaces = out_space if isinstance(out_space, list) else [out_space] * len(outs)
    outs = [pltpu.HBM(a.shape, a.dtype) if b is HBM else a for a, b in zip(outs, spaces)]
    return pl.pallas_call(
        body,
        out_shape=outs,
        in_specs=specs or [SMEM] * smem + [space] * (ins - smem),
        out_specs=spaces,
        scratch_shapes=list(scratch),
        compiler_params=pltpu.CompilerParams(vmem_limit_bytes=16 * 2**20),
        cost_estimate=pl.CostEstimate(
            flops=int(flops), bytes_accessed=2 * sum(sizes), transcendentals=0
        ),
        name=name,
    )


def turned(weights):
    return weights.astype(F32).T.astype(BF16)


def run(copies):
    for copy in copies:
        copy.start()
    for copy in copies:
        copy.wait()


def place():
    per_half = lax.axis_size("row") // 2
    columns = lax.axis_size("ch")
    row = lax.rem(lax.axis_index("row"), per_half)
    core = lax.rem(row, 2)
    return (row - core) * columns + lax.axis_index("ch"), core


def chip_offsets():
    columns = lax.axis_size("ch")
    share = lax.axis_size("row") // 2 * columns
    return [o for o in range(share) if o // columns % 2 == 0]


def chunked(pairs, sems, first, chunks):
    rows = pairs[0][0].shape[0]
    size = rows // chunks
    return [
        [
            pltpu.make_async_copy(
                source.at[pl.ds(chunk * size, size)],
                target.at[pl.ds(chunk * size, size)],
                sems.at[first + k, chunk],
            )
            for k, (source, target) in enumerate(pairs)
        ]
        for chunk in range(chunks)
    ]


def edges_body(length, source_hbm, proj_hbm, gate_hbm, *rest, side):
    outs = rest[:-6]
    source, proj, gate, held, out, sems = rest[-6:]
    rows, cols, channels = source.shape
    share, own = out.shape[:2]
    columns = lax.axis_size("ch")
    span = pl.ds(side * channels, channels)
    fetches = [
        pltpu.make_async_copy(proj_hbm.at[:, span], proj, sems.at[0, 2]),
        pltpu.make_async_copy(gate_hbm.at[:, span], gate, sems.at[0, 3]),
    ]
    chunks = chunked([(source_hbm, source)], sems, 0, 2)
    for copy in fetches + chunks[0] + chunks[1]:
        copy.start()
    row_offset = lax.axis_index("row") * rows
    col_offset = lax.axis_index("ch") * cols
    count = length[0]
    tokens = col_offset + lax.broadcasted_iota(jnp.int32, (1, cols), 1)
    col_valid = jnp.where(tokens < count, 0.5, 0.0)
    for copy in fetches:
        copy.wait()
    weights = jnp.concatenate([turned(proj[...]), turned(gate[...])], axis=0)

    def step(row, carry):
        values = source[row]
        if side:
            values = layer_norm(values.astype(F32), -1).astype(BF16)
            source[row] = values
        mixed = dot(weights, values, (1, 1))
        valid = col_valid * (row_offset + row < count).astype(F32)
        twice = jnp.tanh(0.5 * mixed[channels:]) + 1.0
        held[pl.ds(row, channels, stride=rows), :] = twice * (mixed[:channels] * valid)
        return carry

    for (copy,) in chunks:
        copy.wait()
    lax.fori_loop(0, rows, step, 0, unroll=rows)
    sends = []
    if side:
        sends.append(pltpu.make_async_copy(source, outs[1], sems.at[1, 0]))
        sends[0].start()
    group = share // 4
    for device in range(share):
        part = held[device * own * rows : (device + 1) * own * rows, :].astype(BF16)
        position = share - 1 - device
        out[position] = part.reshape(own, rows, cols)
        if side and device % group == group - 1:
            for k in range(2):
                source_part = out.at[pl.ds(position, group)]
                target = outs[0].at[pl.ds(k * share + position, group)]
                sends.append(
                    pltpu.make_async_copy(source_part, target, sems.at[1 + k, 1 + device // group])
                )
                sends[-1].start()
    if not side:
        chip, core = place()
        for k, offset in enumerate(chip_offsets()):
            for other in range(2):
                index = jnp.bitwise_xor(chip, offset) + lax.rem(core + other, 2) * columns
                outs[other][k] = out[index]
    for copy in sends:
        copy.wait()


def pack_body(mine, sibling, *outs):
    _, core = place()
    for k, out in enumerate(outs):
        out[core] = mine[k]
        out[1 - core] = sibling[k]


def gate_body(pair, normed, weights, bias_proj, out, source, bias_weights):
    turned_weights = turned(weights[...])
    bias_weights[...] = turned(bias_proj[...])

    def step(row, carry):
        out[row] = sigmoid(dot(turned_weights, normed[row], (1, 1))).astype(BF16)
        source[row] = pair[row].astype(F32).T.astype(BF16)
        return carry

    lax.fori_loop(0, pair.shape[0], step, 0, unroll=2)


def triangle_body(right, *rest):
    parts, held = rest[:-1], rest[-1]
    row_devices, col_devices, own, rows, cols = right.shape
    chip, _ = place()
    chip_row = lax.div(chip, col_devices)
    me = lax.axis_index("ch")
    groups = [(first, core) for first in range(0, row_devices // 2, 2) for core in range(2)]
    offsets = chip_offsets()
    for channel in range(own):
        left, whole = [], []
        for flip in range(col_devices):
            left.append(
                jnp.concatenate(
                    [
                        parts[offsets.index(first * col_devices + flip)][core, channel]
                        for first, core in groups
                    ],
                    axis=0,
                )
            )
            whole.append(right[:, jnp.bitwise_xor(me, flip), channel].reshape(-1, cols))
        triangle = dot(
            jnp.concatenate(left, axis=1), jnp.concatenate(whole, axis=1), (1, 1)
        ).astype(BF16)
        for k, (first, core) in enumerate(groups):
            for part in range(col_devices):
                row = row_devices // 2 - 1 - core - jnp.bitwise_xor(chip_row, first)
                held[row, col_devices - 1 - part, channel] = triangle[
                    k * rows : (k + 1) * rows, part * cols : (part + 1) * cols
                ]


def deal_body(*refs):
    parts, out = refs[:-1], refs[-1]
    columns = len(parts)
    per_part = lax.axis_size("row") // columns
    part = lax.div(lax.axis_index("row"), per_part)
    for col in range(columns):
        value = parts[0][...]
        for flip in range(1, columns):
            value = jnp.where(jnp.bitwise_xor(part, col) == flip, parts[flip][...], value)
        for chip in range(out.shape[0] // columns):
            out[chip * columns + col] = value


def spread_sum(values):
    lead = 8
    split = values.reshape((values.shape[0] // lead, lead) + values.shape[1:])
    return jnp.sum(jnp.sum(split, axis=0), axis=0, keepdims=True)


def update_body(triangle, source, gate, tri_out, bias_proj, updated, bias, held, bias_held):
    channels, rows, cols = triangle.shape
    heads = bias_proj.shape[0]
    values = triangle[...].astype(F32)
    centre = values - spread_sum(values) * (1.0 / channels)
    spread = spread_sum(centre * centre) * (1.0 / channels)
    held[...] = (centre * lax.rsqrt(spread + EPS)).reshape(channels * rows, cols)
    out_weights = turned(tri_out[...])
    bias_weights = bias_proj[...]

    def step(row, carry):
        tri_normed = held[pl.ds(row, channels, stride=rows), :].astype(BF16)
        update = gate[row].astype(F32) * dot(out_weights, tri_normed, (1, 0))
        mine = (source[row].astype(F32) + update).astype(BF16)
        updated[row] = mine
        normed = layer_norm(mine.astype(F32), 0).astype(BF16)
        bias_held[pl.ds(row, heads, stride=rows), :] = dot(bias_weights, normed, (1, 0))
        return carry

    lax.fori_loop(0, rows, step, 0, unroll=rows)
    bias[...] = bias_held[...].astype(BF16).reshape(heads, rows, cols)


def project(updated, attn_proj, mixed, row, score_scale, late=None):
    channels = updated.shape[1]
    values = updated[row].astype(F32)
    normed = layer_norm(values, 0)
    natural = normed.T.astype(BF16)

    def put(target, block, array):
        target[row, :, block * channels : (block + 1) * channels] = array.astype(BF16)

    put(mixed, 0, dot(turned(attn_proj[:, channels : 2 * channels]), normed.astype(BF16), (1, 0)))
    put(mixed, 1, dot(natural, attn_proj[:, 2 * channels : 3 * channels], (1, 0)))
    if late is not None:
        put(mixed, 2, dot(natural, attn_proj[:, :channels], (1, 0)) * score_scale)
        put(late, 0, sigmoid(dot(natural, attn_proj[:, 3 * channels :], (1, 0))))
        put(late, 1, values.T)


def own_body(updated, attn_proj, mixed, late, *, score_scale):
    def step(row, carry):
        project(updated, attn_proj, mixed, row, score_scale, late)
        return carry

    lax.fori_loop(0, updated.shape[0], step, 0, unroll=8)


def other_body(attn_proj, *rest):
    pieces = len(rest) // 2
    for updated, target in zip(rest[:pieces], rest[pieces:]):

        def step(row, carry):
            project(updated, attn_proj, target, row, None)
            return carry

        lax.fori_loop(0, updated.shape[0], step, 0, unroll=8)


def attend_body(length, mine, sibling, attn_out, late, *rest):
    mixed, (out_hbm, out, bias_held, sems) = rest[:-4], rest[-4:]
    pieces = len(mixed)
    rows, cols, channels = out.shape
    heads = mine.shape[1]
    me = lax.axis_index("ch")
    its_core = lax.rem(lax.axis_index("row"), 2)
    head_of = lax.broadcasted_iota(jnp.int32, (1, channels), 1) // (channels // heads)
    count = sems.shape[1]
    sends = chunked([(out, out_hbm)], sems, 0, count)
    chips = cols // rows // 2
    for piece in range(pieces):
        block = lax.rem(me + piece, pieces)
        token = block * cols + lax.broadcasted_iota(jnp.int32, (1, cols), 1)
        key_term = jnp.where(token < length[0], 0.0, -1e9)
        for part, core in ((mine, its_core), (sibling, 1 - its_core)):
            for chip in range(chips):
                tiles = part[chip * pieces + block]
                for head in range(heads):
                    first = pl.multiple_of(head * cols + (chip * 2 + core) * rows, rows)
                    bias_held[pl.ds(first, rows), piece * cols : (piece + 1) * cols] = (
                        tiles[head].astype(F32) + key_term
                    )
    both_of = jnp.concatenate([head_of, head_of], axis=1)
    masks = [(head_of == head).astype(BF16) for head in range(heads)]
    ones = jnp.ones((pieces * cols, channels), BF16)

    def load(row):
        keys = jnp.concatenate([part[row, :, :channels] for part in mixed], axis=1)
        values = jnp.concatenate([part[row, :, channels : 2 * channels] for part in mixed], axis=0)
        values = jnp.concatenate([values, ones], axis=1)
        return keys, values, mixed[0][row, :, 2 * channels :]

    def finish(row, total):
        attended = total[:, :channels] / total[:, channels:]
        gate = late[row, :, :channels].astype(F32)
        gated = (attended * gate).astype(BF16)
        residual = late[row, :, channels:].astype(F32)
        out[row] = (residual + dot(gated, attn_out[...], (1, 0))).astype(BF16)

    per_chunk = rows // count
    loaded, logits, weights = {}, {}, {}
    for time in range(rows + 2):
        row = time - 2
        if row >= 0:
            sums = dot(weights.pop(row), loaded.pop(row)[1], (1, 0))
            total = sums[:cols]
            for head in range(1, heads):
                total = jnp.where(both_of == head, sums[head * cols : (head + 1) * cols], total)
            finish(row, total)
            chunk, place_in = divmod(row, per_chunk)
            if place_in == per_chunk - 1:
                for copy in sends[chunk]:
                    copy.start()
        row = time - 1
        if 0 <= row < rows:
            scores = logits.pop(row)
            top = jnp.max(scores, axis=-1, keepdims=True)
            weights[row] = jnp.exp((scores - top).astype(BF16))
        row = time
        if row < rows:
            loaded[row] = load(row)
            keys, _, query = loaded[row]
            queries = jnp.concatenate([query * mask for mask in masks], axis=0)
            logits[row] = dot(queries, keys, (1, 0)) + bias_held[...]
    for send in sends:
        for copy in send:
            copy.wait()


def local(
    pair_act, valid_count, edge_proj, edge_gate, tri_gate, tri_out, attn_proj, bias_proj, attn_out
):
    rows, cols, channels = pair_act.shape
    heads = bias_proj.shape[1]
    row_devices = lax.axis_size("row")
    col_devices = lax.axis_size("ch")
    devices = row_devices * col_devices
    share = devices // 2
    own = channels // share
    everyone = list(reversed(range(devices)))
    halves = [everyone[share:], everyone[:share]]
    shape = jax.ShapeDtypeStruct
    block = (rows, cols, channels)
    turned_block = (rows, channels, cols)

    def in_half(array):
        return lax.all_to_all(
            array, BOTH, split_axis=0, concat_axis=0, axis_index_groups=halves, tiled=True
        )


    weight = pltpu.VMEM((channels, channels), BF16)
    offsets = chip_offsets()
    tile = (own, rows, cols)

    def edges(side, source):
        outs = [shape((devices,) + tile, BF16), shape(block, BF16)]
        return call(
            functools.partial(edges_body, side=side),
            "right_edges" if side else "left_edges",
            outs if side else [shape((len(offsets),) + tile, BF16)] * 2,
            4,
            [
                pltpu.VMEM(block, BF16),
                weight,
                weight,
                pltpu.VMEM((channels * rows, cols), F32),
                pltpu.VMEM((share,) + tile, BF16),
                pltpu.SemaphoreType.DMA((3, 5)),
            ],
            smem=1,
            space=HBM,
            out_space=HBM if side else VMEM,
            flops=3e9,
        )(valid_count, *[in_hbm(a) for a in (source, edge_proj, edge_gate)])

    def flipped(array, bits):
        return lax.ppermute(array, BOTH, [(d, d ^ bits) for d in range(devices)])

    right, normed = edges(1, pair_act)
    right = lax.all_to_all(right, BOTH, split_axis=0, concat_axis=0, tiled=True)
    mine, theirs = edges(0, normed)
    left = call(pack_body, "pack", [shape((2,) + tile, BF16)] * len(offsets), 2)(
        mine, flipped(theirs, col_devices)
    )
    left = [flipped(part, offset) if offset else part for part, offset in zip(left, offsets)]
    tri_gating, source, bias_weights = call(
        gate_body,
        "tri_gate",
        [shape(turned_block, BF16)] * 2 + [shape((heads, channels), BF16)],
        4,
        flops=2e9,
    )(pair_act, normed, tri_gate, bias_proj)
    tri_gating, source, bias_weights, *left = lax.optimization_barrier(
        (tri_gating, source, bias_weights, *left)
    )
    triangle_shape = (row_devices // 2, col_devices, own, rows, cols)
    (triangle,) = call(
        triangle_body,
        "triangle",
        [shape(triangle_shape, BF16)],
        1 + len(left),
        flops=2e9,
    )(right.reshape((row_devices,) + triangle_shape[1:]), *left)
    triangle = in_half(triangle.reshape(share, own, rows, cols))
    bias_shape = (heads, rows, cols)
    updated, bias = call(
        update_body,
        "update",
        [shape(turned_block, BF16), shape(bias_shape, BF16)],
        5,
        [pltpu.VMEM((channels * rows, cols), F32), pltpu.VMEM((heads * rows, cols), F32)],
        flops=2e9,
    )(triangle.reshape(channels, rows, cols), source, tri_gating, tri_out, bias_weights)
    per_part = row_devices // col_devices
    parts = [bias] + [
        flipped(bias, flip * per_part * col_devices) for flip in range(1, col_devices)
    ]
    (dealt,) = call(
        deal_body, "deal_bias", [shape((per_part // 2 * col_devices,) + bias_shape, BF16)], col_devices
    )(*parts)
    one_core = []
    for part in range(col_devices):
        for core in range(2):
            members = range(part * per_part + core, (part + 1) * per_part, 2)
            one_core.append([r * col_devices + c for r in members for c in range(col_devices)])

    others = [
        lax.ppermute(updated, "ch", [((c + s) % col_devices, c) for c in range(col_devices)])
        for s in range(1, col_devices)
    ]
    mixed_shape = (rows, cols, 3 * channels)
    key_shape = (rows, cols, 2 * channels)
    mixed, late = call(
        functools.partial(own_body, score_scale=(channels // heads) ** (-0.5)),
        "own_projections",
        [shape(mixed_shape, BF16), shape(key_shape, BF16)],
        2,
        flops=2e9,
    )(updated, attn_proj)
    dealt, mixed, late = lax.optimization_barrier((dealt, mixed, late))
    bias = lax.all_to_all(
        dealt, BOTH, split_axis=0, concat_axis=0, axis_index_groups=one_core, tiled=True
    )
    bias, *others = lax.optimization_barrier((bias, *others))
    keys = call(
        other_body,
        "other_keys",
        [shape(key_shape, BF16)] * len(others),
        1 + len(others),
        flops=3e9,
    )(attn_proj, *others)
    (result,) = call(
        attend_body,
        "attend",
        [shape(block, BF16)],
        5 + col_devices,
        [
            pltpu.VMEM(block, BF16),
            pltpu.VMEM((heads * cols, col_devices * cols), F32),
            pltpu.SemaphoreType.DMA((1, rows // 2)),
        ],
        smem=1,
        out_space=HBM,
    )(valid_count, bias, flipped(bias, col_devices), attn_out, late, mixed, *keys)
    return result


def solution(mesh):
    placed = (P("row", "ch", None), P(), P(), P(), P(), P(), P(), P(), P())
    return jax.shard_map(
        local, mesh=mesh, in_specs=placed, out_specs=P("row", "ch", None), check_vma=False
    )
```

```python
import functools
import math

import jax
import jax.numpy as jnp
from jax import lax
from jax.experimental import pallas as pl
from jax.experimental.pallas import tpu as pltpu
from jax.sharding import PartitionSpec as P

EPS = 1e-05
BOTH = ("row", "ch")
F32 = jnp.float32
BF16 = jnp.bfloat16
VMEM = pl.BlockSpec(memory_space=pltpu.VMEM)
SMEM = pl.BlockSpec(memory_space=pltpu.SMEM)
HBM = pl.BlockSpec(memory_space=pltpu.HBM)
ANY = pl.BlockSpec(memory_space=pl.ANY)


def layer_norm(values, axis):
    centre = values - jnp.mean(values, axis=axis, keepdims=True)
    spread = jnp.mean(centre * centre, axis=axis, keepdims=True)
    return centre * lax.rsqrt(spread + EPS)


def in_hbm(array):
    return pltpu.with_memory_space_constraint(array, pltpu.HBM)


def sigmoid(values):
    return 0.5 * jnp.tanh(0.5 * values) + 0.5


def dot(a, b, dims):
    return lax.dot_general(a, b, ((dims[:1], dims[1:]), ((), ())), preferred_element_type=F32)


def call(body, name, outs, ins, scratch=(), flops=1e8, smem=0, space=VMEM, out_space=VMEM, specs=None):
    sizes = [math.prod(a.shape) * a.dtype.itemsize for a in outs]
    spaces = out_space if isinstance(out_space, list) else [out_space] * len(outs)
    outs = [pltpu.HBM(a.shape, a.dtype) if b is HBM else a for a, b in zip(outs, spaces)]
    return pl.pallas_call(
        body,
        out_shape=outs,
        in_specs=specs or [SMEM] * smem + [space] * (ins - smem),
        out_specs=spaces,
        scratch_shapes=list(scratch),
        compiler_params=pltpu.CompilerParams(vmem_limit_bytes=16 * 2**20),
        cost_estimate=pl.CostEstimate(
            flops=int(flops), bytes_accessed=2 * sum(sizes), transcendentals=0
        ),
        name=name,
    )


def turned(weights):
    return weights.astype(F32).T.astype(BF16)


def run(copies):
    for copy in copies:
        copy.start()
    for copy in copies:
        copy.wait()


def place():
    per_half = lax.axis_size("row") // 2
    columns = lax.axis_size("ch")
    row = lax.rem(lax.axis_index("row"), per_half)
    core = lax.rem(row, 2)
    return (row - core) * columns + lax.axis_index("ch"), core


def chip_offsets():
    columns = lax.axis_size("ch")
    share = lax.axis_size("row") // 2 * columns
    return [o for o in range(share) if o // columns % 2 == 0]


def chunked(pairs, sems, first, chunks):
    rows = pairs[0][0].shape[0]
    size = rows // chunks
    return [
        [
            pltpu.make_async_copy(
                source.at[pl.ds(chunk * size, size)],
                target.at[pl.ds(chunk * size, size)],
                sems.at[first + k, chunk],
            )
            for k, (source, target) in enumerate(pairs)
        ]
        for chunk in range(chunks)
    ]


def edges_body(length, source_hbm, proj_hbm, gate_hbm, *rest, side):
    outs = rest[:-6]
    source, proj, gate, held, out, sems = rest[-6:]
    rows, cols, channels = source.shape
    share, own = out.shape[:2]
    columns = lax.axis_size("ch")
    span = pl.ds(side * channels, channels)
    fetches = [
        pltpu.make_async_copy(proj_hbm.at[:, span], proj, sems.at[0, 2]),
        pltpu.make_async_copy(gate_hbm.at[:, span], gate, sems.at[0, 3]),
    ]
    chunks = chunked([(source_hbm, source)], sems, 0, 2)
    for copy in fetches + chunks[0] + chunks[1]:
        copy.start()
    row_offset = lax.axis_index("row") * rows
    col_offset = lax.axis_index("ch") * cols
    count = length[0]
    tokens = col_offset + lax.broadcasted_iota(jnp.int32, (1, cols), 1)
    col_valid = jnp.where(tokens < count, 0.5, 0.0)
    for copy in fetches:
        copy.wait()
    weights = jnp.concatenate([turned(proj[...]), turned(gate[...])], axis=0)

    def step(row, carry):
        values = source[row]
        if side:
            values = layer_norm(values.astype(F32), -1).astype(BF16)
            source[row] = values
        mixed = dot(weights, values, (1, 1))
        valid = col_valid * (row_offset + row < count).astype(F32)
        twice = jnp.tanh(0.5 * mixed[channels:]) + 1.0
        held[pl.ds(row, channels, stride=rows), :] = twice * (mixed[:channels] * valid)
        return carry

    for (copy,) in chunks:
        copy.wait()
    lax.fori_loop(0, rows, step, 0, unroll=rows)
    sends = []
    if side:
        sends.append(pltpu.make_async_copy(source, outs[1], sems.at[1, 0]))
        sends[0].start()
    group = share // 4
    for device in range(share):
        part = held[device * own * rows : (device + 1) * own * rows, :].astype(BF16)
        position = share - 1 - device
        out[position] = part.reshape(own, rows, cols)
        if side and device % group == group - 1:
            for k in range(2):
                source_part = out.at[pl.ds(position, group)]
                target = outs[0].at[pl.ds(k * share + position, group)]
                sends.append(
                    pltpu.make_async_copy(source_part, target, sems.at[1 + k, 1 + device // group])
                )
                sends[-1].start()
    if not side:
        chip, core = place()
        for k, offset in enumerate(chip_offsets()):
            for other in range(2):
                index = jnp.bitwise_xor(chip, offset) + lax.rem(core + other, 2) * columns
                outs[other][k] = out[index]
    for copy in sends:
        copy.wait()


def pack_body(mine, sibling, *outs):
    _, core = place()
    for k, out in enumerate(outs):
        out[core] = mine[k]
        out[1 - core] = sibling[k]


def gate_body(pair, normed, weights, bias_proj, out, source, bias_weights):
    turned_weights = turned(weights[...])
    bias_weights[...] = turned(bias_proj[...])

    def step(row, carry):
        out[row] = sigmoid(dot(turned_weights, normed[row], (1, 1))).astype(BF16)
        source[row] = pair[row].astype(F32).T.astype(BF16)
        return carry

    lax.fori_loop(0, pair.shape[0], step, 0, unroll=2)


def triangle_body(right, *rest):
    parts, held = rest[:-1], rest[-1]
    row_devices, col_devices, own, rows, cols = right.shape
    chip, _ = place()
    chip_row = lax.div(chip, col_devices)
    me = lax.axis_index("ch")
    groups = [(first, core) for first in range(0, row_devices // 2, 2) for core in range(2)]
    offsets = chip_offsets()
    for channel in range(own):
        left, whole = [], []
        for flip in range(col_devices):
            left.append(
                jnp.concatenate(
                    [
                        parts[offsets.index(first * col_devices + flip)][core, channel]
                        for first, core in groups
                    ],
                    axis=0,
                )
            )
            whole.append(right[:, jnp.bitwise_xor(me, flip), channel].reshape(-1, cols))
        triangle = dot(
            jnp.concatenate(left, axis=1), jnp.concatenate(whole, axis=1), (1, 1)
        ).astype(BF16)
        for k, (first, core) in enumerate(groups):
            for part in range(col_devices):
                row = row_devices // 2 - 1 - core - jnp.bitwise_xor(chip_row, first)
                held[row, col_devices - 1 - part, channel] = triangle[
                    k * rows : (k + 1) * rows, part * cols : (part + 1) * cols
                ]


def deal_body(*refs):
    parts, out = refs[:-1], refs[-1]
    columns = len(parts)
    per_part = lax.axis_size("row") // columns
    part = lax.div(lax.axis_index("row"), per_part)
    for col in range(columns):
        value = parts[0][...]
        for flip in range(1, columns):
            value = jnp.where(jnp.bitwise_xor(part, col) == flip, parts[flip][...], value)
        for chip in range(out.shape[0] // columns):
            out[chip * columns + col] = value


def spread_sum(values):
    lead = 8
    split = values.reshape((values.shape[0] // lead, lead) + values.shape[1:])
    return jnp.sum(jnp.sum(split, axis=0), axis=0, keepdims=True)


def update_body(triangle, source, gate, tri_out, bias_proj, updated, bias, held, bias_held):
    channels, rows, cols = triangle.shape
    heads = bias_proj.shape[0]
    values = triangle[...].astype(F32)
    centre = values - spread_sum(values) * (1.0 / channels)
    spread = spread_sum(centre * centre) * (1.0 / channels)
    held[...] = (centre * lax.rsqrt(spread + EPS)).reshape(channels * rows, cols)
    out_weights = turned(tri_out[...])
    bias_weights = bias_proj[...]

    def step(row, carry):
        tri_normed = held[pl.ds(row, channels, stride=rows), :].astype(BF16)
        update = gate[row].astype(F32) * dot(out_weights, tri_normed, (1, 0))
        mine = (source[row].astype(F32) + update).astype(BF16)
        updated[row] = mine
        normed = layer_norm(mine.astype(F32), 0).astype(BF16)
        bias_held[pl.ds(row, heads, stride=rows), :] = dot(bias_weights, normed, (1, 0))
        return carry

    lax.fori_loop(0, rows, step, 0, unroll=rows)
    bias[...] = bias_held[...].astype(BF16).reshape(heads, rows, cols)


def project(updated, attn_proj, mixed, row, score_scale, late=None):
    channels = updated.shape[1]
    values = updated[row].astype(F32)
    normed = layer_norm(values, 0)
    natural = normed.T.astype(BF16)

    def put(target, block, array):
        target[row, :, block * channels : (block + 1) * channels] = array.astype(BF16)

    put(mixed, 0, dot(turned(attn_proj[:, channels : 2 * channels]), normed.astype(BF16), (1, 0)))
    put(mixed, 1, dot(natural, attn_proj[:, 2 * channels : 3 * channels], (1, 0)))
    if late is not None:
        put(mixed, 2, dot(natural, attn_proj[:, :channels], (1, 0)) * score_scale)
        put(late, 0, sigmoid(dot(natural, attn_proj[:, 3 * channels :], (1, 0))))
        put(late, 1, values.T)


def own_body(updated, attn_proj, mixed, late, *, score_scale):
    def step(row, carry):
        project(updated, attn_proj, mixed, row, score_scale, late)
        return carry

    lax.fori_loop(0, updated.shape[0], step, 0, unroll=8)


def other_body(attn_proj, *rest):
    pieces = len(rest) // 2
    for updated, target in zip(rest[:pieces], rest[pieces:]):

        def step(row, carry):
            project(updated, attn_proj, target, row, None)
            return carry

        lax.fori_loop(0, updated.shape[0], step, 0, unroll=8)


def attend_body(length, mine, sibling, attn_out, late, *rest):
    mixed, (out_hbm, out, bias_held, sems) = rest[:-4], rest[-4:]
    pieces = len(mixed)
    rows, cols, channels = out.shape
    heads = mine.shape[1]
    me = lax.axis_index("ch")
    its_core = lax.rem(lax.axis_index("row"), 2)
    head_of = lax.broadcasted_iota(jnp.int32, (1, channels), 1) // (channels // heads)
    count = sems.shape[1]
    sends = chunked([(out, out_hbm)], sems, 0, count)
    chips = cols // rows // 2
    for piece in range(pieces):
        block = lax.rem(me + piece, pieces)
        token = block * cols + lax.broadcasted_iota(jnp.int32, (1, cols), 1)
        key_term = jnp.where(token < length[0], 0.0, -1e9)
        for part, core in ((mine, its_core), (sibling, 1 - its_core)):
            for chip in range(chips):
                tiles = part[chip * pieces + block]
                for head in range(heads):
                    first = pl.multiple_of(head * cols + (chip * 2 + core) * rows, rows)
                    bias_held[pl.ds(first, rows), piece * cols : (piece + 1) * cols] = (
                        tiles[head].astype(F32) + key_term
                    )
    both_of = jnp.concatenate([head_of, head_of], axis=1)
    masks = [(head_of == head).astype(BF16) for head in range(heads)]
    ones = jnp.ones((pieces * cols, channels), BF16)

    def load(row):
        keys = jnp.concatenate([part[row, :, :channels] for part in mixed], axis=1)
        values = jnp.concatenate([part[row, :, channels : 2 * channels] for part in mixed], axis=0)
        values = jnp.concatenate([values, ones], axis=1)
        return keys, values, mixed[0][row, :, 2 * channels :]

    def finish(row, total):
        attended = total[:, :channels] / total[:, channels:]
        gate = late[row, :, :channels].astype(F32)
        gated = (attended * gate).astype(BF16)
        residual = late[row, :, channels:].astype(F32)
        out[row] = (residual + dot(gated, attn_out[...], (1, 0))).astype(BF16)

    per_chunk = rows // count
    loaded, logits, weights = {}, {}, {}
    for time in range(rows + 2):
        row = time
        if row < rows:
            loaded[row] = load(row)
            keys, _, query = loaded[row]
            queries = jnp.concatenate([query * mask for mask in masks], axis=0)
            logits[row] = dot(queries, keys, (1, 0)) + bias_held[...]
        row = time - 1
        if 0 <= row < rows:
            scores = logits.pop(row)
            top = jnp.max(scores, axis=-1, keepdims=True)
            weights[row] = jnp.exp((scores - top).astype(BF16))
        row = time - 2
        if row >= 0:
            sums = dot(weights.pop(row), loaded.pop(row)[1], (1, 0))
            total = sums[:cols]
            for head in range(1, heads):
                total = jnp.where(both_of == head, sums[head * cols : (head + 1) * cols], total)
            finish(row, total)
            chunk, place_in = divmod(row, per_chunk)
            if place_in == per_chunk - 1:
                for copy in sends[chunk]:
                    copy.start()
    for send in sends:
        for copy in send:
            copy.wait()


def local(
    pair_act, valid_count, edge_proj, edge_gate, tri_gate, tri_out, attn_proj, bias_proj, attn_out
):
    rows, cols, channels = pair_act.shape
    heads = bias_proj.shape[1]
    row_devices = lax.axis_size("row")
    col_devices = lax.axis_size("ch")
    devices = row_devices * col_devices
    share = devices // 2
    own = channels // share
    everyone = list(reversed(range(devices)))
    halves = [everyone[share:], everyone[:share]]
    shape = jax.ShapeDtypeStruct
    block = (rows, cols, channels)
    turned_block = (rows, channels, cols)

    def in_half(array):
        return lax.all_to_all(
            array, BOTH, split_axis=0, concat_axis=0, axis_index_groups=halves, tiled=True
        )


    weight = pltpu.VMEM((channels, channels), BF16)
    offsets = chip_offsets()
    tile = (own, rows, cols)

    def edges(side, source):
        outs = [shape((devices,) + tile, BF16), shape(block, BF16)]
        return call(
            functools.partial(edges_body, side=side),
            "right_edges" if side else "left_edges",
            outs if side else [shape((len(offsets),) + tile, BF16)] * 2,
            4,
            [
                pltpu.VMEM(block, BF16),
                weight,
                weight,
                pltpu.VMEM((channels * rows, cols), F32),
                pltpu.VMEM((share,) + tile, BF16),
                pltpu.SemaphoreType.DMA((3, 5)),
            ],
            smem=1,
            space=HBM,
            out_space=HBM if side else VMEM,
            flops=3e9,
        )(valid_count, *[in_hbm(a) for a in (source, edge_proj, edge_gate)])

    def flipped(array, bits):
        return lax.ppermute(array, BOTH, [(d, d ^ bits) for d in range(devices)])

    right, normed = edges(1, pair_act)
    right = lax.all_to_all(right, BOTH, split_axis=0, concat_axis=0, tiled=True)
    mine, theirs = edges(0, normed)
    left = call(pack_body, "pack", [shape((2,) + tile, BF16)] * len(offsets), 2)(
        mine, flipped(theirs, col_devices)
    )
    left = [flipped(part, offset) if offset else part for part, offset in zip(left, offsets)]
    tri_gating, source, bias_weights = call(
        gate_body,
        "tri_gate",
        [shape(turned_block, BF16)] * 2 + [shape((heads, channels), BF16)],
        4,
        flops=2e9,
    )(pair_act, normed, tri_gate, bias_proj)
    tri_gating, source, bias_weights, *left = lax.optimization_barrier(
        (tri_gating, source, bias_weights, *left)
    )
    triangle_shape = (row_devices // 2, col_devices, own, rows, cols)
    (triangle,) = call(
        triangle_body,
        "triangle",
        [shape(triangle_shape, BF16)],
        1 + len(left),
        flops=2e9,
    )(right.reshape((row_devices,) + triangle_shape[1:]), *left)
    triangle = in_half(triangle.reshape(share, own, rows, cols))
    bias_shape = (heads, rows, cols)
    updated, bias = call(
        update_body,
        "update",
        [shape(turned_block, BF16), shape(bias_shape, BF16)],
        5,
        [pltpu.VMEM((channels * rows, cols), F32), pltpu.VMEM((heads * rows, cols), F32)],
        flops=2e9,
    )(triangle.reshape(channels, rows, cols), source, tri_gating, tri_out, bias_weights)
    per_part = row_devices // col_devices
    parts = [bias] + [
        flipped(bias, flip * per_part * col_devices) for flip in range(1, col_devices)
    ]
    (dealt,) = call(
        deal_body, "deal_bias", [shape((per_part // 2 * col_devices,) + bias_shape, BF16)], col_devices
    )(*parts)
    one_core = []
    for part in range(col_devices):
        for core in range(2):
            members = range(part * per_part + core, (part + 1) * per_part, 2)
            one_core.append([r * col_devices + c for r in members for c in range(col_devices)])

    others = [
        lax.ppermute(updated, "ch", [((c + s) % col_devices, c) for c in range(col_devices)])
        for s in range(1, col_devices)
    ]
    mixed_shape = (rows, cols, 3 * channels)
    key_shape = (rows, cols, 2 * channels)
    mixed, late = call(
        functools.partial(own_body, score_scale=(channels // heads) ** (-0.5)),
        "own_projections",
        [shape(mixed_shape, BF16), shape(key_shape, BF16)],
        2,
        flops=2e9,
    )(updated, attn_proj)
    dealt, mixed, late = lax.optimization_barrier((dealt, mixed, late))
    bias = lax.all_to_all(
        dealt, BOTH, split_axis=0, concat_axis=0, axis_index_groups=one_core, tiled=True
    )
    bias, *others = lax.optimization_barrier((bias, *others))
    keys = call(
        other_body,
        "other_keys",
        [shape(key_shape, BF16)] * len(others),
        1 + len(others),
        flops=3e9,
    )(attn_proj, *others)
    (result,) = call(
        attend_body,
        "attend",
        [shape(block, BF16)],
        5 + col_devices,
        [
            pltpu.VMEM(block, BF16),
            pltpu.VMEM((heads * cols, col_devices * cols), F32),
            pltpu.SemaphoreType.DMA((1, rows // 2)),
        ],
        smem=1,
        out_space=HBM,
    )(valid_count, bias, flipped(bias, col_devices), attn_out, late, mixed, *keys)
    return result


def solution(mesh):
    placed = (P("row", "ch", None), P(), P(), P(), P(), P(), P(), P(), P())
    return jax.shard_map(
        local, mesh=mesh, in_specs=placed, out_specs=P("row", "ch", None), check_vma=False
    )
```

```python
import functools
import math

import jax
import jax.numpy as jnp
from jax import lax
from jax.experimental import pallas as pl
from jax.experimental.pallas import tpu as pltpu
from jax.sharding import PartitionSpec as P

EPS = 1e-05
BOTH = ("row", "ch")
F32 = jnp.float32
BF16 = jnp.bfloat16
VMEM = pl.BlockSpec(memory_space=pltpu.VMEM)
SMEM = pl.BlockSpec(memory_space=pltpu.SMEM)
HBM = pl.BlockSpec(memory_space=pltpu.HBM)
ANY = pl.BlockSpec(memory_space=pl.ANY)


def layer_norm(values, axis):
    centre = values - jnp.mean(values, axis=axis, keepdims=True)
    spread = jnp.mean(centre * centre, axis=axis, keepdims=True)
    return centre * lax.rsqrt(spread + EPS)


def in_hbm(array):
    return pltpu.with_memory_space_constraint(array, pltpu.HBM)


def sigmoid(values):
    return 0.5 * jnp.tanh(0.5 * values) + 0.5


def dot(a, b, dims):
    return lax.dot_general(a, b, ((dims[:1], dims[1:]), ((), ())), preferred_element_type=F32)


def call(body, name, outs, ins, scratch=(), flops=1e8, smem=0, space=VMEM, out_space=VMEM, specs=None):
    sizes = [math.prod(a.shape) * a.dtype.itemsize for a in outs]
    spaces = out_space if isinstance(out_space, list) else [out_space] * len(outs)
    outs = [pltpu.HBM(a.shape, a.dtype) if b is HBM else a for a, b in zip(outs, spaces)]
    return pl.pallas_call(
        body,
        out_shape=outs,
        in_specs=specs or [SMEM] * smem + [space] * (ins - smem),
        out_specs=spaces,
        scratch_shapes=list(scratch),
        compiler_params=pltpu.CompilerParams(vmem_limit_bytes=16 * 2**20),
        cost_estimate=pl.CostEstimate(
            flops=int(flops), bytes_accessed=2 * sum(sizes), transcendentals=0
        ),
        name=name,
    )


def turned(weights):
    return weights.astype(F32).T.astype(BF16)


def run(copies):
    for copy in copies:
        copy.start()
    for copy in copies:
        copy.wait()


def place():
    per_half = lax.axis_size("row") // 2
    columns = lax.axis_size("ch")
    row = lax.rem(lax.axis_index("row"), per_half)
    core = lax.rem(row, 2)
    return (row - core) * columns + lax.axis_index("ch"), core


def chip_offsets():
    columns = lax.axis_size("ch")
    share = lax.axis_size("row") // 2 * columns
    return [o for o in range(share) if o // columns % 2 == 0]


def chunked(pairs, sems, first, chunks):
    rows = pairs[0][0].shape[0]
    size = rows // chunks
    return [
        [
            pltpu.make_async_copy(
                source.at[pl.ds(chunk * size, size)],
                target.at[pl.ds(chunk * size, size)],
                sems.at[first + k, chunk],
            )
            for k, (source, target) in enumerate(pairs)
        ]
        for chunk in range(chunks)
    ]


def edges_body(length, source_hbm, proj_hbm, gate_hbm, *rest, side):
    outs = rest[:-6]
    source, proj, gate, held, out, sems = rest[-6:]
    rows, cols, channels = source.shape
    share, own = out.shape[:2]
    columns = lax.axis_size("ch")
    span = pl.ds(side * channels, channels)
    fetches = [
        pltpu.make_async_copy(proj_hbm.at[:, span], proj, sems.at[0, 2]),
        pltpu.make_async_copy(gate_hbm.at[:, span], gate, sems.at[0, 3]),
    ]
    chunks = chunked([(source_hbm, source)], sems, 0, 2)
    for copy in fetches + chunks[0] + chunks[1]:
        copy.start()
    row_offset = lax.axis_index("row") * rows
    col_offset = lax.axis_index("ch") * cols
    count = length[0]
    tokens = col_offset + lax.broadcasted_iota(jnp.int32, (1, cols), 1)
    col_valid = jnp.where(tokens < count, 0.5, 0.0)
    for copy in fetches:
        copy.wait()
    weights = jnp.concatenate([turned(proj[...]), turned(gate[...])], axis=0)

    def step(row, carry):
        values = source[row]
        if side:
            values = layer_norm(values.astype(F32), -1).astype(BF16)
            source[row] = values
        mixed = dot(weights, values, (1, 1))
        valid = col_valid * (row_offset + row < count).astype(F32)
        twice = jnp.tanh(0.5 * mixed[channels:]) + 1.0
        held[pl.ds(row, channels, stride=rows), :] = twice * (mixed[:channels] * valid)
        return carry

    for (copy,) in chunks:
        copy.wait()
    lax.fori_loop(0, rows, step, 0, unroll=rows)
    sends = []
    if side:
        sends.append(pltpu.make_async_copy(source, outs[1], sems.at[1, 0]))
        sends[0].start()
    group = share // 4
    for device in range(share):
        part = held[device * own * rows : (device + 1) * own * rows, :].astype(BF16)
        position = share - 1 - device
        out[position] = part.reshape(own, rows, cols)
        if side and device % group == group - 1:
            for k in range(2):
                source_part = out.at[pl.ds(position, group)]
                target = outs[0].at[pl.ds(k * share + position, group)]
                sends.append(
                    pltpu.make_async_copy(source_part, target, sems.at[1 + k, 1 + device // group])
                )
                sends[-1].start()
    if not side:
        chip, core = place()
        for k, offset in enumerate(chip_offsets()):
            for other in range(2):
                index = jnp.bitwise_xor(chip, offset) + lax.rem(core + other, 2) * columns
                outs[other][k] = out[index]
    for copy in sends:
        copy.wait()


def pack_body(mine, sibling, *outs):
    _, core = place()
    for k, out in enumerate(outs):
        out[core] = mine[k]
        out[1 - core] = sibling[k]


def gate_body(pair, normed, weights, bias_proj, out, source, bias_weights):
    turned_weights = turned(weights[...])
    bias_weights[...] = turned(bias_proj[...])

    def step(row, carry):
        out[row] = sigmoid(dot(turned_weights, normed[row], (1, 1))).astype(BF16)
        source[row] = pair[row].astype(F32).T.astype(BF16)
        return carry

    lax.fori_loop(0, pair.shape[0], step, 0, unroll=2)


def triangle_body(right, *rest):
    parts, held = rest[:-1], rest[-1]
    row_devices, col_devices, own, rows, cols = right.shape
    chip, _ = place()
    chip_row = lax.div(chip, col_devices)
    me = lax.axis_index("ch")
    groups = [(first, core) for first in range(0, row_devices // 2, 2) for core in range(2)]
    offsets = chip_offsets()
    for channel in range(own):
        left, whole = [], []
        for flip in range(col_devices):
            left.append(
                jnp.concatenate(
                    [
                        parts[offsets.index(first * col_devices + flip)][core, channel]
                        for first, core in groups
                    ],
                    axis=0,
                )
            )
            whole.append(right[:, jnp.bitwise_xor(me, flip), channel].reshape(-1, cols))
        triangle = dot(
            jnp.concatenate(left, axis=1), jnp.concatenate(whole, axis=1), (1, 1)
        ).astype(BF16)
        for k, (first, core) in enumerate(groups):
            for part in range(col_devices):
                row = row_devices // 2 - 1 - core - jnp.bitwise_xor(chip_row, first)
                held[row, col_devices - 1 - part, channel] = triangle[
                    k * rows : (k + 1) * rows, part * cols : (part + 1) * cols
                ]


def deal_body(*refs):
    parts, out = refs[:-1], refs[-1]
    columns = len(parts)
    per_part = lax.axis_size("row") // columns
    part = lax.div(lax.axis_index("row"), per_part)
    for col in range(columns):
        value = parts[0][...]
        for flip in range(1, columns):
            value = jnp.where(jnp.bitwise_xor(part, col) == flip, parts[flip][...], value)
        for chip in range(out.shape[0] // columns):
            out[out.shape[0] - 1 - chip * columns - col] = value


def spread_sum(values):
    lead = 8
    split = values.reshape((values.shape[0] // lead, lead) + values.shape[1:])
    return jnp.sum(jnp.sum(split, axis=0), axis=0, keepdims=True)


def update_body(triangle, source, gate, tri_out, bias_proj, updated, bias, held, bias_held):
    channels, rows, cols = triangle.shape
    heads = bias_proj.shape[0]
    values = triangle[...].astype(F32)
    centre = values - spread_sum(values) * (1.0 / channels)
    spread = spread_sum(centre * centre) * (1.0 / channels)
    held[...] = (centre * lax.rsqrt(spread + EPS)).reshape(channels * rows, cols)
    out_weights = turned(tri_out[...])
    bias_weights = bias_proj[...]

    def step(row, carry):
        tri_normed = held[pl.ds(row, channels, stride=rows), :].astype(BF16)
        update = gate[row].astype(F32) * dot(out_weights, tri_normed, (1, 0))
        mine = (source[row].astype(F32) + update).astype(BF16)
        updated[row] = mine
        normed = layer_norm(mine.astype(F32), 0).astype(BF16)
        bias_held[pl.ds(row, heads, stride=rows), :] = dot(bias_weights, normed, (1, 0))
        return carry

    lax.fori_loop(0, rows, step, 0, unroll=rows)
    bias[...] = bias_held[...].astype(BF16).reshape(heads, rows, cols)


def project(updated, attn_proj, mixed, row, score_scale, late=None):
    channels = updated.shape[1]
    values = updated[row].astype(F32)
    normed = layer_norm(values, 0)
    natural = normed.T.astype(BF16)

    def put(target, block, array):
        target[row, :, block * channels : (block + 1) * channels] = array.astype(BF16)

    put(mixed, 0, dot(turned(attn_proj[:, channels : 2 * channels]), normed.astype(BF16), (1, 0)))
    put(mixed, 1, dot(natural, attn_proj[:, 2 * channels : 3 * channels], (1, 0)))
    if late is not None:
        put(mixed, 2, dot(natural, attn_proj[:, :channels], (1, 0)) * score_scale)
        put(late, 0, sigmoid(dot(natural, attn_proj[:, 3 * channels :], (1, 0))))
        put(late, 1, values.T)


def own_body(updated, attn_proj, mixed, late, *, score_scale):
    def step(row, carry):
        project(updated, attn_proj, mixed, row, score_scale, late)
        return carry

    lax.fori_loop(0, updated.shape[0], step, 0, unroll=8)


def other_body(attn_proj, *rest):
    pieces = len(rest) // 2
    for updated, target in zip(rest[:pieces], rest[pieces:]):

        def step(row, carry):
            project(updated, attn_proj, target, row, None)
            return carry

        lax.fori_loop(0, updated.shape[0], step, 0, unroll=8)


def attend_body(length, mine, sibling, attn_out, late, *rest):
    mixed, (out_hbm, out, bias_held, sems) = rest[:-4], rest[-4:]
    pieces = len(mixed)
    rows, cols, channels = out.shape
    heads = mine.shape[1]
    me = lax.axis_index("ch")
    its_core = lax.rem(lax.axis_index("row"), 2)
    head_of = lax.broadcasted_iota(jnp.int32, (1, channels), 1) // (channels // heads)
    count = sems.shape[1]
    sends = chunked([(out, out_hbm)], sems, 0, count)
    chips = cols // rows // 2
    for piece in range(pieces):
        block = lax.rem(me + piece, pieces)
        token = block * cols + lax.broadcasted_iota(jnp.int32, (1, cols), 1)
        key_term = jnp.where(token < length[0], 0.0, -1e9)
        for part, core in ((mine, its_core), (sibling, 1 - its_core)):
            for chip in range(chips):
                tiles = part[part.shape[0] - 1 - chip * pieces - block]
                for head in range(heads):
                    first = pl.multiple_of(head * cols + (chip * 2 + core) * rows, rows)
                    bias_held[pl.ds(first, rows), piece * cols : (piece + 1) * cols] = (
                        tiles[head].astype(F32) + key_term
                    )
    both_of = jnp.concatenate([head_of, head_of], axis=1)
    masks = [(head_of == head).astype(BF16) for head in range(heads)]
    ones = jnp.ones((pieces * cols, channels), BF16)

    def load(row):
        keys = jnp.concatenate([part[row, :, :channels] for part in mixed], axis=1)
        values = jnp.concatenate([part[row, :, channels : 2 * channels] for part in mixed], axis=0)
        values = jnp.concatenate([values, ones], axis=1)
        return keys, values, mixed[0][row, :, 2 * channels :]

    def finish(row, total):
        attended = total[:, :channels] / total[:, channels:]
        gate = late[row, :, :channels].astype(F32)
        gated = (attended * gate).astype(BF16)
        residual = late[row, :, channels:].astype(F32)
        out[row] = (residual + dot(gated, attn_out[...], (1, 0))).astype(BF16)

    per_chunk = rows // count
    loaded, logits, weights = {}, {}, {}
    for time in range(rows + 2):
        row = time
        if row < rows:
            loaded[row] = load(row)
            keys, _, query = loaded[row]
            queries = jnp.concatenate([query * mask for mask in masks], axis=0)
            logits[row] = dot(queries, keys, (1, 0)) + bias_held[...]
        row = time - 1
        if 0 <= row < rows:
            scores = logits.pop(row)
            top = jnp.max(scores, axis=-1, keepdims=True)
            weights[row] = jnp.exp((scores - top).astype(BF16))
        row = time - 2
        if row >= 0:
            sums = dot(weights.pop(row), loaded.pop(row)[1], (1, 0))
            total = sums[:cols]
            for head in range(1, heads):
                total = jnp.where(both_of == head, sums[head * cols : (head + 1) * cols], total)
            finish(row, total)
            chunk, place_in = divmod(row, per_chunk)
            if place_in == per_chunk - 1:
                for copy in sends[chunk]:
                    copy.start()
    for send in sends:
        for copy in send:
            copy.wait()


def local(
    pair_act, valid_count, edge_proj, edge_gate, tri_gate, tri_out, attn_proj, bias_proj, attn_out
):
    rows, cols, channels = pair_act.shape
    heads = bias_proj.shape[1]
    row_devices = lax.axis_size("row")
    col_devices = lax.axis_size("ch")
    devices = row_devices * col_devices
    share = devices // 2
    own = channels // share
    everyone = list(reversed(range(devices)))
    halves = [everyone[share:], everyone[:share]]
    shape = jax.ShapeDtypeStruct
    block = (rows, cols, channels)
    turned_block = (rows, channels, cols)

    def in_half(array):
        return lax.all_to_all(
            array, BOTH, split_axis=0, concat_axis=0, axis_index_groups=halves, tiled=True
        )


    weight = pltpu.VMEM((channels, channels), BF16)
    offsets = chip_offsets()
    tile = (own, rows, cols)

    def edges(side, source):
        outs = [shape((devices,) + tile, BF16), shape(block, BF16)]
        return call(
            functools.partial(edges_body, side=side),
            "right_edges" if side else "left_edges",
            outs if side else [shape((len(offsets),) + tile, BF16)] * 2,
            4,
            [
                pltpu.VMEM(block, BF16),
                weight,
                weight,
                pltpu.VMEM((channels * rows, cols), F32),
                pltpu.VMEM((share,) + tile, BF16),
                pltpu.SemaphoreType.DMA((3, 5)),
            ],
            smem=1,
            space=HBM,
            out_space=HBM if side else VMEM,
            flops=3e9,
        )(valid_count, *[in_hbm(a) for a in (source, edge_proj, edge_gate)])

    def flipped(array, bits):
        return lax.ppermute(array, BOTH, [(d, d ^ bits) for d in range(devices)])

    right, normed = edges(1, pair_act)
    right = lax.all_to_all(right, BOTH, split_axis=0, concat_axis=0, tiled=True)
    mine, theirs = edges(0, normed)
    left = call(pack_body, "pack", [shape((2,) + tile, BF16)] * len(offsets), 2)(
        mine, flipped(theirs, col_devices)
    )
    left = [flipped(part, offset) if offset else part for part, offset in zip(left, offsets)]
    tri_gating, source, bias_weights = call(
        gate_body,
        "tri_gate",
        [shape(turned_block, BF16)] * 2 + [shape((heads, channels), BF16)],
        4,
        flops=2e9,
    )(pair_act, normed, tri_gate, bias_proj)
    tri_gating, source, bias_weights, *left = lax.optimization_barrier(
        (tri_gating, source, bias_weights, *left)
    )
    triangle_shape = (row_devices // 2, col_devices, own, rows, cols)
    (triangle,) = call(
        triangle_body,
        "triangle",
        [shape(triangle_shape, BF16)],
        1 + len(left),
        flops=2e9,
    )(right.reshape((row_devices,) + triangle_shape[1:]), *left)
    triangle = in_half(triangle.reshape(share, own, rows, cols))
    bias_shape = (heads, rows, cols)
    updated, bias = call(
        update_body,
        "update",
        [shape(turned_block, BF16), shape(bias_shape, BF16)],
        5,
        [pltpu.VMEM((channels * rows, cols), F32), pltpu.VMEM((heads * rows, cols), F32)],
        flops=2e9,
    )(triangle.reshape(channels, rows, cols), source, tri_gating, tri_out, bias_weights)
    per_part = row_devices // col_devices
    parts = [bias] + [
        flipped(bias, flip * per_part * col_devices) for flip in range(1, col_devices)
    ]
    (dealt,) = call(
        deal_body, "deal_bias", [shape((per_part // 2 * col_devices,) + bias_shape, BF16)], col_devices
    )(*parts)
    one_core = []
    for part in range(col_devices):
        for core in range(2):
            members = range(part * per_part + core, (part + 1) * per_part, 2)
            group = [r * col_devices + c for r in members for c in range(col_devices)]
            one_core.append(group[::-1])

    others = [
        lax.ppermute(updated, "ch", [((c + s) % col_devices, c) for c in range(col_devices)])
        for s in range(1, col_devices)
    ]
    mixed_shape = (rows, cols, 3 * channels)
    key_shape = (rows, cols, 2 * channels)
    mixed, late = call(
        functools.partial(own_body, score_scale=(channels // heads) ** (-0.5)),
        "own_projections",
        [shape(mixed_shape, BF16), shape(key_shape, BF16)],
        2,
        flops=2e9,
    )(updated, attn_proj)
    dealt, mixed, late = lax.optimization_barrier((dealt, mixed, late))
    bias = lax.all_to_all(
        dealt, BOTH, split_axis=0, concat_axis=0, axis_index_groups=one_core, tiled=True
    )
    bias, *others = lax.optimization_barrier((bias, *others))
    keys = call(
        other_body,
        "other_keys",
        [shape(key_shape, BF16)] * len(others),
        1 + len(others),
        flops=3e9,
    )(attn_proj, *others)
    (result,) = call(
        attend_body,
        "attend",
        [shape(block, BF16)],
        5 + col_devices,
        [
            pltpu.VMEM(block, BF16),
            pltpu.VMEM((heads * cols, col_devices * cols), F32),
            pltpu.SemaphoreType.DMA((1, rows // 2)),
        ],
        smem=1,
        out_space=HBM,
    )(valid_count, bias, flipped(bias, col_devices), attn_out, late, mixed, *keys)
    return result


def solution(mesh):
    placed = (P("row", "ch", None), P(), P(), P(), P(), P(), P(), P(), P())
    return jax.shard_map(
        local, mesh=mesh, in_specs=placed, out_specs=P("row", "ch", None), check_vma=False
    )
```

```python
import functools
import math

import jax
import jax.numpy as jnp
from jax import lax
from jax.experimental import pallas as pl
from jax.experimental.pallas import tpu as pltpu
from jax.sharding import PartitionSpec as P

EPS = 1e-05
BOTH = ("row", "ch")
F32 = jnp.float32
BF16 = jnp.bfloat16
VMEM = pl.BlockSpec(memory_space=pltpu.VMEM)
SMEM = pl.BlockSpec(memory_space=pltpu.SMEM)
HBM = pl.BlockSpec(memory_space=pltpu.HBM)
ANY = pl.BlockSpec(memory_space=pl.ANY)


def layer_norm(values, axis):
    centre = values - jnp.mean(values, axis=axis, keepdims=True)
    spread = jnp.mean(centre * centre, axis=axis, keepdims=True)
    return centre * lax.rsqrt(spread + EPS)


def in_hbm(array):
    return pltpu.with_memory_space_constraint(array, pltpu.HBM)


def sigmoid(values):
    return 0.5 * jnp.tanh(0.5 * values) + 0.5


def dot(a, b, dims):
    return lax.dot_general(a, b, ((dims[:1], dims[1:]), ((), ())), preferred_element_type=F32)


def call(body, name, outs, ins, scratch=(), flops=1e8, smem=0, space=VMEM, out_space=VMEM, specs=None):
    sizes = [math.prod(a.shape) * a.dtype.itemsize for a in outs]
    spaces = out_space if isinstance(out_space, list) else [out_space] * len(outs)
    outs = [pltpu.HBM(a.shape, a.dtype) if b is HBM else a for a, b in zip(outs, spaces)]
    return pl.pallas_call(
        body,
        out_shape=outs,
        in_specs=specs or [SMEM] * smem + [space] * (ins - smem),
        out_specs=spaces,
        scratch_shapes=list(scratch),
        compiler_params=pltpu.CompilerParams(vmem_limit_bytes=16 * 2**20),
        cost_estimate=pl.CostEstimate(
            flops=int(flops), bytes_accessed=2 * sum(sizes), transcendentals=0
        ),
        name=name,
    )


def turned(weights):
    return weights.astype(F32).T.astype(BF16)


def run(copies):
    for copy in copies:
        copy.start()
    for copy in copies:
        copy.wait()


def place():
    per_half = lax.axis_size("row") // 2
    columns = lax.axis_size("ch")
    row = lax.rem(lax.axis_index("row"), per_half)
    core = lax.rem(row, 2)
    return (row - core) * columns + lax.axis_index("ch"), core


def chip_offsets():
    columns = lax.axis_size("ch")
    share = lax.axis_size("row") // 2 * columns
    return [o for o in range(share) if o // columns % 2 == 0]


def chunked(pairs, sems, first, chunks):
    rows = pairs[0][0].shape[0]
    size = rows // chunks
    return [
        [
            pltpu.make_async_copy(
                source.at[pl.ds(chunk * size, size)],
                target.at[pl.ds(chunk * size, size)],
                sems.at[first + k, chunk],
            )
            for k, (source, target) in enumerate(pairs)
        ]
        for chunk in range(chunks)
    ]


def edges_body(
    length, source_hbm, proj_hbm, gate_hbm, right, normed, mine, theirs, source, proj, gate, held, out, sems
):
    rows, cols, channels = source.shape
    share, own = out.shape[:2]
    columns = lax.axis_size("ch")
    fetches = [
        pltpu.make_async_copy(proj_hbm, proj, sems.at[0, 2]),
        pltpu.make_async_copy(gate_hbm, gate, sems.at[0, 3]),
    ]
    chunks = chunked([(source_hbm, source)], sems, 0, 2)
    for copy in fetches + chunks[0] + chunks[1]:
        copy.start()
    row_offset = lax.axis_index("row") * rows
    col_offset = lax.axis_index("ch") * cols
    count = length[0]
    tokens = col_offset + lax.broadcasted_iota(jnp.int32, (1, cols), 1)
    col_valid = jnp.where(tokens < count, 0.5, 0.0)
    for copy in fetches:
        copy.wait()
    spans = [slice(side * channels, (side + 1) * channels) for side in range(2)]
    weights = [
        jnp.concatenate([turned(proj[:, span]), turned(gate[:, span])], axis=0) for span in spans
    ]
    for (copy,) in chunks:
        copy.wait()
    sends = []
    for side in (1, 0):

        def step(row, carry):
            values = source[row]
            if side:
                values = layer_norm(values.astype(F32), -1).astype(BF16)
                source[row] = values
            mixed = dot(weights[side], values, (1, 1))
            valid = col_valid * (row_offset + row < count).astype(F32)
            twice = jnp.tanh(0.5 * mixed[channels:]) + 1.0
            held[side, pl.ds(row, channels, stride=rows), :] = twice * (mixed[:channels] * valid)
            return carry

        lax.fori_loop(0, rows, step, 0, unroll=rows)
        if side:
            sends.append(pltpu.make_async_copy(source, normed, sems.at[1, 0]))
            sends[0].start()
        group = share // 4
        for device in range(share):
            part = held[side, device * own * rows : (device + 1) * own * rows, :].astype(BF16)
            position = share - 1 - device
            if side:
                out[position] = part.reshape(own, rows, cols)
            else:
                held_left = part.reshape(own, rows, cols)
                theirs_at = position % (2 * columns) // columns
                place_of(position, theirs_at, held_left, mine, theirs)
            if side and device % group == group - 1:
                for k in range(2):
                    source_part = out.at[pl.ds(position, group)]
                    target = right.at[pl.ds(k * share + position, group)]
                    sends.append(
                        pltpu.make_async_copy(
                            source_part, target, sems.at[1 + k, 1 + device // group]
                        )
                    )
                    sends[-1].start()
    for copy in sends:
        copy.wait()


def place_of(position, its_core, block, mine, theirs):
    columns = lax.axis_size("ch")
    chip, core = place()
    offset = jnp.bitwise_xor(chip, position - its_core * columns)
    col = lax.rem(offset, columns)
    index = lax.div(offset, 2 * columns) * columns + col

    @pl.when(core == its_core)
    def _():
        mine[index] = block

    @pl.when(core != its_core)
    def _():
        theirs[index] = block


def pack_body(mine, sibling, *outs):
    _, core = place()
    for k, out in enumerate(outs):
        out[core] = mine[k]
        out[1 - core] = sibling[k]


def gate_body(pair, normed, weights, bias_proj, out, source, bias_weights):
    turned_weights = turned(weights[...])
    bias_weights[...] = turned(bias_proj[...])

    def step(row, carry):
        out[row] = sigmoid(dot(turned_weights, normed[row], (1, 1))).astype(BF16)
        source[row] = pair[row].astype(F32).T.astype(BF16)
        return carry

    lax.fori_loop(0, pair.shape[0], step, 0, unroll=2)


def triangle_body(right, *rest):
    parts, held = rest[:-1], rest[-1]
    row_devices, col_devices, own, rows, cols = right.shape
    chip, _ = place()
    chip_row = lax.div(chip, col_devices)
    me = lax.axis_index("ch")
    groups = [(first, core) for first in range(0, row_devices // 2, 2) for core in range(2)]
    offsets = chip_offsets()
    for channel in range(own):
        left, whole = [], []
        for flip in range(col_devices):
            left.append(
                jnp.concatenate(
                    [
                        parts[offsets.index(first * col_devices + flip)][core, channel]
                        for first, core in groups
                    ],
                    axis=0,
                )
            )
            whole.append(right[:, jnp.bitwise_xor(me, flip), channel].reshape(-1, cols))
        triangle = dot(
            jnp.concatenate(left, axis=1), jnp.concatenate(whole, axis=1), (1, 1)
        ).astype(BF16)
        for k, (first, core) in enumerate(groups):
            for part in range(col_devices):
                row = row_devices // 2 - 1 - core - jnp.bitwise_xor(chip_row, first)
                held[row, col_devices - 1 - part, channel] = triangle[
                    k * rows : (k + 1) * rows, part * cols : (part + 1) * cols
                ]


def deal_body(*refs):
    parts, out = refs[:-1], refs[-1]
    columns = len(parts)
    per_part = lax.axis_size("row") // columns
    part = lax.div(lax.axis_index("row"), per_part)
    for col in range(columns):
        value = parts[0][...]
        for flip in range(1, columns):
            value = jnp.where(jnp.bitwise_xor(part, col) == flip, parts[flip][...], value)
        for chip in range(out.shape[0] // columns):
            out[out.shape[0] - 1 - chip * columns - col] = value


def spread_sum(values):
    lead = 8
    split = values.reshape((values.shape[0] // lead, lead) + values.shape[1:])
    return jnp.sum(jnp.sum(split, axis=0), axis=0, keepdims=True)


def update_body(triangle, source, gate, tri_out, bias_proj, updated, bias, held, bias_held):
    channels, rows, cols = triangle.shape
    heads = bias_proj.shape[0]
    values = triangle[...].astype(F32)
    centre = values - spread_sum(values) * (1.0 / channels)
    spread = spread_sum(centre * centre) * (1.0 / channels)
    held[...] = (centre * lax.rsqrt(spread + EPS)).reshape(channels * rows, cols)
    out_weights = turned(tri_out[...])
    bias_weights = bias_proj[...]

    def step(row, carry):
        tri_normed = held[pl.ds(row, channels, stride=rows), :].astype(BF16)
        update = gate[row].astype(F32) * dot(out_weights, tri_normed, (1, 0))
        mine = (source[row].astype(F32) + update).astype(BF16)
        updated[row] = mine
        normed = layer_norm(mine.astype(F32), 0).astype(BF16)
        bias_held[pl.ds(row, heads, stride=rows), :] = dot(bias_weights, normed, (1, 0))
        return carry

    lax.fori_loop(0, rows, step, 0, unroll=rows)
    bias[...] = bias_held[...].astype(BF16).reshape(heads, rows, cols)


def project(updated, attn_proj, mixed, row, score_scale, late=None):
    channels = updated.shape[1]
    values = updated[row].astype(F32)
    normed = layer_norm(values, 0)
    natural = normed.T.astype(BF16)

    def put(target, block, array):
        target[row, :, block * channels : (block + 1) * channels] = array.astype(BF16)

    put(mixed, 0, dot(turned(attn_proj[:, channels : 2 * channels]), normed.astype(BF16), (1, 0)))
    put(mixed, 1, dot(natural, attn_proj[:, 2 * channels : 3 * channels], (1, 0)))
    if late is not None:
        put(mixed, 2, dot(natural, attn_proj[:, :channels], (1, 0)) * score_scale)
        put(late, 0, sigmoid(dot(natural, attn_proj[:, 3 * channels :], (1, 0))))
        put(late, 1, values.T)


def own_body(updated, attn_proj, mixed, late, *, score_scale):
    def step(row, carry):
        project(updated, attn_proj, mixed, row, score_scale, late)
        return carry

    lax.fori_loop(0, updated.shape[0], step, 0, unroll=8)


def other_body(attn_proj, *rest):
    pieces = len(rest) // 2
    for updated, target in zip(rest[:pieces], rest[pieces:]):

        def step(row, carry):
            project(updated, attn_proj, target, row, None)
            return carry

        lax.fori_loop(0, updated.shape[0], step, 0, unroll=8)


def attend_body(length, mine, sibling, attn_out, late, *rest):
    mixed, (out_hbm, out, bias_held, sems) = rest[:-4], rest[-4:]
    pieces = len(mixed)
    rows, cols, channels = out.shape
    heads = mine.shape[1]
    me = lax.axis_index("ch")
    its_core = lax.rem(lax.axis_index("row"), 2)
    head_of = lax.broadcasted_iota(jnp.int32, (1, channels), 1) // (channels // heads)
    count = sems.shape[1]
    sends = chunked([(out, out_hbm)], sems, 0, count)
    chips = cols // rows // 2
    for piece in range(pieces):
        block = lax.rem(me + piece, pieces)
        token = block * cols + lax.broadcasted_iota(jnp.int32, (1, cols), 1)
        key_term = jnp.where(token < length[0], 0.0, -1e9)
        for part, core in ((mine, its_core), (sibling, 1 - its_core)):
            for chip in range(chips):
                tiles = part[part.shape[0] - 1 - chip * pieces - block]
                for head in range(heads):
                    first = pl.multiple_of(head * cols + (chip * 2 + core) * rows, rows)
                    bias_held[pl.ds(first, rows), piece * cols : (piece + 1) * cols] = (
                        tiles[head].astype(F32) + key_term
                    )
    both_of = jnp.concatenate([head_of, head_of], axis=1)
    masks = [(head_of == head).astype(BF16) for head in range(heads)]
    ones = jnp.ones((pieces * cols, channels), BF16)

    def load(row):
        keys = jnp.concatenate([part[row, :, :channels] for part in mixed], axis=1)
        values = jnp.concatenate([part[row, :, channels : 2 * channels] for part in mixed], axis=0)
        values = jnp.concatenate([values, ones], axis=1)
        return keys, values, mixed[0][row, :, 2 * channels :]

    def finish(row, total):
        attended = total[:, :channels] / total[:, channels:]
        gate = late[row, :, :channels].astype(F32)
        gated = (attended * gate).astype(BF16)
        residual = late[row, :, channels:].astype(F32)
        out[row] = (residual + dot(gated, attn_out[...], (1, 0))).astype(BF16)

    per_chunk = rows // count
    loaded, logits, weights = {}, {}, {}
    for time in range(rows + 2):
        row = time
        if row < rows:
            loaded[row] = load(row)
            keys, _, query = loaded[row]
            queries = jnp.concatenate([query * mask for mask in masks], axis=0)
            logits[row] = dot(queries, keys, (1, 0)) + bias_held[...]
        row = time - 1
        if 0 <= row < rows:
            scores = logits.pop(row)
            top = jnp.max(scores, axis=-1, keepdims=True)
            weights[row] = jnp.exp((scores - top).astype(BF16))
        row = time - 2
        if row >= 0:
            sums = dot(weights.pop(row), loaded.pop(row)[1], (1, 0))
            total = sums[:cols]
            for head in range(1, heads):
                total = jnp.where(both_of == head, sums[head * cols : (head + 1) * cols], total)
            finish(row, total)
            chunk, place_in = divmod(row, per_chunk)
            if place_in == per_chunk - 1:
                for copy in sends[chunk]:
                    copy.start()
    for send in sends:
        for copy in send:
            copy.wait()


def local(
    pair_act, valid_count, edge_proj, edge_gate, tri_gate, tri_out, attn_proj, bias_proj, attn_out
):
    rows, cols, channels = pair_act.shape
    heads = bias_proj.shape[1]
    row_devices = lax.axis_size("row")
    col_devices = lax.axis_size("ch")
    devices = row_devices * col_devices
    share = devices // 2
    own = channels // share
    everyone = list(reversed(range(devices)))
    halves = [everyone[share:], everyone[:share]]
    shape = jax.ShapeDtypeStruct
    block = (rows, cols, channels)
    turned_block = (rows, channels, cols)

    def in_half(array):
        return lax.all_to_all(
            array, BOTH, split_axis=0, concat_axis=0, axis_index_groups=halves, tiled=True
        )


    offsets = chip_offsets()
    tile = (own, rows, cols)
    both = pltpu.VMEM(edge_proj.shape, BF16)
    right, normed, mine, theirs = call(
        edges_body,
        "edges",
        [shape((devices,) + tile, BF16), shape(block, BF16)]
        + [shape((len(offsets),) + tile, BF16)] * 2,
        4,
        [
            pltpu.VMEM(block, BF16),
            both,
            both,
            pltpu.VMEM((2, channels * rows, cols), F32),
            pltpu.VMEM((share,) + tile, BF16),
            pltpu.SemaphoreType.DMA((3, 5)),
        ],
        smem=1,
        space=HBM,
        out_space=[HBM, HBM, VMEM, VMEM],
        flops=4e9,
    )(valid_count, *[in_hbm(a) for a in (pair_act, edge_proj, edge_gate)])

    def flipped(array, bits):
        return lax.ppermute(array, BOTH, [(d, d ^ bits) for d in range(devices)])

    right = lax.all_to_all(right, BOTH, split_axis=0, concat_axis=0, tiled=True)
    left = call(pack_body, "pack", [shape((2,) + tile, BF16)] * len(offsets), 2)(
        mine, flipped(theirs, col_devices)
    )
    left = [flipped(part, offset) if offset else part for part, offset in zip(left, offsets)]
    tri_gating, source, bias_weights = call(
        gate_body,
        "tri_gate",
        [shape(turned_block, BF16)] * 2 + [shape((heads, channels), BF16)],
        4,
        flops=2e9,
    )(pair_act, normed, tri_gate, bias_proj)
    tri_gating, source, bias_weights, *left = lax.optimization_barrier(
        (tri_gating, source, bias_weights, *left)
    )
    triangle_shape = (row_devices // 2, col_devices, own, rows, cols)
    (triangle,) = call(
        triangle_body,
        "triangle",
        [shape(triangle_shape, BF16)],
        1 + len(left),
        flops=2e9,
    )(right.reshape((row_devices,) + triangle_shape[1:]), *left)
    triangle = in_half(triangle.reshape(share, own, rows, cols))
    bias_shape = (heads, rows, cols)
    updated, bias = call(
        update_body,
        "update",
        [shape(turned_block, BF16), shape(bias_shape, BF16)],
        5,
        [pltpu.VMEM((channels * rows, cols), F32), pltpu.VMEM((heads * rows, cols), F32)],
        flops=2e9,
    )(triangle.reshape(channels, rows, cols), source, tri_gating, tri_out, bias_weights)
    per_part = row_devices // col_devices
    parts = [bias] + [
        flipped(bias, flip * per_part * col_devices) for flip in range(1, col_devices)
    ]
    (dealt,) = call(
        deal_body, "deal_bias", [shape((per_part // 2 * col_devices,) + bias_shape, BF16)], col_devices
    )(*parts)
    one_core = []
    for part in range(col_devices):
        for core in range(2):
            members = range(part * per_part + core, (part + 1) * per_part, 2)
            group = [r * col_devices + c for r in members for c in range(col_devices)]
            one_core.append(group[::-1])

    others = [
        lax.ppermute(updated, "ch", [((c + s) % col_devices, c) for c in range(col_devices)])
        for s in range(1, col_devices)
    ]
    mixed_shape = (rows, cols, 3 * channels)
    key_shape = (rows, cols, 2 * channels)
    mixed, late = call(
        functools.partial(own_body, score_scale=(channels // heads) ** (-0.5)),
        "own_projections",
        [shape(mixed_shape, BF16), shape(key_shape, BF16)],
        2,
        flops=2e9,
    )(updated, attn_proj)
    dealt, mixed, late = lax.optimization_barrier((dealt, mixed, late))
    bias = lax.all_to_all(
        dealt, BOTH, split_axis=0, concat_axis=0, axis_index_groups=one_core, tiled=True
    )
    bias, *others = lax.optimization_barrier((bias, *others))
    keys = call(
        other_body,
        "other_keys",
        [shape(key_shape, BF16)] * len(others),
        1 + len(others),
        flops=3e9,
    )(attn_proj, *others)
    (result,) = call(
        attend_body,
        "attend",
        [shape(block, BF16)],
        5 + col_devices,
        [
            pltpu.VMEM(block, BF16),
            pltpu.VMEM((heads * cols, col_devices * cols), F32),
            pltpu.SemaphoreType.DMA((1, rows // 2)),
        ],
        smem=1,
        out_space=HBM,
    )(valid_count, bias, flipped(bias, col_devices), attn_out, late, mixed, *keys)
    return result


def solution(mesh):
    placed = (P("row", "ch", None), P(), P(), P(), P(), P(), P(), P(), P())
    return jax.shard_map(
        local, mesh=mesh, in_specs=placed, out_specs=P("row", "ch", None), check_vma=False
    )
```

```python
import functools
import math

import jax
import jax.numpy as jnp
from jax import lax
from jax.experimental import pallas as pl
from jax.experimental.pallas import tpu as pltpu
from jax.sharding import PartitionSpec as P

EPS = 1e-05
BOTH = ("row", "ch")
F32 = jnp.float32
BF16 = jnp.bfloat16
VMEM = pl.BlockSpec(memory_space=pltpu.VMEM)
SMEM = pl.BlockSpec(memory_space=pltpu.SMEM)
HBM = pl.BlockSpec(memory_space=pltpu.HBM)
ANY = pl.BlockSpec(memory_space=pl.ANY)


def layer_norm(values, axis):
    centre = values - jnp.mean(values, axis=axis, keepdims=True)
    spread = jnp.mean(centre * centre, axis=axis, keepdims=True)
    return centre * lax.rsqrt(spread + EPS)


def in_hbm(array):
    return pltpu.with_memory_space_constraint(array, pltpu.HBM)


def sigmoid(values):
    return 0.5 * jnp.tanh(0.5 * values) + 0.5


def dot(a, b, dims):
    return lax.dot_general(a, b, ((dims[:1], dims[1:]), ((), ())), preferred_element_type=F32)


def call(body, name, outs, ins, scratch=(), flops=1e8, smem=0, space=VMEM, out_space=VMEM, specs=None):
    sizes = [math.prod(a.shape) * a.dtype.itemsize for a in outs]
    spaces = out_space if isinstance(out_space, list) else [out_space] * len(outs)
    outs = [pltpu.HBM(a.shape, a.dtype) if b is HBM else a for a, b in zip(outs, spaces)]
    return pl.pallas_call(
        body,
        out_shape=outs,
        in_specs=specs or [SMEM] * smem + [space] * (ins - smem),
        out_specs=spaces,
        scratch_shapes=list(scratch),
        compiler_params=pltpu.CompilerParams(vmem_limit_bytes=16 * 2**20),
        cost_estimate=pl.CostEstimate(
            flops=int(flops), bytes_accessed=2 * sum(sizes), transcendentals=0
        ),
        name=name,
    )


def turned(weights):
    return weights.astype(F32).T.astype(BF16)


def run(copies):
    for copy in copies:
        copy.start()
    for copy in copies:
        copy.wait()


def place():
    per_half = lax.axis_size("row") // 2
    columns = lax.axis_size("ch")
    row = lax.rem(lax.axis_index("row"), per_half)
    core = lax.rem(row, 2)
    return (row - core) * columns + lax.axis_index("ch"), core


def chip_offsets():
    columns = lax.axis_size("ch")
    share = lax.axis_size("row") // 2 * columns
    return [o for o in range(share) if o // columns % 2 == 0]


def chunked(pairs, sems, first, chunks):
    rows = pairs[0][0].shape[0]
    size = rows // chunks
    return [
        [
            pltpu.make_async_copy(
                source.at[pl.ds(chunk * size, size)],
                target.at[pl.ds(chunk * size, size)],
                sems.at[first + k, chunk],
            )
            for k, (source, target) in enumerate(pairs)
        ]
        for chunk in range(chunks)
    ]


def edges_body(
    length, source_hbm, proj_hbm, gate_hbm, right, normed, mine, theirs, source, proj, gate, held, out, sems
):
    rows, cols, channels = source.shape
    share, own = out.shape[:2]
    columns = lax.axis_size("ch")
    fetches = [
        pltpu.make_async_copy(proj_hbm, proj, sems.at[0, 2]),
        pltpu.make_async_copy(gate_hbm, gate, sems.at[0, 3]),
    ]
    chunks = chunked([(source_hbm, source)], sems, 0, 2)
    for copy in fetches + chunks[0] + chunks[1]:
        copy.start()
    row_offset = lax.axis_index("row") * rows
    col_offset = lax.axis_index("ch") * cols
    count = length[0]
    tokens = col_offset + lax.broadcasted_iota(jnp.int32, (1, cols), 1)
    col_valid = jnp.where(tokens < count, 0.5, 0.0)
    for copy in fetches:
        copy.wait()
    spans = [slice(side * channels, (side + 1) * channels) for side in range(2)]
    weights = [
        jnp.concatenate([turned(proj[:, span]), turned(gate[:, span])], axis=0) for span in spans
    ]
    for (copy,) in chunks:
        copy.wait()
    sends = []
    for side in (1, 0):

        def step(row, carry):
            values = source[row]
            if side:
                values = layer_norm(values.astype(F32), -1).astype(BF16)
                source[row] = values
            mixed = dot(weights[side], values, (1, 1))
            valid = col_valid * (row_offset + row < count).astype(F32)
            twice = jnp.tanh(0.5 * mixed[channels:]) + 1.0
            held[side, pl.ds(row, channels, stride=rows), :] = twice * (mixed[:channels] * valid)
            return carry

        lax.fori_loop(0, rows, step, 0, unroll=rows)
        if side:
            sends.append(pltpu.make_async_copy(source, normed, sems.at[1, 0]))
            sends[0].start()
        group = share // 4
        for device in range(share):
            part = held[side, device * own * rows : (device + 1) * own * rows, :].astype(BF16)
            position = share - 1 - device
            if side:
                out[position] = part.reshape(own, rows, cols)
            else:
                held_left = part.reshape(own, rows, cols)
                theirs_at = position % (2 * columns) // columns
                place_of(position, theirs_at, held_left, mine, theirs)
            if side and device % group == group - 1:
                for k in range(2):
                    source_part = out.at[pl.ds(position, group)]
                    target = right.at[pl.ds(k * share + position, group)]
                    sends.append(
                        pltpu.make_async_copy(
                            source_part, target, sems.at[1 + k, 1 + device // group]
                        )
                    )
                    sends[-1].start()
    for copy in sends:
        copy.wait()


def place_of(position, its_core, block, mine, theirs):
    columns = lax.axis_size("ch")
    chip, core = place()
    offset = jnp.bitwise_xor(chip, position - its_core * columns)
    col = lax.rem(offset, columns)
    index = lax.div(offset, 2 * columns) * columns + col

    @pl.when(core == its_core)
    def _():
        mine[index] = block

    @pl.when(core != its_core)
    def _():
        theirs[index] = block


def pack_body(mine, sibling, *outs):
    _, core = place()
    for k, out in enumerate(outs):
        out[core] = mine[k]
        out[1 - core] = sibling[k]


def gate_body(pair, normed, weights, bias_proj, out, source, bias_weights):
    turned_weights = turned(weights[...])
    bias_weights[...] = turned(bias_proj[...])

    def step(row, carry):
        out[row] = sigmoid(dot(turned_weights, normed[row], (1, 1))).astype(BF16)
        source[row] = pair[row].astype(F32).T.astype(BF16)
        return carry

    lax.fori_loop(0, pair.shape[0], step, 0, unroll=2)


def triangle_body(right, *rest):
    parts, held = rest[:-1], rest[-1]
    row_devices, col_devices, own, rows, cols = right.shape
    chip, _ = place()
    chip_row = lax.div(chip, col_devices)
    me = lax.axis_index("ch")
    groups = [(first, core) for first in range(0, row_devices // 2, 2) for core in range(2)]
    offsets = chip_offsets()
    for channel in range(own):
        left, whole = [], []
        for flip in range(col_devices):
            left.append(
                jnp.concatenate(
                    [
                        parts[offsets.index(first * col_devices + flip)][core, channel]
                        for first, core in groups
                    ],
                    axis=0,
                )
            )
            whole.append(right[:, jnp.bitwise_xor(me, flip), channel].reshape(-1, cols))
        triangle = dot(
            jnp.concatenate(left, axis=1), jnp.concatenate(whole, axis=1), (1, 1)
        ).astype(BF16)
        for k, (first, core) in enumerate(groups):
            for part in range(col_devices):
                row = row_devices // 2 - 1 - core - jnp.bitwise_xor(chip_row, first)
                held[row, col_devices - 1 - part, channel] = triangle[
                    k * rows : (k + 1) * rows, part * cols : (part + 1) * cols
                ]


def deal_body(*refs):
    parts, out = refs[:-1], refs[-1]
    columns = len(parts)
    per_part = lax.axis_size("row") // columns
    part = lax.div(lax.axis_index("row"), per_part)
    for col in range(columns):
        value = parts[0][...]
        for flip in range(1, columns):
            value = jnp.where(jnp.bitwise_xor(part, col) == flip, parts[flip][...], value)
        for chip in range(out.shape[0] // columns):
            out[out.shape[0] - 1 - chip * columns - col] = value


def spread_sum(values):
    lead = 8
    split = values.reshape((values.shape[0] // lead, lead) + values.shape[1:])
    return jnp.sum(jnp.sum(split, axis=0), axis=0, keepdims=True)


def update_body(triangle, source, gate, tri_out, bias_proj, updated, bias, held, bias_held):
    channels, rows, cols = triangle.shape
    heads = bias_proj.shape[0]
    values = triangle[...].astype(F32)
    centre = values - spread_sum(values) * (1.0 / channels)
    spread = spread_sum(centre * centre) * (1.0 / channels)
    held[...] = (centre * lax.rsqrt(spread + EPS)).reshape(channels * rows, cols)
    out_weights = turned(tri_out[...])
    bias_weights = bias_proj[...]

    def step(row, carry):
        tri_normed = held[pl.ds(row, channels, stride=rows), :].astype(BF16)
        update = gate[row].astype(F32) * dot(out_weights, tri_normed, (1, 0))
        mine = (source[row].astype(F32) + update).astype(BF16)
        updated[row] = mine
        normed = layer_norm(mine.astype(F32), 0).astype(BF16)
        bias_held[pl.ds(row, heads, stride=rows), :] = dot(bias_weights, normed, (1, 0))
        return carry

    lax.fori_loop(0, rows, step, 0, unroll=rows)
    bias[...] = bias_held[...].astype(BF16).reshape(heads, rows, cols)


def project(updated, attn_proj, mixed, row, score_scale, late=None, query=None):
    channels = updated.shape[1]
    values = updated[row].astype(F32)
    normed = layer_norm(values, 0)
    natural = normed.T.astype(BF16)

    def put(target, block, array):
        target[row, :, block * channels : (block + 1) * channels] = array.astype(BF16)

    put(mixed, 0, dot(turned(attn_proj[:, channels : 2 * channels]), normed.astype(BF16), (1, 0)))
    put(mixed, 1, dot(natural, attn_proj[:, 2 * channels : 3 * channels], (1, 0)))
    if late is not None:
        scaled = (dot(natural, attn_proj[:, :channels], (1, 0)) * score_scale).astype(BF16)
        cols = natural.shape[0]
        heads = query.shape[1] // cols
        head_of = lax.broadcasted_iota(jnp.int32, (1, channels), 1) // (channels // heads)
        for head in range(heads):
            mask = (head_of == head).astype(BF16)
            query[row, head * cols : (head + 1) * cols, :] = scaled * mask
        put(late, 0, sigmoid(dot(natural, attn_proj[:, 3 * channels :], (1, 0))))
        put(late, 1, values.T)


def own_body(updated, attn_proj, mixed, late, query, *, score_scale):
    def step(row, carry):
        project(updated, attn_proj, mixed, row, score_scale, late, query)
        return carry

    lax.fori_loop(0, updated.shape[0], step, 0, unroll=8)


def other_body(attn_proj, *rest):
    pieces = len(rest) // 2
    for updated, target in zip(rest[:pieces], rest[pieces:]):

        def step(row, carry):
            project(updated, attn_proj, target, row, None)
            return carry

        lax.fori_loop(0, updated.shape[0], step, 0, unroll=8)


def attend_body(length, mine, sibling, attn_out, late, query, *rest):
    mixed, (out_hbm, out, bias_held, sems) = rest[:-4], rest[-4:]
    pieces = len(mixed)
    rows, cols, channels = out.shape
    heads = mine.shape[1]
    me = lax.axis_index("ch")
    its_core = lax.rem(lax.axis_index("row"), 2)
    head_of = lax.broadcasted_iota(jnp.int32, (1, channels), 1) // (channels // heads)
    count = sems.shape[1]
    sends = chunked([(out, out_hbm)], sems, 0, count)
    chips = cols // rows // 2
    for piece in range(pieces):
        block = lax.rem(me + piece, pieces)
        token = block * cols + lax.broadcasted_iota(jnp.int32, (1, cols), 1)
        key_term = jnp.where(token < length[0], 0.0, -1e9)
        for part, core in ((mine, its_core), (sibling, 1 - its_core)):
            for chip in range(chips):
                tiles = part[part.shape[0] - 1 - chip * pieces - block]
                for head in range(heads):
                    first = pl.multiple_of(head * cols + (chip * 2 + core) * rows, rows)
                    bias_held[pl.ds(first, rows), piece * cols : (piece + 1) * cols] = (
                        tiles[head].astype(F32) + key_term
                    )
    both_of = jnp.concatenate([head_of, head_of], axis=1)
    ones = jnp.ones((pieces * cols, channels), BF16)

    def load(row):
        keys = jnp.concatenate([part[row, :, :channels] for part in mixed], axis=1)
        values = jnp.concatenate([part[row, :, channels : 2 * channels] for part in mixed], axis=0)
        values = jnp.concatenate([values, ones], axis=1)
        return keys, values

    def finish(row, total):
        weight = total[:, channels:]
        inverse = pl.reciprocal(weight, approx=True)
        attended = total[:, :channels] * (inverse * (2.0 - weight * inverse))
        gate = late[row, :, :channels].astype(F32)
        gated = (attended * gate).astype(BF16)
        residual = late[row, :, channels:].astype(F32)
        out[row] = (residual + dot(gated, attn_out[...], (1, 0))).astype(BF16)

    per_chunk = rows // count
    loaded, logits, weights = {}, {}, {}
    for time in range(rows + 2):
        row = time
        if row < rows:
            loaded[row] = load(row)
            logits[row] = dot(query[row], loaded[row][0], (1, 0)) + bias_held[...]
        row = time - 1
        if 0 <= row < rows:
            scores = logits.pop(row)
            top = jnp.max(scores, axis=-1, keepdims=True)
            weights[row] = jnp.exp((scores - top).astype(BF16))
        row = time - 2
        if row >= 0:
            sums = dot(weights.pop(row), loaded.pop(row)[1], (1, 0))
            total = sums[:cols]
            for head in range(1, heads):
                total = jnp.where(both_of == head, sums[head * cols : (head + 1) * cols], total)
            finish(row, total)
            chunk, place_in = divmod(row, per_chunk)
            if place_in == per_chunk - 1:
                for copy in sends[chunk]:
                    copy.start()
    for send in sends:
        for copy in send:
            copy.wait()


def local(
    pair_act, valid_count, edge_proj, edge_gate, tri_gate, tri_out, attn_proj, bias_proj, attn_out
):
    rows, cols, channels = pair_act.shape
    heads = bias_proj.shape[1]
    row_devices = lax.axis_size("row")
    col_devices = lax.axis_size("ch")
    devices = row_devices * col_devices
    share = devices // 2
    own = channels // share
    everyone = list(reversed(range(devices)))
    halves = [everyone[share:], everyone[:share]]
    shape = jax.ShapeDtypeStruct
    block = (rows, cols, channels)
    turned_block = (rows, channels, cols)

    def in_half(array):
        return lax.all_to_all(
            array, BOTH, split_axis=0, concat_axis=0, axis_index_groups=halves, tiled=True
        )


    offsets = chip_offsets()
    tile = (own, rows, cols)
    both = pltpu.VMEM(edge_proj.shape, BF16)
    right, normed, mine, theirs = call(
        edges_body,
        "edges",
        [shape((devices,) + tile, BF16), shape(block, BF16)]
        + [shape((len(offsets),) + tile, BF16)] * 2,
        4,
        [
            pltpu.VMEM(block, BF16),
            both,
            both,
            pltpu.VMEM((2, channels * rows, cols), F32),
            pltpu.VMEM((share,) + tile, BF16),
            pltpu.SemaphoreType.DMA((3, 5)),
        ],
        smem=1,
        space=HBM,
        out_space=[HBM, HBM, VMEM, VMEM],
        flops=4e9,
    )(valid_count, *[in_hbm(a) for a in (pair_act, edge_proj, edge_gate)])

    def flipped(array, bits):
        return lax.ppermute(array, BOTH, [(d, d ^ bits) for d in range(devices)])

    right = lax.all_to_all(right, BOTH, split_axis=0, concat_axis=0, tiled=True)
    left = call(pack_body, "pack", [shape((2,) + tile, BF16)] * len(offsets), 2)(
        mine, flipped(theirs, col_devices)
    )
    left = [flipped(part, offset) if offset else part for part, offset in zip(left, offsets)]
    tri_gating, source, bias_weights = call(
        gate_body,
        "tri_gate",
        [shape(turned_block, BF16)] * 2 + [shape((heads, channels), BF16)],
        4,
        flops=2e9,
    )(pair_act, normed, tri_gate, bias_proj)
    tri_gating, source, bias_weights, *left = lax.optimization_barrier(
        (tri_gating, source, bias_weights, *left)
    )
    triangle_shape = (row_devices // 2, col_devices, own, rows, cols)
    (triangle,) = call(
        triangle_body,
        "triangle",
        [shape(triangle_shape, BF16)],
        1 + len(left),
        flops=2e9,
    )(right.reshape((row_devices,) + triangle_shape[1:]), *left)
    triangle = in_half(triangle.reshape(share, own, rows, cols))
    bias_shape = (heads, rows, cols)
    updated, bias = call(
        update_body,
        "update",
        [shape(turned_block, BF16), shape(bias_shape, BF16)],
        5,
        [pltpu.VMEM((channels * rows, cols), F32), pltpu.VMEM((heads * rows, cols), F32)],
        flops=2e9,
    )(triangle.reshape(channels, rows, cols), source, tri_gating, tri_out, bias_weights)
    per_part = row_devices // col_devices
    parts = [bias] + [
        flipped(bias, flip * per_part * col_devices) for flip in range(1, col_devices)
    ]
    (dealt,) = call(
        deal_body, "deal_bias", [shape((per_part // 2 * col_devices,) + bias_shape, BF16)], col_devices
    )(*parts)
    one_core = []
    for part in range(col_devices):
        for core in range(2):
            members = range(part * per_part + core, (part + 1) * per_part, 2)
            group = [r * col_devices + c for r in members for c in range(col_devices)]
            one_core.append(group[::-1])

    others = [
        lax.ppermute(updated, "ch", [((c + s) % col_devices, c) for c in range(col_devices)])
        for s in range(1, col_devices)
    ]
    key_shape = (rows, cols, 2 * channels)
    mixed, late, query = call(
        functools.partial(own_body, score_scale=(channels // heads) ** (-0.5)),
        "own_projections",
        [shape(key_shape, BF16)] * 2 + [shape((rows, heads * cols, channels), BF16)],
        2,
        flops=2e9,
    )(updated, attn_proj)
    dealt, mixed, late, query = lax.optimization_barrier((dealt, mixed, late, query))
    bias = lax.all_to_all(
        dealt, BOTH, split_axis=0, concat_axis=0, axis_index_groups=one_core, tiled=True
    )
    bias, *others = lax.optimization_barrier((bias, *others))
    keys = call(
        other_body,
        "other_keys",
        [shape(key_shape, BF16)] * len(others),
        1 + len(others),
        flops=3e9,
    )(attn_proj, *others)
    (result,) = call(
        attend_body,
        "attend",
        [shape(block, BF16)],
        6 + col_devices,
        [
            pltpu.VMEM(block, BF16),
            pltpu.VMEM((heads * cols, col_devices * cols), F32),
            pltpu.SemaphoreType.DMA((1, rows // 2)),
        ],
        smem=1,
        out_space=HBM,
    )(valid_count, bias, flipped(bias, col_devices), attn_out, late, query, mixed, *keys)
    return result


def solution(mesh):
    placed = (P("row", "ch", None), P(), P(), P(), P(), P(), P(), P(), P())
    return jax.shard_map(
        local, mesh=mesh, in_specs=placed, out_specs=P("row", "ch", None), check_vma=False
    )
```

```python
import functools
import math

import jax
import jax.numpy as jnp
from jax import lax
from jax.experimental import pallas as pl
from jax.experimental.pallas import tpu as pltpu
from jax.sharding import PartitionSpec as P

EPS = 1e-05
BOTH = ("row", "ch")
F32 = jnp.float32
BF16 = jnp.bfloat16
VMEM = pl.BlockSpec(memory_space=pltpu.VMEM)
SMEM = pl.BlockSpec(memory_space=pltpu.SMEM)
HBM = pl.BlockSpec(memory_space=pltpu.HBM)
ANY = pl.BlockSpec(memory_space=pl.ANY)


def layer_norm(values, axis):
    centre = values - jnp.mean(values, axis=axis, keepdims=True)
    spread = jnp.mean(centre * centre, axis=axis, keepdims=True)
    return centre * lax.rsqrt(spread + EPS)


def in_hbm(array):
    return pltpu.with_memory_space_constraint(array, pltpu.HBM)


def sigmoid(values):
    return 0.5 * jnp.tanh(0.5 * values) + 0.5


def dot(a, b, dims):
    return lax.dot_general(a, b, ((dims[:1], dims[1:]), ((), ())), preferred_element_type=F32)


def call(body, name, outs, ins, scratch=(), flops=1e8, smem=0, space=VMEM, out_space=VMEM, specs=None):
    sizes = [math.prod(a.shape) * a.dtype.itemsize for a in outs]
    spaces = out_space if isinstance(out_space, list) else [out_space] * len(outs)
    outs = [pltpu.HBM(a.shape, a.dtype) if b is HBM else a for a, b in zip(outs, spaces)]
    return pl.pallas_call(
        body,
        out_shape=outs,
        in_specs=specs or [SMEM] * smem + [space] * (ins - smem),
        out_specs=spaces,
        scratch_shapes=list(scratch),
        compiler_params=pltpu.CompilerParams(vmem_limit_bytes=16 * 2**20),
        cost_estimate=pl.CostEstimate(
            flops=int(flops), bytes_accessed=2 * sum(sizes), transcendentals=0
        ),
        name=name,
    )


def turned(weights):
    return weights.astype(F32).T.astype(BF16)


def run(copies):
    for copy in copies:
        copy.start()
    for copy in copies:
        copy.wait()


def place():
    per_half = lax.axis_size("row") // 2
    columns = lax.axis_size("ch")
    row = lax.rem(lax.axis_index("row"), per_half)
    core = lax.rem(row, 2)
    return (row - core) * columns + lax.axis_index("ch"), core


def chip_offsets():
    columns = lax.axis_size("ch")
    share = lax.axis_size("row") // 2 * columns
    return [o for o in range(share) if o // columns % 2 == 0]


def chunked(pairs, sems, first, chunks):
    rows = pairs[0][0].shape[0]
    size = rows // chunks
    return [
        [
            pltpu.make_async_copy(
                source.at[pl.ds(chunk * size, size)],
                target.at[pl.ds(chunk * size, size)],
                sems.at[first + k, chunk],
            )
            for k, (source, target) in enumerate(pairs)
        ]
        for chunk in range(chunks)
    ]


def edges_body(
    length, source_hbm, proj_hbm, gate_hbm, right, normed, mine, theirs, source, proj, gate, held, out, sems
):
    rows, cols, channels = source.shape
    share, own = out.shape[:2]
    columns = lax.axis_size("ch")
    fetches = [
        pltpu.make_async_copy(proj_hbm, proj, sems.at[0, 2]),
        pltpu.make_async_copy(gate_hbm, gate, sems.at[0, 3]),
    ]
    chunks = chunked([(source_hbm, source)], sems, 0, 2)
    for copy in fetches + chunks[0] + chunks[1]:
        copy.start()
    row_offset = lax.axis_index("row") * rows
    col_offset = lax.axis_index("ch") * cols
    count = length[0]
    tokens = col_offset + lax.broadcasted_iota(jnp.int32, (1, cols), 1)
    col_valid = jnp.where(tokens < count, 0.5, 0.0)
    for copy in fetches:
        copy.wait()
    spans = [slice(side * channels, (side + 1) * channels) for side in range(2)]
    weights = [
        jnp.concatenate([turned(proj[:, span]), turned(gate[:, span])], axis=0) for span in spans
    ]
    for (copy,) in chunks:
        copy.wait()
    sends = []
    for side in (1, 0):

        def step(row, carry):
            values = source[row]
            if side:
                values = layer_norm(values.astype(F32), -1).astype(BF16)
                source[row] = values
            mixed = dot(weights[side], values, (1, 1))
            valid = col_valid * (row_offset + row < count).astype(F32)
            twice = jnp.tanh(0.5 * mixed[channels:]) + 1.0
            held[side, pl.ds(row, channels, stride=rows), :] = twice * (mixed[:channels] * valid)
            return carry

        lax.fori_loop(0, rows, step, 0, unroll=rows)
        if side:
            sends.append(pltpu.make_async_copy(source, normed, sems.at[1, 0]))
            sends[0].start()
        group = share // 4
        for device in range(share):
            part = held[side, device * own * rows : (device + 1) * own * rows, :].astype(BF16)
            position = share - 1 - device
            if side:
                out[position] = part.reshape(own, rows, cols)
            else:
                held_left = part.reshape(own, rows, cols)
                theirs_at = position % (2 * columns) // columns
                place_of(position, theirs_at, held_left, mine, theirs)
            if side and device % group == group - 1:
                for k in range(2):
                    source_part = out.at[pl.ds(position, group)]
                    target = right.at[pl.ds(k * share + position, group)]
                    sends.append(
                        pltpu.make_async_copy(
                            source_part, target, sems.at[1 + k, 1 + device // group]
                        )
                    )
                    sends[-1].start()
    for copy in sends:
        copy.wait()


def place_of(position, its_core, block, mine, theirs):
    columns = lax.axis_size("ch")
    chip, core = place()
    offset = jnp.bitwise_xor(chip, position - its_core * columns)
    col = lax.rem(offset, columns)
    index = lax.div(offset, 2 * columns) * columns + col

    @pl.when(core == its_core)
    def _():
        mine[index] = block

    @pl.when(core != its_core)
    def _():
        theirs[index] = block


def pack_body(mine, sibling, *outs):
    _, core = place()
    for k, out in enumerate(outs):
        out[core] = mine[k]
        out[1 - core] = sibling[k]


def gate_body(pair, normed, weights, bias_proj, out, source, bias_weights):
    turned_weights = turned(weights[...])
    bias_weights[...] = turned(bias_proj[...])

    def step(row, carry):
        out[row] = sigmoid(dot(turned_weights, normed[row], (1, 1))).astype(BF16)
        source[row] = pair[row].astype(F32).T.astype(BF16)
        return carry

    lax.fori_loop(0, pair.shape[0], step, 0, unroll=2)


def triangle_body(right, *rest):
    parts, held = rest[:-1], rest[-1]
    row_devices, col_devices, own, rows, cols = right.shape
    chip, _ = place()
    chip_row = lax.div(chip, col_devices)
    me = lax.axis_index("ch")
    groups = [(first, core) for first in range(0, row_devices // 2, 2) for core in range(2)]
    offsets = chip_offsets()
    for channel in range(own):
        left, whole = [], []
        for flip in range(col_devices):
            left.append(
                jnp.concatenate(
                    [
                        parts[offsets.index(first * col_devices + flip)][core, channel]
                        for first, core in groups
                    ],
                    axis=0,
                )
            )
            whole.append(right[:, jnp.bitwise_xor(me, flip), channel].reshape(-1, cols))
        triangle = dot(
            jnp.concatenate(left, axis=1), jnp.concatenate(whole, axis=1), (1, 1)
        ).astype(BF16)
        for k, (first, core) in enumerate(groups):
            for part in range(col_devices):
                row = row_devices // 2 - 1 - core - jnp.bitwise_xor(chip_row, first)
                held[row, col_devices - 1 - part, channel] = triangle[
                    k * rows : (k + 1) * rows, part * cols : (part + 1) * cols
                ]


def deal_body(*refs):
    parts, out = refs[:-1], refs[-1]
    columns = len(parts)
    per_part = lax.axis_size("row") // columns
    part = lax.div(lax.axis_index("row"), per_part)
    for col in range(columns):
        value = parts[0][...]
        for flip in range(1, columns):
            value = jnp.where(jnp.bitwise_xor(part, col) == flip, parts[flip][...], value)
        for chip in range(out.shape[0] // columns):
            out[out.shape[0] - 1 - chip * columns - col] = value


def spread_sum(values):
    lead = 8
    split = values.reshape((values.shape[0] // lead, lead) + values.shape[1:])
    return jnp.sum(jnp.sum(split, axis=0), axis=0, keepdims=True)


def update_body(triangle, source, gate, tri_out, bias_proj, updated, bias, held, bias_held):
    channels, rows, cols = triangle.shape
    heads = bias_proj.shape[0]
    values = triangle[...].astype(F32)
    centre = values - spread_sum(values) * (1.0 / channels)
    spread = spread_sum(centre * centre) * (1.0 / channels)
    held[...] = (centre * lax.rsqrt(spread + EPS)).reshape(channels * rows, cols)
    out_weights = turned(tri_out[...])
    bias_weights = bias_proj[...]

    def step(row, carry):
        tri_normed = held[pl.ds(row, channels, stride=rows), :].astype(BF16)
        update = gate[row].astype(F32) * dot(out_weights, tri_normed, (1, 0))
        mine = (source[row].astype(F32) + update).astype(BF16)
        updated[row] = mine
        normed = layer_norm(mine.astype(F32), 0).astype(BF16)
        bias_held[pl.ds(row, heads, stride=rows), :] = dot(bias_weights, normed, (1, 0))
        return carry

    lax.fori_loop(0, rows, step, 0, unroll=rows)
    bias[...] = bias_held[...].astype(BF16).reshape(heads, rows, cols)


def project(updated, attn_proj, mixed, row, score_scale, late=None):
    channels = updated.shape[1]
    values = updated[row].astype(F32)
    normed = layer_norm(values, 0)
    natural = normed.T.astype(BF16)

    def put(target, block, array):
        target[row, :, block * channels : (block + 1) * channels] = array.astype(BF16)

    put(mixed, 0, dot(turned(attn_proj[:, channels : 2 * channels]), normed.astype(BF16), (1, 0)))
    put(mixed, 1, dot(natural, attn_proj[:, 2 * channels : 3 * channels], (1, 0)))
    if late is not None:
        put(mixed, 2, dot(natural, attn_proj[:, :channels], (1, 0)) * score_scale)
        put(late, 0, sigmoid(dot(natural, attn_proj[:, 3 * channels :], (1, 0))))
        put(late, 1, values.T)


def own_body(updated, attn_proj, mixed, late, *, score_scale):
    def step(row, carry):
        project(updated, attn_proj, mixed, row, score_scale, late)
        return carry

    lax.fori_loop(0, updated.shape[0], step, 0, unroll=8)


def other_body(attn_proj, *rest):
    pieces = len(rest) // 2
    for updated, target in zip(rest[:pieces], rest[pieces:]):

        def step(row, carry):
            project(updated, attn_proj, target, row, None)
            return carry

        lax.fori_loop(0, updated.shape[0], step, 0, unroll=8)


def attend_body(length, mine, sibling, attn_out, late, *rest):
    mixed, (out_hbm, out, bias_held, sems) = rest[:-4], rest[-4:]
    pieces = len(mixed)
    rows, cols, channels = out.shape
    heads = mine.shape[1]
    me = lax.axis_index("ch")
    its_core = lax.rem(lax.axis_index("row"), 2)
    head_of = lax.broadcasted_iota(jnp.int32, (1, channels), 1) // (channels // heads)
    count = sems.shape[1]
    sends = chunked([(out, out_hbm)], sems, 0, count)
    chips = cols // rows // 2
    for piece in range(pieces):
        block = lax.rem(me + piece, pieces)
        token = block * cols + lax.broadcasted_iota(jnp.int32, (1, cols), 1)
        key_term = jnp.where(token < length[0], 0.0, -1e9)
        for part, core in ((mine, its_core), (sibling, 1 - its_core)):
            for chip in range(chips):
                tiles = part[part.shape[0] - 1 - chip * pieces - block]
                for head in range(heads):
                    first = pl.multiple_of(head * cols + (chip * 2 + core) * rows, rows)
                    bias_held[pl.ds(first, rows), piece * cols : (piece + 1) * cols] = (
                        tiles[head].astype(F32) + key_term
                    )
    both_of = jnp.concatenate([head_of, head_of], axis=1)
    masks = [(head_of == head).astype(BF16) for head in range(heads)]
    ones = jnp.ones((pieces * cols, channels), BF16)

    def load(row):
        keys = jnp.concatenate([part[row, :, :channels] for part in mixed], axis=1)
        values = jnp.concatenate([part[row, :, channels : 2 * channels] for part in mixed], axis=0)
        values = jnp.concatenate([values, ones], axis=1)
        return keys, values, mixed[0][row, :, 2 * channels :]

    def finish(row, total):
        attended = total[:, :channels] / total[:, channels:]
        gate = late[row, :, :channels].astype(F32)
        gated = (attended * gate).astype(BF16)
        residual = late[row, :, channels:].astype(F32)
        out[row] = (residual + dot(gated, attn_out[...], (1, 0))).astype(BF16)

    per_chunk = rows // count
    loaded, logits, weights = {}, {}, {}
    for time in range(rows + 2):
        row = time
        if row < rows:
            loaded[row] = load(row)
            keys, _, query = loaded[row]
            queries = jnp.concatenate([query * mask for mask in masks], axis=0)
            logits[row] = dot(queries, keys, (1, 0)) + bias_held[...]
        row = time - 1
        if 0 <= row < rows:
            scores = logits.pop(row)
            top = jnp.max(scores, axis=-1, keepdims=True)
            weights[row] = jnp.exp((scores - top).astype(BF16))
        row = time - 2
        if row >= 0:
            sums = dot(weights.pop(row), loaded.pop(row)[1], (1, 0))
            total = sums[:cols]
            for head in range(1, heads):
                total = jnp.where(both_of == head, sums[head * cols : (head + 1) * cols], total)
            finish(row, total)
            chunk, place_in = divmod(row, per_chunk)
            if place_in == per_chunk - 1:
                for copy in sends[chunk]:
                    copy.start()
    for send in sends:
        for copy in send:
            copy.wait()


def local(
    pair_act, valid_count, edge_proj, edge_gate, tri_gate, tri_out, attn_proj, bias_proj, attn_out
):
    rows, cols, channels = pair_act.shape
    heads = bias_proj.shape[1]
    row_devices = lax.axis_size("row")
    col_devices = lax.axis_size("ch")
    devices = row_devices * col_devices
    share = devices // 2
    own = channels // share
    everyone = list(reversed(range(devices)))
    halves = [everyone[share:], everyone[:share]]
    shape = jax.ShapeDtypeStruct
    block = (rows, cols, channels)
    turned_block = (rows, channels, cols)

    def in_half(array):
        return lax.all_to_all(
            array, BOTH, split_axis=0, concat_axis=0, axis_index_groups=halves, tiled=True
        )


    offsets = chip_offsets()
    tile = (own, rows, cols)
    both = pltpu.VMEM(edge_proj.shape, BF16)
    right, normed, mine, theirs = call(
        edges_body,
        "edges",
        [shape((devices,) + tile, BF16), shape(block, BF16)]
        + [shape((len(offsets),) + tile, BF16)] * 2,
        4,
        [
            pltpu.VMEM(block, BF16),
            both,
            both,
            pltpu.VMEM((2, channels * rows, cols), F32),
            pltpu.VMEM((share,) + tile, BF16),
            pltpu.SemaphoreType.DMA((3, 5)),
        ],
        smem=1,
        space=HBM,
        out_space=[HBM, HBM, VMEM, VMEM],
        flops=4e9,
    )(valid_count, *[in_hbm(a) for a in (pair_act, edge_proj, edge_gate)])

    def flipped(array, bits):
        return lax.ppermute(array, BOTH, [(d, d ^ bits) for d in range(devices)])

    right = lax.all_to_all(right, BOTH, split_axis=0, concat_axis=0, tiled=True)
    left = call(pack_body, "pack", [shape((2,) + tile, BF16)] * len(offsets), 2)(
        mine, flipped(theirs, col_devices)
    )
    left = [flipped(part, offset) if offset else part for part, offset in zip(left, offsets)]
    tri_gating, source, bias_weights = call(
        gate_body,
        "tri_gate",
        [shape(turned_block, BF16)] * 2 + [shape((heads, channels), BF16)],
        4,
        flops=2e9,
    )(pair_act, normed, tri_gate, bias_proj)
    tri_gating, source, bias_weights, *left = lax.optimization_barrier(
        (tri_gating, source, bias_weights, *left)
    )
    triangle_shape = (row_devices // 2, col_devices, own, rows, cols)
    (triangle,) = call(
        triangle_body,
        "triangle",
        [shape(triangle_shape, BF16)],
        1 + len(left),
        flops=2e9,
    )(right.reshape((row_devices,) + triangle_shape[1:]), *left)
    triangle = in_half(triangle.reshape(share, own, rows, cols))
    bias_shape = (heads, rows, cols)
    updated, bias = call(
        update_body,
        "update",
        [shape(turned_block, BF16), shape(bias_shape, BF16)],
        5,
        [pltpu.VMEM((channels * rows, cols), F32), pltpu.VMEM((heads * rows, cols), F32)],
        flops=2e9,
    )(triangle.reshape(channels, rows, cols), source, tri_gating, tri_out, bias_weights)
    per_part = row_devices // col_devices
    parts = [bias] + [
        flipped(bias, flip * per_part * col_devices) for flip in range(1, col_devices)
    ]
    (dealt,) = call(
        deal_body, "deal_bias", [shape((per_part // 2 * col_devices,) + bias_shape, BF16)], col_devices
    )(*parts)
    one_core = []
    for part in range(col_devices):
        for core in range(2):
            members = range(part * per_part + core, (part + 1) * per_part, 2)
            group = [r * col_devices + c for r in members for c in range(col_devices)]
            one_core.append(group[::-1])

    others = [
        lax.ppermute(updated, "ch", [((c + s) % col_devices, c) for c in range(col_devices)])
        for s in range(1, col_devices)
    ]
    mixed_shape = (rows, cols, 3 * channels)
    key_shape = (rows, cols, 2 * channels)
    mixed, late = call(
        functools.partial(own_body, score_scale=(channels // heads) ** (-0.5)),
        "own_projections",
        [shape(mixed_shape, BF16), shape(key_shape, BF16)],
        2,
        flops=2e9,
    )(updated, attn_proj)
    dealt, mixed, late = lax.optimization_barrier((dealt, mixed, late))
    bias = lax.all_to_all(
        dealt, BOTH, split_axis=0, concat_axis=0, axis_index_groups=one_core, tiled=True
    )
    bias, *others = lax.optimization_barrier((bias, *others))
    keys = call(
        other_body,
        "other_keys",
        [shape(key_shape, BF16)] * len(others),
        1 + len(others),
        flops=3e9,
    )(attn_proj, *others)
    (result,) = call(
        attend_body,
        "attend",
        [shape(block, BF16)],
        5 + col_devices,
        [
            pltpu.VMEM(block, BF16),
            pltpu.VMEM((heads * cols, col_devices * cols), F32),
            pltpu.SemaphoreType.DMA((1, rows)),
        ],
        smem=1,
        out_space=HBM,
    )(valid_count, bias, flipped(bias, col_devices), attn_out, late, mixed, *keys)
    return result


def solution(mesh):
    placed = (P("row", "ch", None), P(), P(), P(), P(), P(), P(), P(), P())
    return jax.shard_map(
        local, mesh=mesh, in_specs=placed, out_specs=P("row", "ch", None), check_vma=False
    )
```
